32 devices in a mesh: pair: 16 (over z, y, x), virt: 2 (over core).
Axes of the slice: x: 2, y: 2, z: 4, core: 2. Of those that a mesh axis runs over, the one named last changes fastest.
Arguments:
- t2_amplitudes: float32 [64, 2048], P('pair', 'virt'), may hold values from -6 to 6
- integral_tiles: float32 [16, 2, 32, 128, 128], P('pair', 'virt'), may hold values from -0.125 to 0.125
- out_tiles: int32 [16, 2, 32], P('pair', 'virt'), may hold values from 0 to 15, as said below
- in_tiles: int32 [16, 2, 32], P('pair', 'virt'), may hold values from 0 to 15
- tile_counts: int32 [16, 2], P('pair', 'virt'), may hold values from 1 to 32, as said below
Outputs:
- ladder: float32 [64, 2048], P('pair', 'virt')
The draws below stay inside these ranges and needn't reach their ends.
Inputs may be any that keep to these rules, and one draw needn't show every extreme that they name: `out_tiles`: slots of the devices at virt index v name output tiles v * 8 to (v + 1) * 8 - 1 only. `tile_counts`: in every draw some device has all 32 slots live.
All inputs are finite; a program needn't handle non-finite values.
Results may differ from the reference program's by a relative error of at most 0.0003.
Values sent between devices are 32-bit elements; how exact they have to be, the bound alone decides.
No kernel may reach another device: no remote copies, remote signals or barrier semaphores. Data moves between devices by JAX's collectives and lax.ppermute only.
A program may use at most 64 MiB of HBM per device.

```python
import jax
import jax.numpy as jnp
from jax import lax

W = 128
KV = 8
LIST = 32
KG = 16
P_SIZE = 64
N_PAIR = 16
N_VIRT = 2


def draw_tile_counts(key, part):
    first_key, second_key = jax.random.split(jax.random.fold_in(key, 11))
    base_counts = jax.random.randint(first_key, (N_PAIR, N_VIRT), 1, LIST // 2 + 1)
    hot_rows = jax.random.randint(second_key, (N_VIRT,), 0, N_PAIR)
    hot_mask = jnp.arange(N_PAIR)[:, None] == hot_rows[None, :]
    return jnp.where(hot_mask, LIST, base_counts).astype(jnp.int32)


def draw_out_tiles(key, part):
    virt_index = jnp.arange(N_VIRT, dtype=jnp.int32)[None, :, None]
    picks = jax.random.randint(jax.random.fold_in(key, 23), (N_PAIR, N_VIRT, LIST), 0, KV)
    return (virt_index * KV + picks).astype(jnp.int32)


def with_ends(drawn, rng, smallest, largest):
    longest = drawn.shape.index(max(drawn.shape))
    spots = []
    for shift in (0, 1):
        where = [jax.random.randint(jax.random.fold_in(rng, axis), (), 0, length) for axis, length in enumerate(drawn.shape)]
        where[longest] = (where[longest] + shift) % drawn.shape[longest]
        spots.append(tuple(where))
    return drawn.at[spots[0]].set(smallest).at[spots[1]].set(largest)


def block_scale(stream_key, extent, pieces, smallest, high):
    def one(axis_at, blocks):
        steps = jax.random.uniform(jax.random.fold_in(jax.random.fold_in(stream_key, 6), axis_at), (blocks,), jnp.float32, smallest / len(pieces), high / len(pieces))
        return jnp.repeat(jnp.exp(steps), extent[axis_at] // blocks).reshape((-1,) + (1,) * (len(extent) - axis_at - 1))

    level = one(*pieces[0])
    for cut in pieces[1:]:
        level = level * one(*cut)
    return level


def gaussian(rng, shape, width, limit, shards=(), held_as=jnp.bfloat16):
    values = width * jax.random.normal(rng, shape, jnp.float32)
    if shards:
        values = values * block_scale(rng, shape, shards, -0.22, 0.18)
    return jnp.clip(values, -limit, limit).astype(held_as)


def setup_inputs(seed: int = 0) -> dict:
    key_of = jax.random.split(jax.random.key(seed), 6)
    return {
        "t2_amplitudes": gaussian(key_of[0], (P_SIZE, KG * W), 1.0, 6.0, ((0, 16), (1, 2)), jnp.float32),
        "integral_tiles": gaussian(key_of[1], (N_PAIR, N_VIRT, LIST, W, W), (W * N_PAIR * LIST // (4 * KV)) ** -0.5, 0.125, ((0, 16), (1, 2)), jnp.float32),
        "out_tiles": draw_out_tiles(jax.random.fold_in(key_of[5], 71), 0),
        "in_tiles": with_ends(jax.random.randint(key_of[3], (N_PAIR, N_VIRT, LIST), 0, KG), jax.random.fold_in(key_of[3], 1), 0, KG - 1).astype(jnp.int32),
        "tile_counts": draw_tile_counts(jax.random.fold_in(key_of[5], 71), 0),
    }


def reference(t2_amplitudes, integral_tiles, out_tiles, in_tiles, tile_counts):
    row_count = t2_amplitudes.shape[0]
    blocks = t2_amplitudes.reshape(row_count, KG, W)
    flat_tiles = integral_tiles.reshape(N_PAIR * N_VIRT, LIST, W, W)
    flat_outs = out_tiles.reshape(N_PAIR * N_VIRT, LIST)
    flat_ins = in_tiles.reshape(N_PAIR * N_VIRT, LIST)
    flat_counts = tile_counts.reshape(N_PAIR * N_VIRT)
    virt_ids = jnp.tile(jnp.arange(N_VIRT, dtype=jnp.int32), N_PAIR)

    def owner(totals, packed):
        tiles, outs, ins, count, virt_index = packed
        columns = jnp.take(blocks, ins, axis=1)
        product = jnp.einsum("psc,sca->psa", columns, tiles, precision=lax.Precision.HIGHEST)
        is_live = jnp.arange(LIST, dtype=jnp.int32) < count
        local_tiles = outs - virt_index * KV
        selector = ((local_tiles[:, None] == jnp.arange(KV, dtype=jnp.int32)[None, :]) & is_live[:, None]).astype(jnp.float32)
        part_sum = jnp.einsum("psa,sk->pka", product, selector, precision=lax.Precision.HIGHEST)
        offset = (virt_index * KV).astype(jnp.int32)
        current = lax.dynamic_slice_in_dim(totals, offset, KV, 1)
        totals = lax.dynamic_update_slice_in_dim(totals, current + part_sum, offset, 1)
        return totals, None

    start_totals = jnp.zeros((row_count, KG, W), jnp.float32)
    totals, unused = lax.scan(owner, start_totals, (flat_tiles, flat_outs, flat_ins, flat_counts, virt_ids))
    return totals.reshape(row_count, KG * W)
```

```python
import functools

import jax
import jax.numpy as jnp
from jax import lax
from jax.experimental import pallas as pl
from jax.experimental.pallas import tpu as pltpu
from jax.sharding import PartitionSpec as P

W = 128
GROUP = 4


def split(value):
    high = value.astype(jnp.bfloat16)
    low = (value - high.astype(jnp.float32)).astype(jnp.bfloat16)
    return high, low


def ladder_kernel(ins, outs, live, blocks, tiles, result, columns, flat, totals):
    owners, chunk_count = blocks.shape[:2]
    out_tiles = totals.shape[0] - 1
    rows = result.shape[1] // out_tiles
    in_local = blocks.shape[2] // rows
    totals[...] = jnp.zeros_like(totals)

    def spread(owner, carry):
        def one_chunk(chunk, inner):
            for tile in range(in_local):
                flat[tile, pl.ds(chunk * rows, rows), :] = blocks[owner, chunk, tile * rows : (tile + 1) * rows, :]
            return inner

        lax.fori_loop(0, chunk_count, one_chunk, 0, unroll=min(chunk_count, 16))
        for tile in range(in_local):
            high, low = split(flat[tile])
            columns[owner * in_local + tile, :, :W] = high
            columns[owner * in_local + tile, :, W:] = low
        return carry

    lax.fori_loop(0, owners, spread, 0, unroll=min(owners, 2))

    def one_group(index, carry):
        first = index * GROUP
        products = []
        for step in range(GROUP):
            slot = first + step
            high, low = split(tiles[slot])
            both = jnp.concatenate([high, low], axis=1)
            weights = jnp.concatenate([both, both], axis=0)
            got = jnp.dot(columns[ins[slot]], weights, preferred_element_type=jnp.float32)
            products.append(got[:, :W] + got[:, W:])
        for step in range(GROUP):
            slot = first + step
            place = jnp.where(slot < live[0], outs[slot], out_tiles)
            totals[place] = totals[place] + products[step]
        return carry

    lax.fori_loop(0, (live[0] + GROUP - 1) // GROUP, one_group, 0)

    def give(chunk, carry):
        for tile in range(out_tiles):
            result[chunk, tile * rows : (tile + 1) * rows, :] = totals[tile, pl.ds(chunk * rows, rows), :]
        return carry

    lax.fori_loop(0, chunk_count, give, 0, unroll=min(chunk_count, 16))


def local_terms(blocks, tiles, ins, outs, live, rows, out_tiles):
    owners, chunk_count, chunk_rows, _ = blocks.shape
    total_rows = chunk_count * rows
    in_local = chunk_rows // rows
    smem = pl.BlockSpec(memory_space=pltpu.SMEM)
    vmem = pl.BlockSpec(memory_space=pltpu.VMEM)
    return pl.pallas_call(
        ladder_kernel,
        out_shape=jax.ShapeDtypeStruct((chunk_count, out_tiles * rows, W), jnp.float32),
        in_specs=[smem, smem, smem, vmem, vmem],
        out_specs=vmem,
        scratch_shapes=[
            pltpu.VMEM((owners * in_local, total_rows, 2 * W), jnp.bfloat16),
            pltpu.VMEM((in_local, total_rows, W), jnp.float32),
            pltpu.VMEM((out_tiles + 1, total_rows, W), jnp.float32),
        ],
        compiler_params=pltpu.CompilerParams(vmem_limit_bytes=40 * 1024 * 1024),
    )(ins, outs, live, blocks, tiles)


def shards(t2_amplitudes, integral_tiles, out_tiles, in_tiles, tile_counts):
    rows, columns = t2_amplitudes.shape
    local_tiles = columns // W
    slots = integral_tiles.shape[2]
    pairs = lax.axis_size("pair")
    mine = t2_amplitudes.reshape(rows, local_tiles, W).transpose(1, 0, 2).reshape(local_tiles * rows, W)
    spread = jnp.broadcast_to(mine[None], (pairs,) + mine.shape)
    gathered = lax.all_to_all(spread, "pair", 0, 0)
    blocks = lax.all_gather(gathered, "virt", axis=0)
    outs = out_tiles.reshape(slots) - lax.axis_index("virt") * local_tiles
    partial_sums = local_terms(
        blocks,
        integral_tiles.reshape(slots, W, W),
        in_tiles.reshape(slots),
        outs,
        tile_counts.reshape(1),
        rows,
        local_tiles,
    )
    received = lax.all_to_all(partial_sums, "pair", 0, 0)
    summed = jnp.sum(received, axis=0)
    return summed.reshape(local_tiles, rows, W).transpose(1, 0, 2).reshape(rows, columns)


def solution(mesh):
    return jax.shard_map(
        shards,
        mesh=mesh,
        in_specs=(
            P("pair", "virt"),
            P("pair", "virt", None, None, None),
            P("pair", "virt", None),
            P("pair", "virt", None),
            P("pair", "virt"),
        ),
        out_specs=P("pair", "virt"),
        check_vma=False,
    )
```

```python
import functools

import jax
import jax.numpy as jnp
from jax import lax
from jax.experimental import pallas as pl
from jax.experimental.pallas import tpu as pltpu
from jax.sharding import PartitionSpec as P

W = 128
GROUP = 4


def split(value):
    high = value.astype(jnp.bfloat16)
    low = (value - high.astype(jnp.float32)).astype(jnp.bfloat16)
    return high, low


def ladder_kernel(ins, outs, live, blocks, tiles, result, columns, flat, totals):
    owners, chunk_count = blocks.shape[:2]
    out_tiles = totals.shape[0] - 1
    rows = result.shape[1] // out_tiles
    in_local = blocks.shape[2] // rows
    totals[...] = jnp.zeros_like(totals)

    def spread(owner, carry):
        def one_chunk(chunk, inner):
            for tile in range(in_local):
                flat[tile, pl.ds(chunk * rows, rows), :] = blocks[owner, chunk, tile * rows : (tile + 1) * rows, :]
            return inner

        lax.fori_loop(0, chunk_count, one_chunk, 0, unroll=min(chunk_count, 16))
        for tile in range(in_local):
            high, low = split(flat[tile])
            columns[owner * in_local + tile, :, :W] = high
            columns[owner * in_local + tile, :, W:] = low
        return carry

    lax.fori_loop(0, owners, spread, 0, unroll=min(owners, 2))

    def one_group(index, carry):
        first = index * GROUP
        products = []
        for step in range(GROUP):
            slot = first + step
            high, low = split(tiles[slot])
            both = jnp.concatenate([high, low], axis=1)
            weights = jnp.concatenate([both, both], axis=0)
            got = jnp.dot(columns[ins[slot]], weights, preferred_element_type=jnp.float32)
            products.append(got[:, :W] + got[:, W:])
        for step in range(GROUP):
            slot = first + step
            place = jnp.where(slot < live[0], outs[slot], out_tiles)
            totals[place] = totals[place] + products[step]
        return carry

    lax.fori_loop(0, (live[0] + GROUP - 1) // GROUP, one_group, 0)

    def give(chunk, carry):
        for tile in range(out_tiles):
            result[chunk, tile * rows : (tile + 1) * rows, :] = totals[tile, pl.ds(chunk * rows, rows), :]
        return carry

    lax.fori_loop(0, chunk_count, give, 0, unroll=min(chunk_count, 16))


def local_terms(blocks, tiles, ins, outs, live, rows, out_tiles):
    owners, chunk_count, chunk_rows, _ = blocks.shape
    total_rows = chunk_count * rows
    in_local = chunk_rows // rows
    smem = pl.BlockSpec(memory_space=pltpu.SMEM)
    vmem = pl.BlockSpec(memory_space=pltpu.VMEM)
    return pl.pallas_call(
        ladder_kernel,
        out_shape=jax.ShapeDtypeStruct((chunk_count, out_tiles * rows, W), jnp.float32),
        in_specs=[smem, smem, smem, vmem, vmem],
        out_specs=vmem,
        scratch_shapes=[
            pltpu.VMEM((owners * in_local, total_rows, 2 * W), jnp.bfloat16),
            pltpu.VMEM((in_local, total_rows, W), jnp.float32),
            pltpu.VMEM((out_tiles + 1, total_rows, W), jnp.float32),
        ],
        compiler_params=pltpu.CompilerParams(vmem_limit_bytes=40 * 1024 * 1024),
    )(ins, outs, live, blocks, tiles)


def masks_of(size, radices):
    stages, unit = [], size
    for radix in radices:
        unit //= radix
        stages.append([digit * unit for digit in range(1, radix)])
    return stages


def radices_of(size):
    return [4] + [2] * ((size // 4).bit_length() - 1)


def swap(value, axis, size, mask):
    return lax.ppermute(value, axis, [(index, index ^ mask) for index in range(size)])


def gather(value, axis, size):
    held = value[None]
    for masks in masks_of(size, radices_of(size)):
        held = jnp.concatenate([held] + [swap(held, axis, size, mask) for mask in masks], axis=0)
    return held


def scatter_sum(parts, axis, size):
    held = parts
    for masks in reversed(masks_of(size, radices_of(size))):
        pieces = jnp.split(held, len(masks) + 1, axis=0)
        held = pieces[0]
        for mask, piece in zip(masks, pieces[1:]):
            held = held + swap(piece, axis, size, mask)
    return held[0]


def shards(t2_amplitudes, integral_tiles, out_tiles, in_tiles, tile_counts):
    rows, columns = t2_amplitudes.shape
    local_tiles = columns // W
    slots = integral_tiles.shape[2]
    pairs, virts = lax.axis_size("pair"), lax.axis_size("virt")
    virt = lax.axis_index("virt")
    mine = t2_amplitudes.reshape(rows, local_tiles, W).transpose(1, 0, 2).reshape(local_tiles * rows, W)
    blocks = gather(mine, "pair", pairs)
    blocks = lax.all_gather(blocks, "virt", axis=0)
    outs = out_tiles.reshape(slots) - virt * local_tiles
    partial_sums = local_terms(
        blocks,
        integral_tiles.reshape(slots, W, W),
        in_tiles.reshape(slots),
        outs,
        tile_counts.reshape(1),
        rows,
        local_tiles,
    )
    summed = scatter_sum(partial_sums, "pair", pairs)
    return summed.reshape(local_tiles, rows, W).transpose(1, 0, 2).reshape(rows, columns)


def solution(mesh):
    return jax.shard_map(
        shards,
        mesh=mesh,
        in_specs=(
            P("pair", "virt"),
            P("pair", "virt", None, None, None),
            P("pair", "virt", None),
            P("pair", "virt", None),
            P("pair", "virt"),
        ),
        out_specs=P("pair", "virt"),
        check_vma=False,
    )
```

```python
import functools

import jax
import jax.numpy as jnp
from jax import lax
from jax.experimental import pallas as pl
from jax.experimental.pallas import tpu as pltpu
from jax.sharding import PartitionSpec as P

W = 128
GROUP = 4


def split(value):
    high = value.astype(jnp.bfloat16)
    low = (value - high.astype(jnp.float32)).astype(jnp.bfloat16)
    return high, low


def units_of(size):
    return [1 << bit for bit in range(size.bit_length() - 1)]


def ladder_kernel(ins, outs, live, blocks, tiles, result, columns, flat, totals, held, arrived):
    owners, chunk_count = blocks.shape[:2]
    out_tiles = totals.shape[0] - 1
    rows = result.shape[1] // out_tiles
    in_local = blocks.shape[2] // rows
    count = live[0]
    groups = (count + GROUP - 1) // GROUP

    def tile_copy(index):
        part = pl.ds(index * GROUP, GROUP)
        return pltpu.make_async_copy(tiles.at[part], held.at[part], arrived.at[index])

    def begin(index, carry):
        tile_copy(index).start()
        return carry

    lax.fori_loop(0, groups, begin, 0)
    totals[...] = jnp.zeros_like(totals)

    def spread(owner, carry):
        def one_chunk(chunk, inner):
            for tile in range(in_local):
                flat[tile, pl.ds(chunk * rows, rows), :] = blocks[owner, chunk, tile * rows : (tile + 1) * rows, :]
            return inner

        lax.fori_loop(0, chunk_count, one_chunk, 0, unroll=min(chunk_count, 16))
        for tile in range(in_local):
            high, low = split(flat[tile])
            columns[owner * in_local + tile, :, :W] = high
            columns[owner * in_local + tile, :, W:] = low
        return carry

    lax.fori_loop(0, owners, spread, 0, unroll=min(owners, 2))

    def one_group(index, carry):
        tile_copy(index).wait()
        first = index * GROUP
        products = []
        for step in range(GROUP):
            slot = first + step
            high, low = split(held[slot])
            both = jnp.concatenate([high, low], axis=1)
            weights = jnp.concatenate([both, both], axis=0)
            got = jnp.dot(columns[ins[slot]], weights, preferred_element_type=jnp.float32)
            products.append(got[:, :W] + got[:, W:])
        for step in range(GROUP):
            slot = first + step
            place = jnp.where(slot < count, lax.rem(outs[slot], out_tiles), out_tiles)
            totals[place] = totals[place] + products[step]
        return carry

    lax.fori_loop(0, groups, one_group, 0)
    me = lax.axis_index("pair")
    place_of_me = sum(me // unit % 2 * (chunk_count // 2 // unit) for unit in units_of(chunk_count))

    def give(chunk, carry):
        for tile in range(out_tiles):
            piece = totals[tile, pl.ds(chunk * rows, rows), :]
            result[lax.bitwise_xor(chunk, place_of_me), tile * rows : (tile + 1) * rows, :] = piece
        return carry

    lax.fori_loop(0, chunk_count, give, 0, unroll=min(chunk_count, 16))


def local_terms(blocks, tiles, ins, outs, live, rows, out_tiles):
    owners, chunk_count, chunk_rows, _ = blocks.shape
    total_rows = chunk_count * rows
    in_local = chunk_rows // rows
    slots = tiles.shape[0]
    smem = pl.BlockSpec(memory_space=pltpu.SMEM)
    vmem = pl.BlockSpec(memory_space=pltpu.VMEM)
    return pl.pallas_call(
        ladder_kernel,
        out_shape=jax.ShapeDtypeStruct((chunk_count, out_tiles * rows, W), jnp.float32),
        in_specs=[smem, smem, smem, vmem, pl.BlockSpec(memory_space=pltpu.HBM)],
        out_specs=vmem,
        scratch_shapes=[
            pltpu.VMEM((owners * in_local, total_rows, 2 * W), jnp.bfloat16),
            pltpu.VMEM((in_local, total_rows, W), jnp.float32),
            pltpu.VMEM((out_tiles + 1, total_rows, W), jnp.float32),
            pltpu.VMEM((slots, W, W), jnp.float32),
            pltpu.SemaphoreType.DMA((slots // GROUP,)),
        ],
        compiler_params=pltpu.CompilerParams(vmem_limit_bytes=48 * 1024 * 1024),
    )(ins, outs, live, blocks, tiles)


def both_of(value, axis, size, unit):
    groups = [[index, index + unit] for index in range(size) if not index & unit]
    return lax.all_gather(value, axis, axis=0, axis_index_groups=groups)


def gather(value, axis, size):
    held = value[None]
    for unit in reversed(units_of(size)):
        held = both_of(held, axis, size, unit)
        held = held.reshape((-1,) + value.shape)
    return held


def scatter_sum(parts, axis, size):
    me = lax.axis_index(axis)
    held = parts
    for unit in units_of(size):
        half = held.shape[0] // 2
        two = both_of(held[half:], axis, size, unit)
        other = lax.dynamic_index_in_dim(two, 1 - me // unit % 2, 0, keepdims=False)
        held = held[:half] + other
    return held[0]


def shards(t2_amplitudes, integral_tiles, out_tiles, in_tiles, tile_counts):
    rows, columns = t2_amplitudes.shape
    local_tiles = columns // W
    slots = integral_tiles.shape[2]
    pairs = lax.axis_size("pair")
    mine = t2_amplitudes.reshape(rows, local_tiles, W).transpose(1, 0, 2).reshape(local_tiles * rows, W)
    blocks = gather(mine, "pair", pairs)
    blocks = lax.all_gather(blocks, "virt", axis=0)
    partial_sums = local_terms(
        blocks,
        integral_tiles.reshape(slots, W, W),
        in_tiles.reshape(slots),
        out_tiles.reshape(slots),
        tile_counts.reshape(1),
        rows,
        local_tiles,
    )
    summed = scatter_sum(partial_sums, "pair", pairs)
    return summed.reshape(local_tiles, rows, W).transpose(1, 0, 2).reshape(rows, columns)


def solution(mesh):
    return jax.shard_map(
        shards,
        mesh=mesh,
        in_specs=(
            P("pair", "virt"),
            P("pair", "virt", None, None, None),
            P("pair", "virt", None),
            P("pair", "virt", None),
            P("pair", "virt"),
        ),
        out_specs=P("pair", "virt"),
        check_vma=False,
    )
```

```python
import functools

import jax
import jax.numpy as jnp
from jax import lax
from jax.experimental import pallas as pl
from jax.experimental.pallas import tpu as pltpu
from jax.sharding import PartitionSpec as P

W = 128
GROUP = 4


def split(value):
    high = value.astype(jnp.bfloat16)
    low = (value - high.astype(jnp.float32)).astype(jnp.bfloat16)
    return high, low


def ladder_kernel(ins, outs, live, blocks, tiles, result, columns, flat, totals, held, arrived):
    owners, chunk_count = blocks.shape[:2]
    out_tiles = totals.shape[0] - 1
    rows = result.shape[1] // out_tiles
    in_local = blocks.shape[2] // rows
    count = live[0]
    groups = (count + GROUP - 1) // GROUP

    def tile_copy(index):
        part = pl.ds(index * GROUP, GROUP)
        return pltpu.make_async_copy(tiles.at[part], held.at[part], arrived.at[index])

    def begin(index, carry):
        tile_copy(index).start()
        return carry

    lax.fori_loop(0, groups, begin, 0)
    totals[...] = jnp.zeros_like(totals)

    def spread(owner, carry):
        def one_chunk(chunk, inner):
            for tile in range(in_local):
                flat[tile, pl.ds(chunk * rows, rows), :] = blocks[owner, chunk, tile * rows : (tile + 1) * rows, :]
            return inner

        lax.fori_loop(0, chunk_count, one_chunk, 0, unroll=min(chunk_count, 16))
        for tile in range(in_local):
            high, low = split(flat[tile])
            columns[owner * in_local + tile, :, :W] = high
            columns[owner * in_local + tile, :, W:] = low
        return carry

    lax.fori_loop(0, owners, spread, 0, unroll=min(owners, 2))

    def one_group(index, carry):
        tile_copy(index).wait()
        first = index * GROUP
        products = []
        for step in range(GROUP):
            slot = first + step
            high, low = split(held[slot])
            both = jnp.concatenate([high, low], axis=1)
            weights = jnp.concatenate([both, both], axis=0)
            got = jnp.dot(columns[ins[slot]], weights, preferred_element_type=jnp.float32)
            products.append(got[:, :W] + got[:, W:])
        for step in range(GROUP):
            slot = first + step
            place = jnp.where(slot < count, lax.rem(outs[slot], out_tiles), out_tiles)
            totals[place] = totals[place] + products[step]
        return carry

    lax.fori_loop(0, groups, one_group, 0)
    def give(chunk, carry):
        for tile in range(out_tiles):
            piece = totals[tile, pl.ds(chunk * rows, rows), :]
            result[chunk, tile * rows : (tile + 1) * rows, :] = piece
        return carry

    lax.fori_loop(0, chunk_count, give, 0, unroll=min(chunk_count, 16))


def local_terms(blocks, tiles, ins, outs, live, rows, out_tiles):
    owners, chunk_count, chunk_rows, _ = blocks.shape
    total_rows = chunk_count * rows
    in_local = chunk_rows // rows
    slots = tiles.shape[0]
    smem = pl.BlockSpec(memory_space=pltpu.SMEM)
    vmem = pl.BlockSpec(memory_space=pltpu.VMEM)
    return pl.pallas_call(
        ladder_kernel,
        out_shape=jax.ShapeDtypeStruct((chunk_count, out_tiles * rows, W), jnp.float32),
        in_specs=[smem, smem, smem, vmem, pl.BlockSpec(memory_space=pltpu.HBM)],
        out_specs=vmem,
        scratch_shapes=[
            pltpu.VMEM((owners * in_local, total_rows, 2 * W), jnp.bfloat16),
            pltpu.VMEM((in_local, total_rows, W), jnp.float32),
            pltpu.VMEM((out_tiles + 1, total_rows, W), jnp.float32),
            pltpu.VMEM((slots, W, W), jnp.float32),
            pltpu.SemaphoreType.DMA((slots // GROUP,)),
        ],
        compiler_params=pltpu.CompilerParams(vmem_limit_bytes=56 * 1024 * 1024),
    )(ins, outs, live, blocks, tiles)


def groups_of(size):
    inner = min(4, size)
    runs = [list(range(first, first + inner)) for first in range(0, size, inner)]
    strides = [list(range(first, size, inner)) for first in range(inner)]
    return runs, strides


def exchange(value, axis, groups):
    return lax.all_to_all(value, axis, 0, 0, axis_index_groups=groups)


def gather(value, axis, size):
    held = value
    runs, strides = groups_of(size)
    for groups in (strides, runs):
        held = exchange(jnp.broadcast_to(held[None], (len(groups[0]),) + held.shape), axis, groups)
    return held


def scatter_sum(parts, axis, size):
    held = parts
    runs, strides = groups_of(size)
    for groups in (runs, strides):
        held = jnp.sum(exchange(held, axis, groups), axis=0)
    return held


def shards(t2_amplitudes, integral_tiles, out_tiles, in_tiles, tile_counts):
    rows, columns = t2_amplitudes.shape
    local_tiles = columns // W
    slots = integral_tiles.shape[2]
    pairs = lax.axis_size("pair")
    mine = t2_amplitudes.reshape(rows, local_tiles, W).transpose(1, 0, 2).reshape(local_tiles * rows, W)
    gathered = gather(mine, "pair", pairs)
    blocks = lax.all_gather(gathered, "virt", axis=0)
    blocks = blocks.reshape((-1, pairs) + mine.shape)
    partial_sums = local_terms(
        blocks,
        integral_tiles.reshape(slots, W, W),
        in_tiles.reshape(slots),
        out_tiles.reshape(slots),
        tile_counts.reshape(1),
        rows,
        local_tiles,
    )
    summed = scatter_sum(partial_sums.reshape(gathered.shape), "pair", pairs)
    return summed.reshape(local_tiles, rows, W).transpose(1, 0, 2).reshape(rows, columns)


def solution(mesh):
    return jax.shard_map(
        shards,
        mesh=mesh,
        in_specs=(
            P("pair", "virt"),
            P("pair", "virt", None, None, None),
            P("pair", "virt", None),
            P("pair", "virt", None),
            P("pair", "virt"),
        ),
        out_specs=P("pair", "virt"),
        check_vma=False,
    )
```

```python
import jax
import jax.numpy as jnp
from jax import lax
from jax.experimental import pallas as pl
from jax.experimental.pallas import tpu as pltpu
from jax.sharding import PartitionSpec as P

W = 128
GROUP = 8
SMEM = pl.BlockSpec(memory_space=pltpu.SMEM)
VMEM = pl.BlockSpec(memory_space=pltpu.VMEM)


def split(value):
    high = value.astype(jnp.bfloat16)
    low = (value - high.astype(jnp.float32)).astype(jnp.bfloat16)
    return high, low


def repeat_kernel(value, result):
    held = value[...]
    for copy in range(result.shape[0]):
        result[copy] = held


def repeat(value, count):
    return pl.pallas_call(
        repeat_kernel,
        out_shape=jax.ShapeDtypeStruct((count,) + value.shape, value.dtype),
        in_specs=[VMEM],
        out_specs=VMEM,
    )(value)


def tile_kernel(out_tiles, ins, outs, live, tiles, halves, codes, held, arrived):
    count = live[0, 0]
    groups = (count + GROUP - 1) // GROUP

    def tile_copy(index):
        part = pl.ds(index * GROUP, GROUP)
        return pltpu.make_async_copy(tiles.at[part], held.at[part], arrived.at[index])

    def begin(index, carry):
        tile_copy(index).start()
        return carry

    lax.fori_loop(0, groups, begin, 0)
    slots = lax.broadcasted_iota(jnp.int32, ins.shape, 1)
    codes[0:1, :] = ins[...]
    codes[1:2, :] = jnp.where(slots < count, lax.rem(outs[...], out_tiles), out_tiles)
    codes[2:3, :] = jnp.full(ins.shape, count, jnp.int32)

    def one_group(index, carry):
        tile_copy(index).wait()
        for step in range(GROUP):
            slot = index * GROUP + step
            high, low = split(held[slot])
            halves[slot, :, :W] = high
            halves[slot, :, W:] = low
        return carry

    lax.fori_loop(0, groups, one_group, 0)


def prepare_tiles(tiles, ins, outs, live, out_tiles):
    slots = tiles.shape[0]

    def kernel(*refs):
        tile_kernel(out_tiles, *refs)

    return pl.pallas_call(
        kernel,
        out_shape=(
            jax.ShapeDtypeStruct((slots, W, 2 * W), jnp.bfloat16),
            jax.ShapeDtypeStruct((3, slots), jnp.int32),
        ),
        in_specs=[VMEM, VMEM, SMEM, pl.BlockSpec(memory_space=pltpu.HBM)],
        out_specs=(VMEM, VMEM),
        scratch_shapes=[pltpu.VMEM((slots, W, W), jnp.float32), pltpu.SemaphoreType.DMA((slots // GROUP,))],
        compiler_params=pltpu.CompilerParams(vmem_limit_bytes=32 * 1024 * 1024),
        cost_estimate=pl.CostEstimate(flops=4 * slots * W * W, bytes_accessed=8 * slots * W * W, transcendentals=0),
    )(ins, outs, live, tiles)


def ladder_kernel(codes, blocks, halves, result, columns, flat, totals):
    owners, chunk_count = blocks.shape[:2]
    out_tiles = totals.shape[0] - 1
    rows = result.shape[1] // out_tiles
    in_local = blocks.shape[2] // rows
    totals[...] = jnp.zeros_like(totals)

    def spread(owner, carry):
        def one_chunk(chunk, inner):
            for tile in range(in_local):
                flat[tile, pl.ds(chunk * rows, rows), :] = blocks[owner, chunk, tile * rows : (tile + 1) * rows, :]
            return inner

        lax.fori_loop(0, chunk_count, one_chunk, 0, unroll=min(chunk_count, 16))
        for tile in range(in_local):
            high, low = split(flat[tile])
            columns[owner * in_local + tile, :, :W] = high
            columns[owner * in_local + tile, :, W:] = low
        return carry

    lax.fori_loop(0, owners, spread, 0, unroll=min(owners, 2))

    def one_group(index, carry):
        first = index * GROUP
        products = []
        for step in range(GROUP):
            both = halves[first + step]
            weights = jnp.concatenate([both, both], axis=0)
            got = jnp.dot(columns[codes[0, first + step]], weights, preferred_element_type=jnp.float32)
            products.append(got[:, :W] + got[:, W:])
        for step in range(GROUP):
            place = codes[1, first + step]
            totals[place] = totals[place] + products[step]
        return carry

    lax.fori_loop(0, (codes[2, 0] + GROUP - 1) // GROUP, one_group, 0)

    def give(chunk, carry):
        for tile in range(out_tiles):
            result[chunk, tile * rows : (tile + 1) * rows, :] = totals[tile, pl.ds(chunk * rows, rows), :]
        return carry

    lax.fori_loop(0, chunk_count, give, 0, unroll=min(chunk_count, 16))


def local_terms(codes, blocks, halves, rows, out_tiles):
    owners, chunk_count, chunk_rows, _ = blocks.shape
    total_rows = chunk_count * rows
    in_local = chunk_rows // rows
    return pl.pallas_call(
        ladder_kernel,
        out_shape=jax.ShapeDtypeStruct((chunk_count, out_tiles * rows, W), jnp.float32),
        in_specs=[SMEM, VMEM, VMEM],
        out_specs=VMEM,
        scratch_shapes=[
            pltpu.VMEM((owners * in_local, total_rows, 2 * W), jnp.bfloat16),
            pltpu.VMEM((in_local, total_rows, W), jnp.float32),
            pltpu.VMEM((out_tiles + 1, total_rows, W), jnp.float32),
        ],
        compiler_params=pltpu.CompilerParams(vmem_limit_bytes=32 * 1024 * 1024),
    )(codes, blocks, halves)


def shards(t2_amplitudes, integral_tiles, out_tiles, in_tiles, tile_counts):
    rows, columns = t2_amplitudes.shape
    local_tiles = columns // W
    slots = integral_tiles.shape[2]
    pairs = lax.axis_size("pair")
    mine = t2_amplitudes.reshape(rows, local_tiles, W).transpose(1, 0, 2).reshape(local_tiles * rows, W)
    gathered = lax.all_to_all(repeat(mine, pairs), "pair", 0, 0)
    halves, codes = prepare_tiles(
        integral_tiles.reshape(slots, W, W),
        in_tiles.reshape(1, slots),
        out_tiles.reshape(1, slots),
        tile_counts,
        local_tiles,
    )
    blocks = lax.all_gather(gathered, "virt", axis=0)
    partial_sums = local_terms(codes, blocks, halves, rows, local_tiles)
    received = lax.all_to_all(partial_sums, "pair", 0, 0)
    summed = jnp.sum(received, axis=0)
    return summed.reshape(local_tiles, rows, W).transpose(1, 0, 2).reshape(rows, columns)


def solution(mesh):
    return jax.shard_map(
        shards,
        mesh=mesh,
        in_specs=(
            P("pair", "virt"),
            P("pair", "virt", None, None, None),
            P("pair", "virt", None),
            P("pair", "virt", None),
            P("pair", "virt"),
        ),
        out_specs=P("pair", "virt"),
        check_vma=False,
    )
```

```python
import jax
import jax.numpy as jnp
from jax import lax
from jax.experimental import pallas as pl
from jax.experimental.pallas import tpu as pltpu
from jax.sharding import PartitionSpec as P

W = 128
GROUP = 8
NEAR = 4
SMEM = pl.BlockSpec(memory_space=pltpu.SMEM)
VMEM = pl.BlockSpec(memory_space=pltpu.VMEM)


def split(value):
    high = value.astype(jnp.bfloat16)
    low = (value - high.astype(jnp.float32)).astype(jnp.bfloat16)
    return high, low


def tile_kernel(out_tiles, live, ins, outs, tiles, mine, halves, codes, own, held, index_rows, arrived, singles):
    singles_of = ((ins, index_rows.at[0]), (outs, index_rows.at[1]), (mine, own))
    others = [pltpu.make_async_copy(here, there, singles.at[at]) for at, (here, there) in enumerate(singles_of)]
    for copy in others:
        copy.start()
    count = live[0, 0]
    groups = (count + GROUP - 1) // GROUP

    def tile_copy(index):
        part = pl.ds(index * GROUP, GROUP)
        return pltpu.make_async_copy(tiles.at[part], held.at[part], arrived.at[index])

    def begin(index, carry):
        tile_copy(index).start()
        return carry

    lax.fori_loop(0, groups, begin, 0)
    for copy in others:
        copy.wait()
    slots = lax.broadcasted_iota(jnp.int32, ins.shape, 1)
    codes[0:1, :] = index_rows[0]
    codes[1:2, :] = jnp.where(slots < count, lax.rem(index_rows[1], out_tiles), out_tiles)
    codes[2:3, :] = jnp.full(ins.shape, count, jnp.int32)

    def one_group(index, carry):
        tile_copy(index).wait()
        for step in range(GROUP):
            slot = index * GROUP + step
            high, low = split(held[slot])
            halves[slot, :, :W] = high
            halves[slot, :, W:] = low
        return carry

    lax.fori_loop(0, groups, one_group, 0)


def prepare(tiles, ins, outs, live, mine, out_tiles):
    slots = tiles.shape[0]

    def kernel(*refs):
        tile_kernel(out_tiles, *refs)

    operands = [pltpu.with_memory_space_constraint(value, pltpu.HBM) for value in (ins, outs, tiles, mine)]
    return pl.pallas_call(
        kernel,
        out_shape=(
            jax.ShapeDtypeStruct((slots, W, 2 * W), jnp.bfloat16),
            jax.ShapeDtypeStruct((3, slots), jnp.int32),
            jax.ShapeDtypeStruct(mine.shape, mine.dtype),
        ),
        in_specs=[SMEM] + [pl.BlockSpec(memory_space=pltpu.HBM)] * 4,
        out_specs=(VMEM, VMEM, VMEM),
        scratch_shapes=[
            pltpu.VMEM((slots, W, W), jnp.float32),
            pltpu.VMEM((2, 1, slots), jnp.int32),
            pltpu.SemaphoreType.DMA((slots // GROUP,)),
            pltpu.SemaphoreType.DMA((3,)),
        ],
        compiler_params=pltpu.CompilerParams(vmem_limit_bytes=32 * 1024 * 1024),
        cost_estimate=pl.CostEstimate(flops=4 * slots * W * W, bytes_accessed=8 * slots * W * W, transcendentals=0),
    )(live, *operands)


def ladder_kernel(codes, blocks, halves, result, columns, flat, totals):
    owners, chunk_count = blocks.shape[:2]
    out_tiles = totals.shape[0] - 1
    rows = result.shape[1] // out_tiles
    in_local = blocks.shape[2] // rows
    totals[...] = jnp.zeros_like(totals)

    def spread(owner, carry):
        def one_chunk(chunk, inner):
            for tile in range(in_local):
                flat[tile, pl.ds(chunk * rows, rows), :] = blocks[owner, chunk, tile * rows : (tile + 1) * rows, :]
            return inner

        lax.fori_loop(0, chunk_count, one_chunk, 0, unroll=min(chunk_count, 16))
        for tile in range(in_local):
            high, low = split(flat[tile])
            columns[owner * in_local + tile, :, :W] = high
            columns[owner * in_local + tile, :, W:] = low
        return carry

    lax.fori_loop(0, owners, spread, 0, unroll=min(owners, 2))

    def one_group(index, carry):
        first = index * GROUP
        products = []
        for step in range(GROUP):
            both = halves[first + step]
            weights = jnp.concatenate([both, both], axis=0)
            got = jnp.dot(columns[codes[0, first + step]], weights, preferred_element_type=jnp.float32)
            products.append(got[:, :W] + got[:, W:])
        for step in range(GROUP):
            place = codes[1, first + step]
            totals[place] = totals[place] + products[step]
        return carry

    lax.fori_loop(0, (codes[2, 0] + GROUP - 1) // GROUP, one_group, 0)
    me = lax.axis_index("pair")
    far = chunk_count // NEAR

    def give(chunk, carry):
        device = lax.bitwise_xor(me, lax.rem(chunk, far) * NEAR + chunk // far)
        for tile in range(out_tiles):
            result[device, tile * rows : (tile + 1) * rows, :] = totals[tile, pl.ds(chunk * rows, rows), :]
        return carry

    lax.fori_loop(0, chunk_count, give, 0, unroll=min(chunk_count, 16))


def local_terms(codes, blocks, halves, rows, out_tiles):
    owners, chunk_count, chunk_rows, _ = blocks.shape
    total_rows = chunk_count * rows
    in_local = chunk_rows // rows
    return pl.pallas_call(
        ladder_kernel,
        out_shape=jax.ShapeDtypeStruct((chunk_count, out_tiles * rows, W), jnp.float32),
        in_specs=[SMEM, VMEM, VMEM],
        out_specs=VMEM,
        scratch_shapes=[
            pltpu.VMEM((owners * in_local, total_rows, 2 * W), jnp.bfloat16),
            pltpu.VMEM((in_local, total_rows, W), jnp.float32),
            pltpu.VMEM((out_tiles + 1, total_rows, W), jnp.float32),
        ],
        compiler_params=pltpu.CompilerParams(vmem_limit_bytes=32 * 1024 * 1024),
    )(codes, blocks, halves)


def from_partners(value, axis, size, masks):
    return [lax.ppermute(value, axis, [(index, index ^ mask) for index in range(size)]) for mask in masks]


def shards(t2_amplitudes, integral_tiles, out_tiles, in_tiles, tile_counts):
    rows, columns = t2_amplitudes.shape
    local_tiles = columns // W
    slots = integral_tiles.shape[2]
    pairs = lax.axis_size("pair")
    mine = t2_amplitudes.reshape(rows, local_tiles, W).transpose(1, 0, 2).reshape(local_tiles * rows, W)
    halves, codes, own = prepare(
        integral_tiles.reshape(slots, W, W),
        in_tiles.reshape(1, slots),
        out_tiles.reshape(1, slots),
        tile_counts,
        mine,
        local_tiles,
    )
    line = jnp.stack([own] + from_partners(mine, "pair", pairs, range(NEAR, pairs, NEAR)))
    gathered = jnp.concatenate([line] + from_partners(line, "pair", pairs, range(1, NEAR)))
    blocks = lax.all_gather(gathered, "virt", axis=0)
    partial_sums = local_terms(codes, blocks, halves, rows, local_tiles)
    received = lax.all_to_all(partial_sums, "pair", 0, 0)
    summed = jnp.sum(received, axis=0)
    return summed.reshape(local_tiles, rows, W).transpose(1, 0, 2).reshape(rows, columns)


def solution(mesh):
    return jax.shard_map(
        shards,
        mesh=mesh,
        in_specs=(
            P("pair", "virt"),
            P("pair", "virt", None, None, None),
            P("pair", "virt", None),
            P("pair", "virt", None),
            P("pair", "virt"),
        ),
        out_specs=P("pair", "virt"),
        check_vma=False,
    )
```

```python
import jax
import jax.numpy as jnp
from jax import lax
from jax.experimental import pallas as pl
from jax.experimental.pallas import tpu as pltpu
from jax.sharding import PartitionSpec as P

W = 128
GROUP = 8
NEAR = 4
SMEM = pl.BlockSpec(memory_space=pltpu.SMEM)
VMEM = pl.BlockSpec(memory_space=pltpu.VMEM)


def split(value):
    high = value.astype(jnp.bfloat16)
    low = (value - high.astype(jnp.float32)).astype(jnp.bfloat16)
    return high, low


def tile_kernel(out_tiles, live, ins, outs, tiles, mine, halves, codes, own, held, index_rows, arrived, singles):
    singles_of = ((ins, index_rows.at[0]), (outs, index_rows.at[1]), (mine, own))
    others = [pltpu.make_async_copy(here, there, singles.at[at]) for at, (here, there) in enumerate(singles_of)]
    for copy in others:
        copy.start()
    count = live[0, 0]
    groups = (count + GROUP - 1) // GROUP

    def tile_copy(index):
        part = pl.ds(index * GROUP, GROUP)
        return pltpu.make_async_copy(tiles.at[part], held.at[part], arrived.at[index])

    def begin(index, carry):
        tile_copy(index).start()
        return carry

    lax.fori_loop(0, groups, begin, 0)
    for copy in others:
        copy.wait()
    slots = lax.broadcasted_iota(jnp.int32, ins.shape, 1)
    codes[0:1, :] = index_rows[0]
    codes[1:2, :] = jnp.where(slots < count, lax.rem(index_rows[1], out_tiles), out_tiles)
    codes[2:3, :] = jnp.full(ins.shape, count, jnp.int32)

    def one_group(index, carry):
        tile_copy(index).wait()
        for step in range(GROUP):
            slot = index * GROUP + step
            high, low = split(held[slot])
            halves[slot, :, :W] = high
            halves[slot, :, W:] = low
        return carry

    lax.fori_loop(0, groups, one_group, 0)


def prepare(tiles, ins, outs, live, mine, out_tiles):
    slots = tiles.shape[0]

    def kernel(*refs):
        tile_kernel(out_tiles, *refs)

    operands = [pltpu.with_memory_space_constraint(value, pltpu.HBM) for value in (ins, outs, tiles, mine)]
    return pl.pallas_call(
        kernel,
        out_shape=(
            jax.ShapeDtypeStruct((slots, W, 2 * W), jnp.bfloat16),
            jax.ShapeDtypeStruct((3, slots), jnp.int32),
            jax.ShapeDtypeStruct(mine.shape, mine.dtype),
        ),
        in_specs=[SMEM] + [pl.BlockSpec(memory_space=pltpu.HBM)] * 4,
        out_specs=(VMEM, VMEM, VMEM),
        scratch_shapes=[
            pltpu.VMEM((slots, W, W), jnp.float32),
            pltpu.VMEM((2, 1, slots), jnp.int32),
            pltpu.SemaphoreType.DMA((slots // GROUP,)),
            pltpu.SemaphoreType.DMA((3,)),
        ],
        compiler_params=pltpu.CompilerParams(vmem_limit_bytes=32 * 1024 * 1024),
        cost_estimate=pl.CostEstimate(flops=4 * slots * W * W, bytes_accessed=8 * slots * W * W, transcendentals=0),
    )(live, *operands)


def ladder_kernel(codes, blocks, halves, result, columns, flat, totals):
    owners, chunk_count = blocks.shape[:2]
    out_tiles = totals.shape[0] - 1
    rows = result.shape[1] // out_tiles
    in_local = blocks.shape[2] // rows
    totals[...] = jnp.zeros_like(totals)

    far = chunk_count // NEAR

    def spread(owner, carry):
        def one_chunk(chunk, inner):
            crossed = (chunk >= far).astype(jnp.int32) ^ (lax.rem(chunk, far) > 0).astype(jnp.int32)
            source = lax.bitwise_xor(owner, crossed)
            for tile in range(in_local):
                flat[tile, pl.ds(chunk * rows, rows), :] = blocks[source, chunk, tile * rows : (tile + 1) * rows, :]
            return inner

        lax.fori_loop(0, chunk_count, one_chunk, 0, unroll=min(chunk_count, 16))
        for tile in range(in_local):
            high, low = split(flat[tile])
            columns[owner * in_local + tile, :, :W] = high
            columns[owner * in_local + tile, :, W:] = low
        return carry

    lax.fori_loop(0, owners, spread, 0, unroll=min(owners, 2))

    def one_group(index, carry):
        first = index * GROUP
        products = []
        for step in range(GROUP):
            both = halves[first + step]
            weights = jnp.concatenate([both, both], axis=0)
            got = jnp.dot(columns[codes[0, first + step]], weights, preferred_element_type=jnp.float32)
            products.append(got[:, :W] + got[:, W:])
        for step in range(GROUP):
            place = codes[1, first + step]
            totals[place] = totals[place] + products[step]
        return carry

    lax.fori_loop(0, (codes[2, 0] + GROUP - 1) // GROUP, one_group, 0)
    me = lax.axis_index("pair")

    def give(chunk, carry):
        device = lax.bitwise_xor(me, lax.rem(chunk, far) * NEAR + chunk // far)
        for tile in range(out_tiles):
            result[device, tile * rows : (tile + 1) * rows, :] = totals[tile, pl.ds(chunk * rows, rows), :]
        return carry

    lax.fori_loop(0, chunk_count, give, 0, unroll=min(chunk_count, 16))


def local_terms(codes, blocks, halves, rows, out_tiles):
    owners, chunk_count, chunk_rows, _ = blocks.shape
    total_rows = chunk_count * rows
    in_local = chunk_rows // rows
    return pl.pallas_call(
        ladder_kernel,
        out_shape=jax.ShapeDtypeStruct((chunk_count, out_tiles * rows, W), jnp.float32),
        in_specs=[SMEM, VMEM, VMEM],
        out_specs=VMEM,
        scratch_shapes=[
            pltpu.VMEM((owners * in_local, total_rows, 2 * W), jnp.bfloat16),
            pltpu.VMEM((in_local, total_rows, W), jnp.float32),
            pltpu.VMEM((out_tiles + 1, total_rows, W), jnp.float32),
        ],
        compiler_params=pltpu.CompilerParams(vmem_limit_bytes=32 * 1024 * 1024),
    )(codes, blocks, halves)


def from_partners(value, pairs, virts, masks):
    received = []
    for mask in masks:
        routes = [(a * virts + b, (a ^ mask) * virts + (b ^ 1)) for a in range(pairs) for b in range(virts)]
        received.append(lax.ppermute(value, ("pair", "virt"), routes))
    return received


def shards(t2_amplitudes, integral_tiles, out_tiles, in_tiles, tile_counts):
    rows, columns = t2_amplitudes.shape
    local_tiles = columns // W
    slots = integral_tiles.shape[2]
    pairs, virts = lax.axis_size("pair"), lax.axis_size("virt")
    mine = t2_amplitudes.reshape(rows, local_tiles, W).transpose(1, 0, 2).reshape(local_tiles * rows, W)
    halves, codes, own = prepare(
        integral_tiles.reshape(slots, W, W),
        in_tiles.reshape(1, slots),
        out_tiles.reshape(1, slots),
        tile_counts,
        mine,
        local_tiles,
    )
    line = jnp.stack([own] + from_partners(mine, pairs, virts, range(NEAR, pairs, NEAR)))
    gathered = jnp.concatenate([line] + from_partners(line, pairs, virts, range(1, NEAR)))
    blocks = lax.all_gather(gathered, "virt", axis=0)
    partial_sums = local_terms(codes, blocks, halves, rows, local_tiles)
    received = lax.all_to_all(partial_sums, "pair", 0, 0)
    summed = jnp.sum(received, axis=0)
    return summed.reshape(local_tiles, rows, W).transpose(1, 0, 2).reshape(rows, columns)


def solution(mesh):
    return jax.shard_map(
        shards,
        mesh=mesh,
        in_specs=(
            P("pair", "virt"),
            P("pair", "virt", None, None, None),
            P("pair", "virt", None),
            P("pair", "virt", None),
            P("pair", "virt"),
        ),
        out_specs=P("pair", "virt"),
        check_vma=False,
    )
```

```python
import jax
import jax.numpy as jnp
from jax import lax
from jax.experimental import pallas as pl
from jax.experimental.pallas import tpu as pltpu
from jax.sharding import PartitionSpec as P

W = 128
GROUP = 8
NEAR = 4
SMEM = pl.BlockSpec(memory_space=pltpu.SMEM)
VMEM = pl.BlockSpec(memory_space=pltpu.VMEM)


def split(value):
    high = value.astype(jnp.bfloat16)
    low = (value - high.astype(jnp.float32)).astype(jnp.bfloat16)
    return high, low


def tile_kernel(out_tiles, live, ins, outs, tiles, mine, halves, codes, own, held, index_rows, arrived, singles):
    singles_of = ((ins, index_rows.at[0]), (outs, index_rows.at[1]), (mine, own))
    others = [pltpu.make_async_copy(here, there, singles.at[at]) for at, (here, there) in enumerate(singles_of)]
    for copy in others:
        copy.start()
    count = live[0, 0]
    groups = (count + GROUP - 1) // GROUP

    def tile_copy(index):
        part = pl.ds(index * GROUP, GROUP)
        return pltpu.make_async_copy(tiles.at[part], held.at[part], arrived.at[index])

    def begin(index, carry):
        tile_copy(index).start()
        return carry

    lax.fori_loop(0, groups, begin, 0)
    for copy in others:
        copy.wait()
    slots = lax.broadcasted_iota(jnp.int32, ins.shape, 1)
    codes[0:1, :] = index_rows[0]
    codes[1:2, :] = jnp.where(slots < count, lax.rem(index_rows[1], out_tiles), out_tiles)
    codes[2:3, :] = jnp.full(ins.shape, count, jnp.int32)

    def one_group(index, carry):
        tile_copy(index).wait()
        for step in range(GROUP):
            slot = index * GROUP + step
            high, low = split(held[slot])
            halves[slot, :, :W] = high
            halves[slot, :, W:] = low
        return carry

    lax.fori_loop(0, groups, one_group, 0)


def prepare(tiles, ins, outs, live, mine, out_tiles):
    slots = tiles.shape[0]

    def kernel(*refs):
        tile_kernel(out_tiles, *refs)

    operands = [pltpu.with_memory_space_constraint(value, pltpu.HBM) for value in (ins, outs, tiles, mine)]
    return pl.pallas_call(
        kernel,
        out_shape=(
            jax.ShapeDtypeStruct((slots, W, 2 * W), jnp.bfloat16),
            jax.ShapeDtypeStruct((3, slots), jnp.int32),
            jax.ShapeDtypeStruct(mine.shape, mine.dtype),
        ),
        in_specs=[SMEM] + [pl.BlockSpec(memory_space=pltpu.HBM)] * 4,
        out_specs=(VMEM, VMEM, VMEM),
        scratch_shapes=[
            pltpu.VMEM((slots, W, W), jnp.float32),
            pltpu.VMEM((2, 1, slots), jnp.int32),
            pltpu.SemaphoreType.DMA((slots // GROUP,)),
            pltpu.SemaphoreType.DMA((3,)),
        ],
        compiler_params=pltpu.CompilerParams(vmem_limit_bytes=32 * 1024 * 1024),
        cost_estimate=pl.CostEstimate(flops=4 * slots * W * W, bytes_accessed=8 * slots * W * W, transcendentals=0),
    )(live, *operands)


def ladder_kernel(codes, blocks, halves, result, columns, flat, totals):
    owners, chunk_count = blocks.shape[:2]
    out_tiles = totals.shape[0] - 1
    rows = result.shape[2] // out_tiles
    in_local = blocks.shape[2] // rows
    totals[...] = jnp.zeros_like(totals)

    far = chunk_count // NEAR

    def spread(owner, carry):
        def one_chunk(chunk, inner):
            crossed = (chunk >= far).astype(jnp.int32) ^ (lax.rem(chunk, far) > 0).astype(jnp.int32)
            source = lax.bitwise_xor(owner, crossed)
            for tile in range(in_local):
                flat[tile, pl.ds(chunk * rows, rows), :] = blocks[source, chunk, tile * rows : (tile + 1) * rows, :]
            return inner

        lax.fori_loop(0, chunk_count, one_chunk, 0, unroll=min(chunk_count, 16))
        for tile in range(in_local):
            high, low = split(flat[tile])
            columns[owner * in_local + tile, :, :W] = high
            columns[owner * in_local + tile, :, W:] = low
        return carry

    lax.fori_loop(0, owners, spread, 0, unroll=min(owners, 2))

    def one_group(index, carry):
        first = index * GROUP
        products = []
        for step in range(GROUP):
            both = halves[first + step]
            weights = jnp.concatenate([both, both], axis=0)
            got = jnp.dot(columns[codes[0, first + step]], weights, preferred_element_type=jnp.float32)
            products.append(got[:, :W] + got[:, W:])
        for step in range(GROUP):
            place = codes[1, first + step]
            totals[place] = totals[place] + products[step]
        return carry

    lax.fori_loop(0, (codes[2, 0] + GROUP - 1) // GROUP, one_group, 0)
    turned = lax.rem(lax.axis_index("virt"), 2) == 1

    def give(chunk, carry):
        a, b = chunk // far, lax.rem(chunk, far)
        low, next_low = lax.rem(a, 2), a // 2
        side = jnp.where(turned, next_low, low)
        place = b * (NEAR // 2) + jnp.where(turned, low, next_low)
        for tile in range(out_tiles):
            result[side, place, tile * rows : (tile + 1) * rows, :] = totals[tile, pl.ds(chunk * rows, rows), :]
        return carry

    lax.fori_loop(0, chunk_count, give, 0, unroll=min(chunk_count, 16))


def local_terms(codes, blocks, halves, rows, out_tiles):
    owners, chunk_count, chunk_rows, _ = blocks.shape
    total_rows = chunk_count * rows
    in_local = chunk_rows // rows
    return pl.pallas_call(
        ladder_kernel,
        out_shape=jax.ShapeDtypeStruct((2, chunk_count // 2, out_tiles * rows, W), jnp.float32),
        in_specs=[SMEM, VMEM, VMEM],
        out_specs=VMEM,
        scratch_shapes=[
            pltpu.VMEM((owners * in_local, total_rows, 2 * W), jnp.bfloat16),
            pltpu.VMEM((in_local, total_rows, W), jnp.float32),
            pltpu.VMEM((out_tiles + 1, total_rows, W), jnp.float32),
        ],
        compiler_params=pltpu.CompilerParams(vmem_limit_bytes=32 * 1024 * 1024),
    )(codes, blocks, halves)


def from_partners(value, pairs, virts, masks):
    received = []
    for mask in masks:
        routes = [(a * virts + b, (a ^ mask) * virts + (b ^ 1)) for a in range(pairs) for b in range(virts)]
        received.append(lax.ppermute(value, ("pair", "virt"), routes))
    return received


def distance(place, side, b):
    mask = 2 * place + side
    return mask if b % 2 == 0 else mask & ~3 | (mask & 1) << 1 | (mask & 2) >> 1


def exchange_routes(pairs, virts):
    return [(a * virts + b, (a ^ distance(0, 1, b)) * virts + b) for a in range(pairs) for b in range(virts)]


def one_way_routes(pairs, virts, place, half):
    return [
        (a * virts + b, (a ^ distance(place, 1, b)) * virts + b)
        for a in range(pairs)
        for b in range(virts)
        if ((a & distance(0, 1, b)) != 0) == half
    ]


def scatter_sum(parts, pairs, virts):
    axes = ("pair", "virt")
    held = parts[1] + lax.ppermute(parts[0], axes, exchange_routes(pairs, virts))
    received = []
    for half in (False, True):
        if half:
            held, received[0] = lax.optimization_barrier((held, received[0]))
        received += [
            lax.ppermute(held[place], axes, one_way_routes(pairs, virts, place, half)) for place in range(pairs // 2)
        ]
    return sum(received[1:], received[0])


def shards(t2_amplitudes, integral_tiles, out_tiles, in_tiles, tile_counts):
    rows, columns = t2_amplitudes.shape
    local_tiles = columns // W
    slots = integral_tiles.shape[2]
    pairs, virts = lax.axis_size("pair"), lax.axis_size("virt")
    mine = t2_amplitudes.reshape(rows, local_tiles, W).transpose(1, 0, 2).reshape(local_tiles * rows, W)
    halves, codes, own = prepare(
        integral_tiles.reshape(slots, W, W),
        in_tiles.reshape(1, slots),
        out_tiles.reshape(1, slots),
        tile_counts,
        mine,
        local_tiles,
    )
    line = jnp.stack([own] + from_partners(mine, pairs, virts, range(NEAR, pairs, NEAR)))
    gathered = jnp.concatenate([line] + from_partners(line, pairs, virts, range(1, NEAR)))
    blocks = lax.all_gather(gathered, "virt", axis=0)
    partial_sums = local_terms(codes, blocks, halves, rows, local_tiles)
    summed = scatter_sum(partial_sums, pairs, virts)
    return summed.reshape(local_tiles, rows, W).transpose(1, 0, 2).reshape(rows, columns)


def solution(mesh):
    return jax.shard_map(
        shards,
        mesh=mesh,
        in_specs=(
            P("pair", "virt"),
            P("pair", "virt", None, None, None),
            P("pair", "virt", None),
            P("pair", "virt", None),
            P("pair", "virt"),
        ),
        out_specs=P("pair", "virt"),
        check_vma=False,
    )
```

```python
import jax
import jax.numpy as jnp
from jax import lax
from jax.experimental import pallas as pl
from jax.experimental.pallas import tpu as pltpu
from jax.sharding import PartitionSpec as P

W = 128
GROUP = 8
NEAR = 4
SMEM = pl.BlockSpec(memory_space=pltpu.SMEM)
VMEM = pl.BlockSpec(memory_space=pltpu.VMEM)


def split(value):
    high = value.astype(jnp.bfloat16)
    low = (value - high.astype(jnp.float32)).astype(jnp.bfloat16)
    return high, low


def tile_kernel(out_tiles, live, ins, outs, tiles, mine, halves, codes, own, held, index_rows, arrived, singles):
    singles_of = ((ins, index_rows.at[0]), (outs, index_rows.at[1]), (mine, own))
    others = [pltpu.make_async_copy(here, there, singles.at[at]) for at, (here, there) in enumerate(singles_of)]
    for copy in others:
        copy.start()
    count = live[0, 0]
    groups = (count + GROUP - 1) // GROUP

    def tile_copy(index):
        part = pl.ds(index * GROUP, GROUP)
        return pltpu.make_async_copy(tiles.at[part], held.at[part], arrived.at[index])

    def begin(index, carry):
        tile_copy(index).start()
        return carry

    lax.fori_loop(0, groups, begin, 0)
    for copy in others:
        copy.wait()
    slots = lax.broadcasted_iota(jnp.int32, ins.shape, 1)
    codes[0:1, :] = index_rows[0]
    codes[1:2, :] = jnp.where(slots < count, lax.rem(index_rows[1], out_tiles), out_tiles)
    codes[2:3, :] = jnp.full(ins.shape, count, jnp.int32)

    def one_group(index, carry):
        tile_copy(index).wait()
        for step in range(GROUP):
            slot = index * GROUP + step
            high, low = split(held[slot])
            halves[slot, :, :W] = high
            halves[slot, :, W:] = low
        return carry

    lax.fori_loop(0, groups, one_group, 0)


def prepare(tiles, ins, outs, live, mine, out_tiles):
    slots = tiles.shape[0]

    def kernel(*refs):
        tile_kernel(out_tiles, *refs)

    operands = [pltpu.with_memory_space_constraint(value, pltpu.HBM) for value in (ins, outs, tiles, mine)]
    return pl.pallas_call(
        kernel,
        out_shape=(
            jax.ShapeDtypeStruct((slots, W, 2 * W), jnp.bfloat16),
            jax.ShapeDtypeStruct((3, slots), jnp.int32),
            jax.ShapeDtypeStruct(mine.shape, mine.dtype),
        ),
        in_specs=[SMEM] + [pl.BlockSpec(memory_space=pltpu.HBM)] * 4,
        out_specs=(VMEM, VMEM, VMEM),
        scratch_shapes=[
            pltpu.VMEM((slots, W, W), jnp.float32),
            pltpu.VMEM((2, 1, slots), jnp.int32),
            pltpu.SemaphoreType.DMA((slots // GROUP,)),
            pltpu.SemaphoreType.DMA((3,)),
        ],
        compiler_params=pltpu.CompilerParams(vmem_limit_bytes=32 * 1024 * 1024),
        cost_estimate=pl.CostEstimate(flops=4 * slots * W * W, bytes_accessed=8 * slots * W * W, transcendentals=0),
    )(live, *operands)


def ladder_kernel(codes, blocks, halves, result, columns, flat, totals):
    owners, chunk_count = blocks.shape[:2]
    out_tiles = totals.shape[0] - 1
    rows = result.shape[1] // out_tiles
    in_local = blocks.shape[2] // rows
    totals[...] = jnp.zeros_like(totals)

    far = chunk_count // NEAR

    def spread(owner, carry):
        def one_chunk(chunk, inner):
            crossed = (chunk >= far).astype(jnp.int32) ^ (lax.rem(chunk, far) > 0).astype(jnp.int32)
            source = lax.bitwise_xor(owner, crossed)
            for tile in range(in_local):
                flat[tile, pl.ds(chunk * rows, rows), :] = blocks[source, chunk, tile * rows : (tile + 1) * rows, :]
            return inner

        lax.fori_loop(0, chunk_count, one_chunk, 0, unroll=min(chunk_count, 16))
        for tile in range(in_local):
            high, low = split(flat[tile])
            columns[owner * in_local + tile, :, :W] = high
            columns[owner * in_local + tile, :, W:] = low
        return carry

    lax.fori_loop(0, owners, spread, 0, unroll=min(owners, 2))

    def one_group(index, carry):
        first = index * GROUP
        products = []
        for step in range(GROUP):
            both = halves[first + step]
            weights = jnp.concatenate([both, both], axis=0)
            got = jnp.dot(columns[codes[0, first + step]], weights, preferred_element_type=jnp.float32)
            products.append(got[:, :W] + got[:, W:])
        for step in range(GROUP):
            place = codes[1, first + step]
            totals[place] = totals[place] + products[step]
        return carry

    lax.fori_loop(0, (codes[2, 0] + GROUP - 1) // GROUP, one_group, 0)
    def give(chunk, carry):
        for tile in range(out_tiles):
            result[chunk, tile * rows : (tile + 1) * rows, :] = totals[tile, pl.ds(chunk * rows, rows), :]
        return carry

    lax.fori_loop(0, chunk_count, give, 0, unroll=min(chunk_count, 16))


def local_terms(codes, blocks, halves, rows, out_tiles):
    owners, chunk_count, chunk_rows, _ = blocks.shape
    total_rows = chunk_count * rows
    in_local = chunk_rows // rows
    return pl.pallas_call(
        ladder_kernel,
        out_shape=jax.ShapeDtypeStruct((chunk_count, out_tiles * rows, W), jnp.float32),
        in_specs=[SMEM, VMEM, VMEM],
        out_specs=VMEM,
        scratch_shapes=[
            pltpu.VMEM((owners * in_local, total_rows, 2 * W), jnp.bfloat16),
            pltpu.VMEM((in_local, total_rows, W), jnp.float32),
            pltpu.VMEM((out_tiles + 1, total_rows, W), jnp.float32),
        ],
        compiler_params=pltpu.CompilerParams(vmem_limit_bytes=32 * 1024 * 1024),
    )(codes, blocks, halves)


def swap(value, pairs, virts, mask):
    routes = [(a * virts + b, (a ^ mask) * virts + (b ^ 1)) for a in range(pairs) for b in range(virts)]
    return lax.ppermute(value, ("pair", "virt"), routes)


def swap_sum(parts, pairs, virts, masks):
    received = [swap(part, pairs, virts, mask) for part, mask in zip(parts, masks)]
    return sum(received[1:], received[0])


def shards(t2_amplitudes, integral_tiles, out_tiles, in_tiles, tile_counts):
    rows, columns = t2_amplitudes.shape
    local_tiles = columns // W
    slots = integral_tiles.shape[2]
    pairs, virts = lax.axis_size("pair"), lax.axis_size("virt")
    mine = t2_amplitudes.reshape(rows, local_tiles, W).transpose(1, 0, 2).reshape(local_tiles * rows, W)
    halves, codes, own = prepare(
        integral_tiles.reshape(slots, W, W),
        in_tiles.reshape(1, slots),
        out_tiles.reshape(1, slots),
        tile_counts,
        mine,
        local_tiles,
    )
    far_masks, near_masks = range(0, pairs, NEAR), range(NEAR)
    line = jnp.stack([own] + [swap(mine, pairs, virts, mask) for mask in far_masks[1:]])
    gathered = jnp.concatenate([line] + [swap(line, pairs, virts, mask) for mask in near_masks[1:]])
    blocks = lax.all_gather(gathered, "virt", axis=0)
    partial_sums = local_terms(codes, blocks, halves, rows, local_tiles)
    line_sums = swap_sum(partial_sums.reshape((NEAR, pairs // NEAR) + mine.shape), pairs, virts, near_masks)
    summed = swap_sum(line_sums, pairs, virts, far_masks)
    return summed.reshape(local_tiles, rows, W).transpose(1, 0, 2).reshape(rows, columns)


def solution(mesh):
    return jax.shard_map(
        shards,
        mesh=mesh,
        in_specs=(
            P("pair", "virt"),
            P("pair", "virt", None, None, None),
            P("pair", "virt", None),
            P("pair", "virt", None),
            P("pair", "virt"),
        ),
        out_specs=P("pair", "virt"),
        check_vma=False,
    )
```

```python
import jax
import jax.numpy as jnp
from jax import lax
from jax.experimental import pallas as pl
from jax.experimental.pallas import tpu as pltpu
from jax.sharding import PartitionSpec as P

W = 128
GROUP = 8
NEAR = 4
SMEM = pl.BlockSpec(memory_space=pltpu.SMEM)
VMEM = pl.BlockSpec(memory_space=pltpu.VMEM)


def split(value):
    high = value.astype(jnp.bfloat16)
    low = (value - high.astype(jnp.float32)).astype(jnp.bfloat16)
    return high, low


def tile_kernel(out_tiles, live, ins, outs, tiles, mine, halves, codes, own, held, index_rows, arrived, singles):
    singles_of = ((ins, index_rows.at[0]), (outs, index_rows.at[1]), (mine, own))
    others = [pltpu.make_async_copy(here, there, singles.at[at]) for at, (here, there) in enumerate(singles_of)]
    for copy in others:
        copy.start()
    count = live[0, 0]
    groups = (count + GROUP - 1) // GROUP

    def tile_copy(index):
        part = pl.ds(index * GROUP, GROUP)
        return pltpu.make_async_copy(tiles.at[part], held.at[part], arrived.at[index])

    def begin(index, carry):
        tile_copy(index).start()
        return carry

    lax.fori_loop(0, groups, begin, 0)
    for copy in others:
        copy.wait()
    slots = lax.broadcasted_iota(jnp.int32, ins.shape, 1)
    tile_in = index_rows[0]
    owner = lax.bitwise_xor(lax.div(tile_in, out_tiles), lax.axis_index("virt"))
    codes[0:1, :] = owner * out_tiles + lax.rem(tile_in, out_tiles)
    codes[1:2, :] = jnp.where(slots < count, lax.rem(index_rows[1], out_tiles), out_tiles)
    codes[2:3, :] = jnp.full(ins.shape, count, jnp.int32)

    def one_group(index, carry):
        tile_copy(index).wait()
        for step in range(GROUP):
            slot = index * GROUP + step
            high, low = split(held[slot])
            halves[slot, :, :W] = high
            halves[slot, :, W:] = low
        return carry

    lax.fori_loop(0, groups, one_group, 0)


def prepare(tiles, ins, outs, live, mine, out_tiles):
    slots = tiles.shape[0]

    def kernel(*refs):
        tile_kernel(out_tiles, *refs)

    operands = [pltpu.with_memory_space_constraint(value, pltpu.HBM) for value in (ins, outs, tiles, mine)]
    return pl.pallas_call(
        kernel,
        out_shape=(
            jax.ShapeDtypeStruct((slots, W, 2 * W), jnp.bfloat16),
            jax.ShapeDtypeStruct((3, slots), jnp.int32),
            jax.ShapeDtypeStruct(mine.shape, mine.dtype),
        ),
        in_specs=[SMEM] + [pl.BlockSpec(memory_space=pltpu.HBM)] * 4,
        out_specs=(VMEM, VMEM, VMEM),
        scratch_shapes=[
            pltpu.VMEM((slots, W, W), jnp.float32),
            pltpu.VMEM((2, 1, slots), jnp.int32),
            pltpu.SemaphoreType.DMA((slots // GROUP,)),
            pltpu.SemaphoreType.DMA((3,)),
        ],
        compiler_params=pltpu.CompilerParams(vmem_limit_bytes=32 * 1024 * 1024),
        cost_estimate=pl.CostEstimate(flops=4 * slots * W * W, bytes_accessed=8 * slots * W * W, transcendentals=0),
    )(live, *operands)


def ladder_kernel(virts, codes, halves, *refs):
    blocks, (result, columns, flat, totals) = refs[: virts * NEAR], refs[virts * NEAR :]
    far = blocks[0].shape[0]
    chunk_count = NEAR * far
    out_tiles = totals.shape[0] - 1
    rows = result.shape[1] // out_tiles
    in_local = columns.shape[0] // virts
    totals[...] = jnp.zeros_like(totals)

    for owner in range(virts):
        for a in range(NEAR):
            for b in range(far):
                source = blocks[(owner ^ int((a > 0) != (b > 0))) * NEAR + a]
                place = pl.ds((a * far + b) * rows, rows)
                for tile in range(in_local):
                    flat[tile, place, :] = source[b, tile * rows : (tile + 1) * rows, :]
        for tile in range(in_local):
            high, low = split(flat[tile])
            columns[owner * in_local + tile, :, :W] = high
            columns[owner * in_local + tile, :, W:] = low

    def one_group(index, carry):
        first = index * GROUP
        products = []
        for step in range(GROUP):
            both = halves[first + step]
            weights = jnp.concatenate([both, both], axis=0)
            got = jnp.dot(columns[codes[0, first + step]], weights, preferred_element_type=jnp.float32)
            products.append(got[:, :W] + got[:, W:])
        for step in range(GROUP):
            place = codes[1, first + step]
            totals[place] = totals[place] + products[step]
        return carry

    lax.fori_loop(0, (codes[2, 0] + GROUP - 1) // GROUP, one_group, 0)
    me = lax.axis_index("pair")

    def give(chunk, carry):
        device = lax.bitwise_xor(me, lax.rem(chunk, far) * NEAR + chunk // far)
        for tile in range(out_tiles):
            result[device, tile * rows : (tile + 1) * rows, :] = totals[tile, pl.ds(chunk * rows, rows), :]
        return carry

    lax.fori_loop(0, chunk_count, give, 0, unroll=min(chunk_count, 16))


def local_terms(codes, blocks, halves, rows, out_tiles):
    far, chunk_rows, _ = blocks[0].shape
    virts = len(blocks) // NEAR
    total_rows = NEAR * far * rows
    in_local = chunk_rows // rows

    def kernel(*refs):
        ladder_kernel(virts, *refs)

    return pl.pallas_call(
        kernel,
        out_shape=jax.ShapeDtypeStruct((NEAR * far, out_tiles * rows, W), jnp.float32),
        in_specs=[SMEM, VMEM] + [VMEM] * len(blocks),
        out_specs=VMEM,
        scratch_shapes=[
            pltpu.VMEM((virts * in_local, total_rows, 2 * W), jnp.bfloat16),
            pltpu.VMEM((in_local, total_rows, W), jnp.float32),
            pltpu.VMEM((out_tiles + 1, total_rows, W), jnp.float32),
        ],
        compiler_params=pltpu.CompilerParams(vmem_limit_bytes=32 * 1024 * 1024),
    )(codes, halves, *blocks)


def swap(value, pairs, virts, mask, virt_mask):
    routes = [(a * virts + b, (a ^ mask) * virts + (b ^ virt_mask)) for a in range(pairs) for b in range(virts)]
    return lax.ppermute(value, ("pair", "virt"), routes)


def shards(t2_amplitudes, integral_tiles, out_tiles, in_tiles, tile_counts):
    rows, columns = t2_amplitudes.shape
    local_tiles = columns // W
    slots = integral_tiles.shape[2]
    pairs, virts = lax.axis_size("pair"), lax.axis_size("virt")
    mine = t2_amplitudes.reshape(rows, local_tiles, W).transpose(1, 0, 2).reshape(local_tiles * rows, W)
    halves, codes, own = prepare(
        integral_tiles.reshape(slots, W, W),
        in_tiles.reshape(1, slots),
        out_tiles.reshape(1, slots),
        tile_counts,
        mine,
        local_tiles,
    )
    line = jnp.stack([own] + [swap(mine, pairs, virts, mask, 1) for mask in range(NEAR, pairs, NEAR)])
    pieces = [line] + [swap(line, pairs, virts, mask, 1) for mask in range(1, NEAR)]
    blocks = pieces + [swap(piece, pairs, virts, 0, mask) for mask in range(1, virts) for piece in pieces]
    partial_sums = local_terms(codes, blocks, halves, rows, local_tiles)
    received = lax.all_to_all(partial_sums, "pair", 0, 0)
    summed = jnp.sum(received, axis=0)
    return summed.reshape(local_tiles, rows, W).transpose(1, 0, 2).reshape(rows, columns)


def solution(mesh):
    return jax.shard_map(
        shards,
        mesh=mesh,
        in_specs=(
            P("pair", "virt"),
            P("pair", "virt", None, None, None),
            P("pair", "virt", None),
            P("pair", "virt", None),
            P("pair", "virt"),
        ),
        out_specs=P("pair", "virt"),
        check_vma=False,
    )
```

```python
import jax
import jax.numpy as jnp
from jax import lax
from jax.experimental import pallas as pl
from jax.experimental.pallas import tpu as pltpu
from jax.sharding import PartitionSpec as P

W = 128
GROUP = 8
NEAR = 4
SMEM = pl.BlockSpec(memory_space=pltpu.SMEM)
VMEM = pl.BlockSpec(memory_space=pltpu.VMEM)


def split(value):
    high = value.astype(jnp.bfloat16)
    low = (value - high.astype(jnp.float32)).astype(jnp.bfloat16)
    return high, low


def tile_kernel(out_tiles, live, ins, outs, tiles, mine, halves, codes, own, held, index_rows, arrived, singles):
    singles_of = ((ins, index_rows.at[0]), (outs, index_rows.at[1]), (mine, own))
    others = [pltpu.make_async_copy(here, there, singles.at[at]) for at, (here, there) in enumerate(singles_of)]
    for copy in others:
        copy.start()
    count = live[0, 0]
    groups = (count + GROUP - 1) // GROUP

    def tile_copy(index):
        part = pl.ds(index * GROUP, GROUP)
        return pltpu.make_async_copy(tiles.at[part], held.at[part], arrived.at[index])

    def begin(index, carry):
        tile_copy(index).start()
        return carry

    lax.fori_loop(0, groups, begin, 0)
    for copy in others:
        copy.wait()
    slots = lax.broadcasted_iota(jnp.int32, ins.shape, 1)
    tile_in = index_rows[0]
    owner = lax.bitwise_xor(lax.div(tile_in, out_tiles), lax.axis_index("virt"))
    codes[0:1, :] = owner * out_tiles + lax.rem(tile_in, out_tiles)
    codes[1:2, :] = jnp.where(slots < count, lax.rem(index_rows[1], out_tiles), out_tiles)
    codes[2:3, :] = jnp.full(ins.shape, count, jnp.int32)

    def one_group(index, carry):
        tile_copy(index).wait()
        for step in range(GROUP):
            slot = index * GROUP + step
            high, low = split(held[slot])
            halves[slot, :, :W] = high
            halves[slot, :, W:] = low
        return carry

    lax.fori_loop(0, groups, one_group, 0)


def prepare(tiles, ins, outs, live, mine, out_tiles):
    slots = tiles.shape[0]

    def kernel(*refs):
        tile_kernel(out_tiles, *refs)

    operands = [pltpu.with_memory_space_constraint(value, pltpu.HBM) for value in (ins, outs, tiles, mine)]
    return pl.pallas_call(
        kernel,
        out_shape=(
            jax.ShapeDtypeStruct((slots, W, 2 * W), jnp.bfloat16),
            jax.ShapeDtypeStruct((3, slots), jnp.int32),
            jax.ShapeDtypeStruct(mine.shape, mine.dtype),
        ),
        in_specs=[SMEM] + [pl.BlockSpec(memory_space=pltpu.HBM)] * 4,
        out_specs=(VMEM, VMEM, VMEM),
        scratch_shapes=[
            pltpu.VMEM((slots, W, W), jnp.float32),
            pltpu.VMEM((2, 1, slots), jnp.int32),
            pltpu.SemaphoreType.DMA((slots // GROUP,)),
            pltpu.SemaphoreType.DMA((3,)),
        ],
        compiler_params=pltpu.CompilerParams(vmem_limit_bytes=32 * 1024 * 1024),
        cost_estimate=pl.CostEstimate(flops=4 * slots * W * W, bytes_accessed=8 * slots * W * W, transcendentals=0),
    )(live, *operands)


def ladder_kernel(virts, codes_here, halves, *refs):
    blocks, (result, columns, flat, totals, codes, copied) = refs[: virts * NEAR], refs[virts * NEAR :]
    fetch = pltpu.make_async_copy(codes_here, codes, copied)
    fetch.start()
    far = blocks[0].shape[0]
    chunk_count = NEAR * far
    out_tiles = totals.shape[0] - 1
    rows = result.shape[1] // out_tiles
    total_rows = chunk_count * rows
    in_local = columns.shape[0] // virts
    totals[...] = jnp.zeros_like(totals)

    for owner in range(virts):
        for a in range(NEAR):
            for b in range(far):
                source = blocks[(owner ^ int((a > 0) != (b > 0))) * NEAR + a]
                place = pl.ds((a * far + b) * rows, rows)
                for tile in range(in_local):
                    flat[tile, place, :] = source[b, tile * rows : (tile + 1) * rows, :]
        for tile in range(in_local):
            high, low = split(flat[tile])
            columns[owner * in_local + tile, :total_rows, :] = high
            columns[owner * in_local + tile, total_rows:, :] = low

    fetch.wait()

    def one_group(index, carry):
        first = index * GROUP
        products = []
        for step in range(GROUP):
            both = columns[codes[0, first + step]]
            upper = jnp.dot(both, halves[first + step, :, :W], preferred_element_type=jnp.float32)
            lower = jnp.dot(both[:total_rows], halves[first + step, :, W:], preferred_element_type=jnp.float32)
            products.append(upper[:total_rows] + (upper[total_rows:] + lower))
        for step in range(GROUP):
            place = codes[1, first + step]
            totals[place] = totals[place] + products[step]
        return carry

    lax.fori_loop(0, (codes[2, 0] + GROUP - 1) // GROUP, one_group, 0)
    me = lax.axis_index("pair")

    def give(chunk, carry):
        device = lax.bitwise_xor(me, lax.rem(chunk, far) * NEAR + chunk // far)
        for tile in range(out_tiles):
            result[device, tile * rows : (tile + 1) * rows, :] = totals[tile, pl.ds(chunk * rows, rows), :]
        return carry

    lax.fori_loop(0, chunk_count, give, 0, unroll=min(chunk_count, 16))


def local_terms(codes, blocks, halves, rows, out_tiles):
    far, chunk_rows, _ = blocks[0].shape
    virts = len(blocks) // NEAR
    total_rows = NEAR * far * rows
    in_local = chunk_rows // rows

    def kernel(*refs):
        ladder_kernel(virts, *refs)

    return pl.pallas_call(
        kernel,
        out_shape=jax.ShapeDtypeStruct((NEAR * far, out_tiles * rows, W), jnp.float32),
        in_specs=[VMEM, VMEM] + [VMEM] * len(blocks),
        out_specs=VMEM,
        scratch_shapes=[
            pltpu.VMEM((virts * in_local, 2 * total_rows, W), jnp.bfloat16),
            pltpu.VMEM((in_local, total_rows, W), jnp.float32),
            pltpu.VMEM((out_tiles + 1, total_rows, W), jnp.float32),
            pltpu.SMEM(codes.shape, jnp.int32),
            pltpu.SemaphoreType.DMA,
        ],
        compiler_params=pltpu.CompilerParams(vmem_limit_bytes=32 * 1024 * 1024),
    )(codes, halves, *blocks)


def swap(value, pairs, virts, mask, virt_mask):
    routes = [(a * virts + b, (a ^ mask) * virts + (b ^ virt_mask)) for a in range(pairs) for b in range(virts)]
    return lax.ppermute(value, ("pair", "virt"), routes)


def shards(t2_amplitudes, integral_tiles, out_tiles, in_tiles, tile_counts):
    rows, columns = t2_amplitudes.shape
    local_tiles = columns // W
    slots = integral_tiles.shape[2]
    pairs, virts = lax.axis_size("pair"), lax.axis_size("virt")
    mine = t2_amplitudes.reshape(rows, local_tiles, W).transpose(1, 0, 2).reshape(local_tiles * rows, W)
    halves, codes, own = prepare(
        integral_tiles.reshape(slots, W, W),
        in_tiles.reshape(1, slots),
        out_tiles.reshape(1, slots),
        tile_counts,
        mine,
        local_tiles,
    )
    line = jnp.stack([own] + [swap(mine, pairs, virts, mask, 1) for mask in range(NEAR, pairs, NEAR)])
    pieces = [line] + [swap(line, pairs, virts, mask, 1) for mask in range(1, NEAR)]
    blocks = pieces + [swap(piece, pairs, virts, 0, mask) for mask in range(1, virts) for piece in pieces]
    partial_sums = local_terms(codes, blocks, halves, rows, local_tiles)
    received = lax.all_to_all(partial_sums, "pair", 0, 0)
    summed = jnp.sum(received, axis=0)
    return summed.reshape(local_tiles, rows, W).transpose(1, 0, 2).reshape(rows, columns)


def solution(mesh):
    return jax.shard_map(
        shards,
        mesh=mesh,
        in_specs=(
            P("pair", "virt"),
            P("pair", "virt", None, None, None),
            P("pair", "virt", None),
            P("pair", "virt", None),
            P("pair", "virt"),
        ),
        out_specs=P("pair", "virt"),
        check_vma=False,
    )
```

```python
import jax
import jax.numpy as jnp
from jax import lax
from jax.experimental import pallas as pl
from jax.experimental.pallas import tpu as pltpu
from jax.sharding import PartitionSpec as P

W = 128
GROUP = 8
NEAR = 4
SMEM = pl.BlockSpec(memory_space=pltpu.SMEM)
VMEM = pl.BlockSpec(memory_space=pltpu.VMEM)


def split(value):
    high = value.astype(jnp.bfloat16)
    low = (value - high.astype(jnp.float32)).astype(jnp.bfloat16)
    return high, low


def tile_kernel(out_tiles, live, ins, outs, tiles, mine, halves, codes, own, held, index_rows, arrived, singles):
    singles_of = ((ins, index_rows.at[0]), (outs, index_rows.at[1]), (mine, own))
    others = [pltpu.make_async_copy(here, there, singles.at[at]) for at, (here, there) in enumerate(singles_of)]
    for copy in others:
        copy.start()
    count = live[0, 0]
    groups = (count + GROUP - 1) // GROUP

    def tile_copy(index):
        part = pl.ds(index * GROUP, GROUP)
        return pltpu.make_async_copy(tiles.at[part], held.at[part], arrived.at[index])

    def begin(index, carry):
        tile_copy(index).start()
        return carry

    lax.fori_loop(0, groups, begin, 0)
    for copy in others:
        copy.wait()
    slots = lax.broadcasted_iota(jnp.int32, ins.shape, 1)
    tile_in = index_rows[0]
    owner = lax.bitwise_xor(lax.div(tile_in, out_tiles), lax.axis_index("virt"))
    codes[0:1, :] = owner * out_tiles + lax.rem(tile_in, out_tiles)
    codes[1:2, :] = jnp.where(slots < count, lax.rem(index_rows[1], out_tiles), out_tiles)
    codes[2:3, :] = jnp.full(ins.shape, count, jnp.int32)

    def one_group(index, carry):
        tile_copy(index).wait()
        for step in range(GROUP):
            slot = index * GROUP + step
            high, low = split(held[slot])
            halves[slot, :, :W] = high
            halves[slot, :, W:] = low
        return carry

    lax.fori_loop(0, groups, one_group, 0)


def prepare(tiles, ins, outs, live, mine, out_tiles):
    slots = tiles.shape[0]

    def kernel(*refs):
        tile_kernel(out_tiles, *refs)

    operands = [pltpu.with_memory_space_constraint(value, pltpu.HBM) for value in (ins, outs, tiles, mine)]
    return pl.pallas_call(
        kernel,
        out_shape=(
            jax.ShapeDtypeStruct((slots, W, 2 * W), jnp.bfloat16),
            jax.ShapeDtypeStruct((3, slots), jnp.int32),
            jax.ShapeDtypeStruct(mine.shape, mine.dtype),
        ),
        in_specs=[SMEM] + [pl.BlockSpec(memory_space=pltpu.HBM)] * 4,
        out_specs=(VMEM, VMEM, VMEM),
        scratch_shapes=[
            pltpu.VMEM((slots, W, W), jnp.float32),
            pltpu.VMEM((2, 1, slots), jnp.int32),
            pltpu.SemaphoreType.DMA((slots // GROUP,)),
            pltpu.SemaphoreType.DMA((3,)),
        ],
        compiler_params=pltpu.CompilerParams(vmem_limit_bytes=32 * 1024 * 1024),
        cost_estimate=pl.CostEstimate(flops=4 * slots * W * W, bytes_accessed=8 * slots * W * W, transcendentals=0),
    )(live, *operands)


def ladder_kernel(virts, codes_here, halves, *refs):
    blocks, (result, columns, flat, totals, codes, copied) = refs[: virts * NEAR], refs[virts * NEAR :]
    fetch = pltpu.make_async_copy(codes_here, codes, copied)
    fetch.start()
    far = blocks[0].shape[0]
    chunk_count = NEAR * far
    out_tiles = totals.shape[0] - 1
    rows = result.shape[1] // out_tiles
    total_rows = chunk_count * rows
    in_local = columns.shape[0] // virts
    totals[...] = jnp.zeros_like(totals)

    for owner in range(virts):
        for a in range(NEAR):
            for b in range(far):
                source = blocks[(owner ^ int((a > 0) != (b > 0))) * NEAR + a]
                place = pl.ds((a * far + b) * rows, rows)
                for tile in range(in_local):
                    flat[tile, place, :] = source[b, tile * rows : (tile + 1) * rows, :]
        for tile in range(in_local):
            high, low = split(flat[tile])
            columns[owner * in_local + tile, :, :W] = high
            columns[owner * in_local + tile, :, W:] = low

    fetch.wait()

    def add(first, is_live, products):
        for step, product in enumerate(products):
            place = jnp.where(is_live, codes[1, first + step], out_tiles)
            totals[place] = totals[place] + product

    def one_group(index, earlier):
        first = index * GROUP
        products = []
        for step in range(GROUP):
            both = halves[first + step]
            weights = jnp.concatenate([both, both], axis=0)
            got = jnp.dot(columns[codes[0, first + step]], weights, preferred_element_type=jnp.float32)
            products.append(got[:, :W] + got[:, W:])
        add(jnp.maximum(first - GROUP, 0), index > 0, earlier)
        return tuple(products)

    groups = (codes[2, 0] + GROUP - 1) // GROUP
    nothing = (jnp.zeros((total_rows, W), jnp.float32),) * GROUP
    last = lax.fori_loop(0, groups, one_group, nothing)
    add((groups - 1) * GROUP, groups > 0, last)
    me = lax.axis_index("pair")

    def give(chunk, carry):
        device = lax.bitwise_xor(me, lax.rem(chunk, far) * NEAR + chunk // far)
        for tile in range(out_tiles):
            result[device, tile * rows : (tile + 1) * rows, :] = totals[tile, pl.ds(chunk * rows, rows), :]
        return carry

    lax.fori_loop(0, chunk_count, give, 0, unroll=min(chunk_count, 16))


def local_terms(codes, blocks, halves, rows, out_tiles):
    far, chunk_rows, _ = blocks[0].shape
    virts = len(blocks) // NEAR
    total_rows = NEAR * far * rows
    in_local = chunk_rows // rows

    def kernel(*refs):
        ladder_kernel(virts, *refs)

    return pl.pallas_call(
        kernel,
        out_shape=jax.ShapeDtypeStruct((NEAR * far, out_tiles * rows, W), jnp.float32),
        in_specs=[VMEM, VMEM] + [VMEM] * len(blocks),
        out_specs=VMEM,
        scratch_shapes=[
            pltpu.VMEM((virts * in_local, total_rows, 2 * W), jnp.bfloat16),
            pltpu.VMEM((in_local, total_rows, W), jnp.float32),
            pltpu.VMEM((out_tiles + 1, total_rows, W), jnp.float32),
            pltpu.SMEM(codes.shape, jnp.int32),
            pltpu.SemaphoreType.DMA,
        ],
        compiler_params=pltpu.CompilerParams(vmem_limit_bytes=32 * 1024 * 1024),
    )(codes, halves, *blocks)


def swap(value, pairs, virts, mask, virt_mask):
    routes = [(a * virts + b, (a ^ mask) * virts + (b ^ virt_mask)) for a in range(pairs) for b in range(virts)]
    return lax.ppermute(value, ("pair", "virt"), routes)


def shards(t2_amplitudes, integral_tiles, out_tiles, in_tiles, tile_counts):
    rows, columns = t2_amplitudes.shape
    local_tiles = columns // W
    slots = integral_tiles.shape[2]
    pairs, virts = lax.axis_size("pair"), lax.axis_size("virt")
    mine = t2_amplitudes.reshape(rows, local_tiles, W).transpose(1, 0, 2).reshape(local_tiles * rows, W)
    halves, codes, own = prepare(
        integral_tiles.reshape(slots, W, W),
        in_tiles.reshape(1, slots),
        out_tiles.reshape(1, slots),
        tile_counts,
        mine,
        local_tiles,
    )
    line = jnp.stack([own] + [swap(mine, pairs, virts, mask, 1) for mask in range(NEAR, pairs, NEAR)])
    pieces = [line] + [swap(line, pairs, virts, mask, 1) for mask in range(1, NEAR)]
    blocks = pieces + [swap(piece, pairs, virts, 0, mask) for mask in range(1, virts) for piece in pieces]
    partial_sums = local_terms(codes, blocks, halves, rows, local_tiles)
    received = lax.all_to_all(partial_sums, "pair", 0, 0)
    summed = jnp.sum(received, axis=0)
    return summed.reshape(local_tiles, rows, W).transpose(1, 0, 2).reshape(rows, columns)


def solution(mesh):
    return jax.shard_map(
        shards,
        mesh=mesh,
        in_specs=(
            P("pair", "virt"),
            P("pair", "virt", None, None, None),
            P("pair", "virt", None),
            P("pair", "virt", None),
            P("pair", "virt"),
        ),
        out_specs=P("pair", "virt"),
        check_vma=False,
    )
```

```python
import jax
import jax.numpy as jnp
from jax import lax
from jax.experimental import pallas as pl
from jax.experimental.pallas import tpu as pltpu
from jax.sharding import PartitionSpec as P

W = 128
GROUP = 8
NEAR = 4
SMEM = pl.BlockSpec(memory_space=pltpu.SMEM)
VMEM = pl.BlockSpec(memory_space=pltpu.VMEM)


def split(value):
    high = value.astype(jnp.bfloat16)
    low = (value - high.astype(jnp.float32)).astype(jnp.bfloat16)
    return high, low


def tile_kernel(out_tiles, live, ins, outs, tiles, mine, halves, codes, own, held, index_rows, arrived, singles):
    singles_of = ((ins, index_rows.at[0]), (outs, index_rows.at[1]), (mine, own))
    others = [pltpu.make_async_copy(here, there, singles.at[at]) for at, (here, there) in enumerate(singles_of)]
    for copy in others:
        copy.start()
    count = live[0, 0]
    groups = (count + GROUP - 1) // GROUP

    def tile_copy(index):
        part = pl.ds(index * GROUP, GROUP)
        return pltpu.make_async_copy(tiles.at[part], held.at[part], arrived.at[index])

    def begin(index, carry):
        tile_copy(index).start()
        return carry

    lax.fori_loop(0, groups, begin, 0)
    for copy in others:
        copy.wait()
    slots = lax.broadcasted_iota(jnp.int32, ins.shape, 1)
    tile_in = index_rows[0]
    owner = lax.bitwise_xor(lax.div(tile_in, out_tiles), lax.axis_index("virt"))
    codes[0:1, :] = owner * out_tiles + lax.rem(tile_in, out_tiles)
    codes[1:2, :] = jnp.where(slots < count, lax.rem(index_rows[1], out_tiles), out_tiles)
    codes[2:3, :] = jnp.full(ins.shape, count, jnp.int32)

    def one_group(index, carry):
        tile_copy(index).wait()
        for step in range(GROUP):
            slot = index * GROUP + step
            high, low = split(held[slot])
            halves[slot, :, :W] = high
            halves[slot, :, W:] = low
        return carry

    lax.fori_loop(0, groups, one_group, 0)


def prepare(tiles, ins, outs, live, mine, out_tiles):
    slots = tiles.shape[0]

    def kernel(*refs):
        tile_kernel(out_tiles, *refs)

    operands = [pltpu.with_memory_space_constraint(value, pltpu.HBM) for value in (ins, outs, tiles, mine)]
    return pl.pallas_call(
        kernel,
        out_shape=(
            jax.ShapeDtypeStruct((slots, W, 2 * W), jnp.bfloat16),
            jax.ShapeDtypeStruct((3, slots), jnp.int32),
            jax.ShapeDtypeStruct(mine.shape, mine.dtype),
        ),
        in_specs=[SMEM] + [pl.BlockSpec(memory_space=pltpu.HBM)] * 4,
        out_specs=(VMEM, VMEM, VMEM),
        scratch_shapes=[
            pltpu.VMEM((slots, W, W), jnp.float32),
            pltpu.VMEM((2, 1, slots), jnp.int32),
            pltpu.SemaphoreType.DMA((slots // GROUP,)),
            pltpu.SemaphoreType.DMA((3,)),
        ],
        compiler_params=pltpu.CompilerParams(vmem_limit_bytes=32 * 1024 * 1024),
        cost_estimate=pl.CostEstimate(flops=4 * slots * W * W, bytes_accessed=8 * slots * W * W, transcendentals=0),
    )(live, *operands)


def ladder_kernel(virts, codes_here, halves, *refs):
    blocks, (result, columns, flat, totals, codes, copied) = refs[: virts * NEAR], refs[virts * NEAR :]
    fetch = pltpu.make_async_copy(codes_here, codes, copied)
    fetch.start()
    far = blocks[0].shape[0]
    chunk_count = NEAR * far
    out_tiles = totals.shape[0] - 1
    rows = result.shape[1] // out_tiles
    total_rows = chunk_count * rows
    in_local = columns.shape[0] // virts
    totals[...] = jnp.zeros_like(totals)

    for owner in range(virts):
        for a in range(NEAR):
            for b in range(far):
                source = blocks[(owner ^ int((a > 0) != (b > 0))) * NEAR + a]
                place = pl.ds((a * far + b) * rows, rows)
                for tile in range(in_local):
                    flat[tile, place, :] = source[b, tile * rows : (tile + 1) * rows, :]
        for tile in range(in_local):
            high, low = split(flat[tile])
            columns[owner * in_local + tile, :total_rows, :] = high
            columns[owner * in_local + tile, total_rows:, :] = low

    fetch.wait()

    def one_group(index, carry):
        first = index * GROUP
        products = []
        for step in range(GROUP):
            got = jnp.dot(columns[codes[0, first + step]], halves[first + step], preferred_element_type=jnp.float32)
            upper, lower = got[:total_rows], got[total_rows:]
            products.append((upper[:, :W] + lower[:, :W]) + (upper[:, W:] + lower[:, W:]))
        for step in range(GROUP):
            place = codes[1, first + step]
            totals[place] = totals[place] + products[step]
        return carry

    lax.fori_loop(0, (codes[2, 0] + GROUP - 1) // GROUP, one_group, 0)
    def give(chunk, carry):
        for tile in range(out_tiles):
            result[chunk, tile * rows : (tile + 1) * rows, :] = totals[tile, pl.ds(chunk * rows, rows), :]
        return carry

    lax.fori_loop(0, chunk_count, give, 0, unroll=min(chunk_count, 16))


def local_terms(codes, blocks, halves, rows, out_tiles):
    far, chunk_rows, _ = blocks[0].shape
    virts = len(blocks) // NEAR
    total_rows = NEAR * far * rows
    in_local = chunk_rows // rows

    def kernel(*refs):
        ladder_kernel(virts, *refs)

    return pl.pallas_call(
        kernel,
        out_shape=jax.ShapeDtypeStruct((NEAR * far, out_tiles * rows, W), jnp.float32),
        in_specs=[VMEM, VMEM] + [VMEM] * len(blocks),
        out_specs=VMEM,
        scratch_shapes=[
            pltpu.VMEM((virts * in_local, 2 * total_rows, W), jnp.bfloat16),
            pltpu.VMEM((in_local, total_rows, W), jnp.float32),
            pltpu.VMEM((out_tiles + 1, total_rows, W), jnp.float32),
            pltpu.SMEM(codes.shape, jnp.int32),
            pltpu.SemaphoreType.DMA,
        ],
        compiler_params=pltpu.CompilerParams(vmem_limit_bytes=32 * 1024 * 1024),
    )(codes, halves, *blocks)


def swap(value, pairs, virts, mask, virt_mask):
    routes = [(a * virts + b, (a ^ mask) * virts + (b ^ virt_mask)) for a in range(pairs) for b in range(virts)]
    return lax.ppermute(value, ("pair", "virt"), routes)


def swap_sum(parts, pairs, virts, unit):
    order = [0, *range(len(parts) - 1, 0, -1)]
    received = [swap(parts[i], pairs, virts, i * unit, 1) for i in order]
    return sum(received[1:], received[0])


def shards(t2_amplitudes, integral_tiles, out_tiles, in_tiles, tile_counts):
    rows, columns = t2_amplitudes.shape
    local_tiles = columns // W
    slots = integral_tiles.shape[2]
    pairs, virts = lax.axis_size("pair"), lax.axis_size("virt")
    mine = t2_amplitudes.reshape(rows, local_tiles, W).transpose(1, 0, 2).reshape(local_tiles * rows, W)
    halves, codes, own = prepare(
        integral_tiles.reshape(slots, W, W),
        in_tiles.reshape(1, slots),
        out_tiles.reshape(1, slots),
        tile_counts,
        mine,
        local_tiles,
    )
    line = jnp.stack([own] + [swap(mine, pairs, virts, mask, 1) for mask in range(NEAR, pairs, NEAR)])
    pieces = [line] + [swap(line, pairs, virts, mask, 1) for mask in range(1, NEAR)]
    blocks = pieces + [swap(piece, pairs, virts, 0, mask) for mask in range(1, virts) for piece in pieces]
    partial_sums = local_terms(codes, blocks, halves, rows, local_tiles)
    line_sums = swap_sum(partial_sums.reshape((NEAR, pairs // NEAR) + mine.shape), pairs, virts, 1)
    summed = swap_sum(line_sums, pairs, virts, NEAR)
    return summed.reshape(local_tiles, rows, W).transpose(1, 0, 2).reshape(rows, columns)


def solution(mesh):
    return jax.shard_map(
        shards,
        mesh=mesh,
        in_specs=(
            P("pair", "virt"),
            P("pair", "virt", None, None, None),
            P("pair", "virt", None),
            P("pair", "virt", None),
            P("pair", "virt"),
        ),
        out_specs=P("pair", "virt"),
        check_vma=False,
    )
```

```python
import jax
import jax.numpy as jnp
from jax import lax
from jax.experimental import pallas as pl
from jax.experimental.pallas import tpu as pltpu
from jax.sharding import PartitionSpec as P

W = 128
COPY_GROUP = 8
GROUP = 16
NEAR = 4
SMEM = pl.BlockSpec(memory_space=pltpu.SMEM)
VMEM = pl.BlockSpec(memory_space=pltpu.VMEM)


def split(value):
    high = value.astype(jnp.bfloat16)
    low = (value - high.astype(jnp.float32)).astype(jnp.bfloat16)
    return high, low


def tile_kernel(out_tiles, live, ins, outs, tiles, mine, halves, codes, own, held, index_rows, arrived, singles):
    singles_of = ((ins, index_rows.at[0]), (outs, index_rows.at[1]), (mine, own))
    others = [pltpu.make_async_copy(here, there, singles.at[at]) for at, (here, there) in enumerate(singles_of)]
    for copy in others:
        copy.start()
    count = live[0, 0]
    groups = (count + COPY_GROUP - 1) // COPY_GROUP

    def tile_copy(index):
        part = pl.ds(index * COPY_GROUP, COPY_GROUP)
        return pltpu.make_async_copy(tiles.at[part], held.at[part], arrived.at[index])

    def begin(index, carry):
        tile_copy(index).start()
        return carry

    lax.fori_loop(0, groups, begin, 0)
    for copy in others:
        copy.wait()
    slots = lax.broadcasted_iota(jnp.int32, ins.shape, 1)
    tile_in = index_rows[0]
    owner = lax.bitwise_xor(lax.div(tile_in, out_tiles), lax.axis_index("virt"))
    codes[0:1, :] = owner * out_tiles + lax.rem(tile_in, out_tiles)
    codes[1:2, :] = jnp.where(slots < count, lax.rem(index_rows[1], out_tiles), out_tiles)
    codes[2:3, :] = jnp.full(ins.shape, count, jnp.int32)

    def one_group(index, carry):
        tile_copy(index).wait()
        for step in range(COPY_GROUP):
            slot = index * COPY_GROUP + step
            high, low = split(held[slot])
            halves[slot, :, :W] = high
            halves[slot, :, W:] = low
        return carry

    lax.fori_loop(0, groups, one_group, 0)


def prepare(tiles, ins, outs, live, mine, out_tiles):
    slots = tiles.shape[0]

    def kernel(*refs):
        tile_kernel(out_tiles, *refs)

    operands = [pltpu.with_memory_space_constraint(value, pltpu.HBM) for value in (ins, outs, tiles, mine)]
    return pl.pallas_call(
        kernel,
        out_shape=(
            jax.ShapeDtypeStruct((slots, W, 2 * W), jnp.bfloat16),
            jax.ShapeDtypeStruct((3, slots), jnp.int32),
            jax.ShapeDtypeStruct(mine.shape, mine.dtype),
        ),
        in_specs=[SMEM] + [pl.BlockSpec(memory_space=pltpu.HBM)] * 4,
        out_specs=(VMEM, VMEM, VMEM),
        scratch_shapes=[
            pltpu.VMEM((slots, W, W), jnp.float32),
            pltpu.VMEM((2, 1, slots), jnp.int32),
            pltpu.SemaphoreType.DMA((slots // COPY_GROUP,)),
            pltpu.SemaphoreType.DMA((3,)),
        ],
        compiler_params=pltpu.CompilerParams(vmem_limit_bytes=32 * 1024 * 1024),
        cost_estimate=pl.CostEstimate(flops=4 * slots * W * W, bytes_accessed=8 * slots * W * W, transcendentals=0),
    )(live, *operands)


def ladder_kernel(virts, codes_here, halves, *refs):
    blocks, (result, columns, flat, totals, codes, copied) = refs[: virts * NEAR], refs[virts * NEAR :]
    fetch = pltpu.make_async_copy(codes_here, codes, copied)
    fetch.start()
    far = blocks[0].shape[0]
    chunk_count = NEAR * far
    out_tiles = totals.shape[0] - 1
    rows = result.shape[1] // out_tiles
    total_rows = chunk_count * rows
    in_local = columns.shape[0] // virts
    totals[...] = jnp.zeros_like(totals)

    for owner in range(virts):
        for a in range(NEAR):
            for b in range(far):
                source = blocks[(owner ^ int((a > 0) != (b > 0))) * NEAR + a]
                place = pl.ds((a * far + b) * rows, rows)
                for tile in range(in_local):
                    flat[tile, place, :] = source[b, tile * rows : (tile + 1) * rows, :]
        for tile in range(in_local):
            high, low = split(flat[tile])
            columns[owner * in_local + tile, :total_rows, :] = high
            columns[owner * in_local + tile, total_rows:, :] = low

    fetch.wait()

    def one_group(index, carry):
        first = index * GROUP
        products = []
        for step in range(GROUP):
            got = jnp.dot(columns[codes[0, first + step]], halves[first + step], preferred_element_type=jnp.float32)
            upper, lower = got[:total_rows], got[total_rows:]
            products.append((upper[:, :W] + lower[:, :W]) + (upper[:, W:] + lower[:, W:]))
        for step in range(GROUP):
            place = codes[1, first + step]
            totals[place] = totals[place] + products[step]
        return carry

    lax.fori_loop(0, (codes[2, 0] + GROUP - 1) // GROUP, one_group, 0)
    def give(chunk, carry):
        for tile in range(out_tiles):
            result[chunk, tile * rows : (tile + 1) * rows, :] = totals[tile, pl.ds(chunk * rows, rows), :]
        return carry

    lax.fori_loop(0, chunk_count, give, 0, unroll=min(chunk_count, 16))


def local_terms(codes, blocks, halves, rows, out_tiles):
    far, chunk_rows, _ = blocks[0].shape
    virts = len(blocks) // NEAR
    total_rows = NEAR * far * rows
    in_local = chunk_rows // rows

    def kernel(*refs):
        ladder_kernel(virts, *refs)

    return pl.pallas_call(
        kernel,
        out_shape=jax.ShapeDtypeStruct((NEAR * far, out_tiles * rows, W), jnp.float32),
        in_specs=[VMEM, VMEM] + [VMEM] * len(blocks),
        out_specs=VMEM,
        scratch_shapes=[
            pltpu.VMEM((virts * in_local, 2 * total_rows, W), jnp.bfloat16),
            pltpu.VMEM((in_local, total_rows, W), jnp.float32),
            pltpu.VMEM((out_tiles + 1, total_rows, W), jnp.float32),
            pltpu.SMEM(codes.shape, jnp.int32),
            pltpu.SemaphoreType.DMA,
        ],
        compiler_params=pltpu.CompilerParams(vmem_limit_bytes=32 * 1024 * 1024),
    )(codes, halves, *blocks)


def swap(value, pairs, virts, mask, virt_mask):
    routes = [(a * virts + b, (a ^ mask) * virts + (b ^ virt_mask)) for a in range(pairs) for b in range(virts)]
    return lax.ppermute(value, ("pair", "virt"), routes)


def swap_sum(parts, pairs, virts, unit):
    last = len(parts) - 1
    received = [swap(parts[i], pairs, virts, i * unit, 1) for i in (0, last, *range(1, last))]
    return sum(received[1:], received[0])


def shards(t2_amplitudes, integral_tiles, out_tiles, in_tiles, tile_counts):
    rows, columns = t2_amplitudes.shape
    local_tiles = columns // W
    slots = integral_tiles.shape[2]
    pairs, virts = lax.axis_size("pair"), lax.axis_size("virt")
    mine = t2_amplitudes.reshape(rows, local_tiles, W).transpose(1, 0, 2).reshape(local_tiles * rows, W)
    halves, codes, own = prepare(
        integral_tiles.reshape(slots, W, W),
        in_tiles.reshape(1, slots),
        out_tiles.reshape(1, slots),
        tile_counts,
        mine,
        local_tiles,
    )
    line = jnp.stack([own] + [swap(mine, pairs, virts, mask, 1) for mask in range(NEAR, pairs, NEAR)])
    pieces = [line] + [swap(line, pairs, virts, mask, 1) for mask in range(1, NEAR)]
    blocks = pieces + [swap(piece, pairs, virts, 0, mask) for mask in range(1, virts) for piece in pieces]
    partial_sums = local_terms(codes, blocks, halves, rows, local_tiles)
    line_sums = swap_sum(partial_sums.reshape((NEAR, pairs // NEAR) + mine.shape), pairs, virts, 1)
    summed = swap_sum(line_sums, pairs, virts, NEAR)
    return summed.reshape(local_tiles, rows, W).transpose(1, 0, 2).reshape(rows, columns)


def solution(mesh):
    return jax.shard_map(
        shards,
        mesh=mesh,
        in_specs=(
            P("pair", "virt"),
            P("pair", "virt", None, None, None),
            P("pair", "virt", None),
            P("pair", "virt", None),
            P("pair", "virt"),
        ),
        out_specs=P("pair", "virt"),
        check_vma=False,
    )
```

```python
import jax
import jax.numpy as jnp
from jax import lax
from jax.experimental import pallas as pl
from jax.experimental.pallas import tpu as pltpu
from jax.sharding import PartitionSpec as P

W = 128
COPY_GROUP = 8
GROUP = 16
NEAR = 4
SMEM = pl.BlockSpec(memory_space=pltpu.SMEM)
VMEM = pl.BlockSpec(memory_space=pltpu.VMEM)


def split(value):
    high = value.astype(jnp.bfloat16)
    low = (value - high.astype(jnp.float32)).astype(jnp.bfloat16)
    return high, low


def tile_kernel(out_tiles, live, ins, outs, tiles, mine, halves, codes, own, held, index_rows, arrived, singles):
    singles_of = ((ins, index_rows.at[0]), (outs, index_rows.at[1]), (mine, own))
    others = [pltpu.make_async_copy(here, there, singles.at[at]) for at, (here, there) in enumerate(singles_of)]
    for copy in others:
        copy.start()
    count = live[0, 0]
    groups = (count + COPY_GROUP - 1) // COPY_GROUP

    def tile_copy(index):
        part = pl.ds(index * COPY_GROUP, COPY_GROUP)
        return pltpu.make_async_copy(tiles.at[part], held.at[part], arrived.at[index])

    def begin(index, carry):
        tile_copy(index).start()
        return carry

    lax.fori_loop(0, groups, begin, 0)
    for copy in others:
        copy.wait()
    slots = lax.broadcasted_iota(jnp.int32, ins.shape, 1)
    tile_in = index_rows[0]
    owner = lax.bitwise_xor(lax.div(tile_in, out_tiles), lax.axis_index("virt"))
    codes[0:1, :] = owner * out_tiles + lax.rem(tile_in, out_tiles)
    codes[1:2, :] = jnp.where(slots < count, lax.rem(index_rows[1], out_tiles), out_tiles)
    codes[2:3, :] = jnp.full(ins.shape, count, jnp.int32)

    def one_group(index, carry):
        tile_copy(index).wait()
        for step in range(COPY_GROUP):
            slot = index * COPY_GROUP + step
            high, low = split(held[slot])
            halves[slot, :, :W] = high
            halves[slot, :, W:] = low
        return carry

    lax.fori_loop(0, groups, one_group, 0)


def prepare(tiles, ins, outs, live, mine, out_tiles):
    slots = tiles.shape[0]

    def kernel(*refs):
        tile_kernel(out_tiles, *refs)

    operands = [pltpu.with_memory_space_constraint(value, pltpu.HBM) for value in (ins, outs, tiles, mine)]
    return pl.pallas_call(
        kernel,
        out_shape=(
            jax.ShapeDtypeStruct((slots, W, 2 * W), jnp.bfloat16),
            jax.ShapeDtypeStruct((3, slots), jnp.int32),
            jax.ShapeDtypeStruct(mine.shape, mine.dtype),
        ),
        in_specs=[SMEM] + [pl.BlockSpec(memory_space=pltpu.HBM)] * 4,
        out_specs=(VMEM, VMEM, VMEM),
        scratch_shapes=[
            pltpu.VMEM((slots, W, W), jnp.float32),
            pltpu.VMEM((2, 1, slots), jnp.int32),
            pltpu.SemaphoreType.DMA((slots // COPY_GROUP,)),
            pltpu.SemaphoreType.DMA((3,)),
        ],
        compiler_params=pltpu.CompilerParams(vmem_limit_bytes=32 * 1024 * 1024),
        cost_estimate=pl.CostEstimate(flops=4 * slots * W * W, bytes_accessed=8 * slots * W * W, transcendentals=0),
    )(live, *operands)


def far_masks(far):
    if far % 4:
        return list(range(1, far)), []
    singles = [mask for mask in range(1, far) if mask % 4 in (0, 3)]
    return singles, [(mask, mask + 1) for mask in range(1, far, 4)]


def turn(index):
    far = index // NEAR
    return (far ^ far // 2) % 2


def ladder_kernel(virts, codes_here, halves, *refs):
    blocks, (result, columns, flat, totals, codes, copied) = refs[: virts * NEAR], refs[virts * NEAR :]
    fetch = pltpu.make_async_copy(codes_here, codes, copied)
    fetch.start()
    far = blocks[0].shape[0]
    chunk_count = NEAR * far
    out_tiles = totals.shape[0] - 1
    rows = result.shape[1] // out_tiles
    total_rows = chunk_count * rows
    in_local = columns.shape[0] // virts
    totals[...] = jnp.zeros_like(totals)

    singles, couples = far_masks(far)
    base = 1 + len(singles)
    for owner in range(virts):
        odd = owner % 2
        for a in range(NEAR):
            same = blocks[(owner ^ int(a > 0)) * NEAR + a]
            other = blocks[(owner ^ int(a == 0)) * NEAR + a]
            sources = [(same, 0)] + [(other, at) for at in range(1, base)]
            for at in range(base, far, 2):
                sources += [(other, at), (same, at + 1)] if odd else [(same, at + 1), (other, at)]
            for b, (source, at) in enumerate(sources):
                place = pl.ds((a * far + b) * rows, rows)
                for tile in range(in_local):
                    flat[tile, place, :] = source[at, tile * rows : (tile + 1) * rows, :]
        for tile in range(in_local):
            high, low = split(flat[tile])
            columns[owner * in_local + tile, :total_rows, :] = high
            columns[owner * in_local + tile, total_rows:, :] = low

    fetch.wait()

    def one_group(index, carry):
        first = index * GROUP
        products = []
        for step in range(GROUP):
            got = jnp.dot(columns[codes[0, first + step]], halves[first + step], preferred_element_type=jnp.float32)
            upper, lower = got[:total_rows], got[total_rows:]
            products.append((upper[:, :W] + lower[:, :W]) + (upper[:, W:] + lower[:, W:]))
        for step in range(GROUP):
            place = codes[1, first + step]
            totals[place] = totals[place] + products[step]
        return carry

    lax.fori_loop(0, (codes[2, 0] + GROUP - 1) // GROUP, one_group, 0)
    swapped = lax.rem(lax.axis_index("virt"), 2) ^ turn(lax.axis_index("pair"))
    masks = [0] + singles
    for first, second in couples:
        masks += [jnp.where(swapped == 0, first, second), jnp.where(swapped == 0, second, first)]
    for a in range(NEAR):
        for b, mask in enumerate(masks):
            place = pl.ds((a * far + b) * rows, rows)
            for tile in range(out_tiles):
                result[a * far + mask, tile * rows : (tile + 1) * rows, :] = totals[tile, place, :]


def local_terms(codes, blocks, halves, rows, out_tiles):
    far, chunk_rows, _ = blocks[0].shape
    virts = len(blocks) // NEAR
    total_rows = NEAR * far * rows
    in_local = chunk_rows // rows

    def kernel(*refs):
        ladder_kernel(virts, *refs)

    return pl.pallas_call(
        kernel,
        out_shape=jax.ShapeDtypeStruct((NEAR * far, out_tiles * rows, W), jnp.float32),
        in_specs=[VMEM, VMEM] + [VMEM] * len(blocks),
        out_specs=VMEM,
        scratch_shapes=[
            pltpu.VMEM((virts * in_local, 2 * total_rows, W), jnp.bfloat16),
            pltpu.VMEM((in_local, total_rows, W), jnp.float32),
            pltpu.VMEM((out_tiles + 1, total_rows, W), jnp.float32),
            pltpu.SMEM(codes.shape, jnp.int32),
            pltpu.SemaphoreType.DMA,
        ],
        compiler_params=pltpu.CompilerParams(vmem_limit_bytes=32 * 1024 * 1024),
    )(codes, halves, *blocks)


def swap(value, pairs, virts, mask, virt_mask):
    mask_at = mask if callable(mask) else lambda a, b: mask
    routes = [
        (a * virts + b, (a ^ mask_at(a, b)) * virts + (b ^ virt_mask)) for a in range(pairs) for b in range(virts)
    ]
    return lax.ppermute(value, ("pair", "virt"), routes)


def gather_line(mine, own, pairs, virts):
    singles, couples = far_masks(pairs // NEAR)
    neighbour = swap(mine, pairs, virts, 0, 1)
    near = copy_near(mine)
    line = [own[None]] + [swap(near, pairs, virts, mask * NEAR, 1)[None] for mask in singles]
    both = jnp.stack([near, neighbour])
    for couple in couples:
        line.append(swap(both, pairs, virts, lambda a, b: couple[turn(a) ^ b % 2] * NEAR, 1))
    return jnp.concatenate(line)


def copy_kernel(value, result, copied):
    copy = pltpu.make_async_copy(value, result, copied)
    copy.start()
    copy.wait()


def copy_near(value):
    return pl.pallas_call(
        copy_kernel,
        out_shape=jax.ShapeDtypeStruct(value.shape, value.dtype),
        in_specs=[pl.BlockSpec(memory_space=pltpu.HBM)],
        out_specs=VMEM,
        scratch_shapes=[pltpu.SemaphoreType.DMA],
        cost_estimate=pl.CostEstimate(flops=0, bytes_accessed=1 << 22, transcendentals=0),
    )(pltpu.with_memory_space_constraint(value, pltpu.HBM))


def swap_sum(parts, pairs, virts, unit):
    last = len(parts) - 1
    received = [swap(parts[i], pairs, virts, i * unit, 1) for i in (0, last, *range(1, last))]
    return sum(received[1:], received[0])


def shards(t2_amplitudes, integral_tiles, out_tiles, in_tiles, tile_counts):
    rows, columns = t2_amplitudes.shape
    local_tiles = columns // W
    slots = integral_tiles.shape[2]
    pairs, virts = lax.axis_size("pair"), lax.axis_size("virt")
    mine = t2_amplitudes.reshape(rows, local_tiles, W).transpose(1, 0, 2).reshape(local_tiles * rows, W)
    halves, codes, own = prepare(
        integral_tiles.reshape(slots, W, W),
        in_tiles.reshape(1, slots),
        out_tiles.reshape(1, slots),
        tile_counts,
        mine,
        local_tiles,
    )
    line = gather_line(mine, own, pairs, virts)
    pieces = [line] + [swap(line, pairs, virts, mask, 1) for mask in range(1, NEAR)]
    blocks = pieces + [swap(piece, pairs, virts, 0, mask) for mask in range(1, virts) for piece in pieces]
    partial_sums = local_terms(codes, blocks, halves, rows, local_tiles)
    line_sums = swap_sum(partial_sums.reshape((NEAR, pairs // NEAR) + mine.shape), pairs, virts, 1)
    summed = swap_sum(line_sums, pairs, virts, NEAR)
    return summed.reshape(local_tiles, rows, W).transpose(1, 0, 2).reshape(rows, columns)


def solution(mesh):
    return jax.shard_map(
        shards,
        mesh=mesh,
        in_specs=(
            P("pair", "virt"),
            P("pair", "virt", None, None, None),
            P("pair", "virt", None),
            P("pair", "virt", None),
            P("pair", "virt"),
        ),
        out_specs=P("pair", "virt"),
        check_vma=False,
    )
```

```python
import jax
import jax.numpy as jnp
from jax import lax
from jax.experimental import pallas as pl
from jax.experimental.pallas import tpu as pltpu
from jax.sharding import PartitionSpec as P

W = 128
COPY_GROUP = 8
GROUP = 16
NEAR = 4
SWITCHED = (0, 2, 1, 3)
SMEM = pl.BlockSpec(memory_space=pltpu.SMEM)
VMEM = pl.BlockSpec(memory_space=pltpu.VMEM)


def split(value):
    high = value.astype(jnp.bfloat16)
    low = (value - high.astype(jnp.float32)).astype(jnp.bfloat16)
    return high, low


def tile_kernel(out_tiles, live, ins, outs, tiles, mine, halves, codes, own, held, index_rows, arrived, singles):
    singles_of = ((ins, index_rows.at[0]), (outs, index_rows.at[1]), (mine, own))
    others = [pltpu.make_async_copy(here, there, singles.at[at]) for at, (here, there) in enumerate(singles_of)]
    for copy in others:
        copy.start()
    count = live[0, 0]
    groups = (count + COPY_GROUP - 1) // COPY_GROUP

    def tile_copy(index):
        part = pl.ds(index * COPY_GROUP, COPY_GROUP)
        return pltpu.make_async_copy(tiles.at[part], held.at[part], arrived.at[index])

    def begin(index, carry):
        tile_copy(index).start()
        return carry

    lax.fori_loop(0, groups, begin, 0)
    for copy in others:
        copy.wait()
    slots = lax.broadcasted_iota(jnp.int32, ins.shape, 1)
    tile_in = index_rows[0]
    owner = lax.bitwise_xor(lax.div(tile_in, out_tiles), lax.axis_index("virt"))
    codes[0:1, :] = owner * out_tiles + lax.rem(tile_in, out_tiles)
    codes[1:2, :] = jnp.where(slots < count, lax.rem(index_rows[1], out_tiles), out_tiles)
    codes[2:3, :] = jnp.full(ins.shape, count, jnp.int32)

    def one_group(index, carry):
        tile_copy(index).wait()
        for step in range(COPY_GROUP):
            slot = index * COPY_GROUP + step
            high, low = split(held[slot])
            halves[slot, :, :W] = high
            halves[slot, :, W:] = low
        return carry

    lax.fori_loop(0, groups, one_group, 0)


def prepare(tiles, ins, outs, live, mine, out_tiles):
    slots = tiles.shape[0]

    def kernel(*refs):
        tile_kernel(out_tiles, *refs)

    operands = [pltpu.with_memory_space_constraint(value, pltpu.HBM) for value in (ins, outs, tiles, mine)]
    return pl.pallas_call(
        kernel,
        out_shape=(
            jax.ShapeDtypeStruct((slots, W, 2 * W), jnp.bfloat16),
            jax.ShapeDtypeStruct((3, slots), jnp.int32),
            jax.ShapeDtypeStruct(mine.shape, mine.dtype),
        ),
        in_specs=[SMEM] + [pl.BlockSpec(memory_space=pltpu.HBM)] * 4,
        out_specs=(VMEM, VMEM, VMEM),
        scratch_shapes=[
            pltpu.VMEM((slots, W, W), jnp.float32),
            pltpu.VMEM((2, 1, slots), jnp.int32),
            pltpu.SemaphoreType.DMA((slots // COPY_GROUP,)),
            pltpu.SemaphoreType.DMA((3,)),
        ],
        compiler_params=pltpu.CompilerParams(vmem_limit_bytes=32 * 1024 * 1024),
        cost_estimate=pl.CostEstimate(flops=4 * slots * W * W, bytes_accessed=8 * slots * W * W, transcendentals=0),
    )(live, *operands)


def ladder_kernel(virts, codes_here, halves, *refs):
    blocks, (result, columns, flat, totals, codes, copied) = refs[: virts * NEAR], refs[virts * NEAR :]
    fetch = pltpu.make_async_copy(codes_here, codes, copied)
    fetch.start()
    far = blocks[0].shape[0]
    chunk_count = NEAR * far
    out_tiles = totals.shape[0] - 1
    rows = result.shape[1] // out_tiles
    total_rows = chunk_count * rows
    in_local = columns.shape[0] // virts
    totals[...] = jnp.zeros_like(totals)

    for owner in range(virts):
        for a in range(NEAR):
            for b in range(far):
                from_virt = owner ^ int((a > 0) != (b > 0))
                source = blocks[from_virt * NEAR + (SWITCHED[a] if from_virt % 2 else a)]
                place = pl.ds((a * far + b) * rows, rows)
                for tile in range(in_local):
                    flat[tile, place, :] = source[b, tile * rows : (tile + 1) * rows, :]
        for tile in range(in_local):
            high, low = split(flat[tile])
            columns[owner * in_local + tile, :total_rows, :] = high
            columns[owner * in_local + tile, total_rows:, :] = low

    fetch.wait()

    def one_group(index, carry):
        first = index * GROUP
        products = []
        for step in range(GROUP):
            got = jnp.dot(columns[codes[0, first + step]], halves[first + step], preferred_element_type=jnp.float32)
            upper, lower = got[:total_rows], got[total_rows:]
            products.append((upper[:, :W] + lower[:, :W]) + (upper[:, W:] + lower[:, W:]))
        for step in range(GROUP):
            place = codes[1, first + step]
            totals[place] = totals[place] + products[step]
        return carry

    lax.fori_loop(0, (codes[2, 0] + GROUP - 1) // GROUP, one_group, 0)
    def give(chunk, carry):
        for tile in range(out_tiles):
            result[chunk, tile * rows : (tile + 1) * rows, :] = totals[tile, pl.ds(chunk * rows, rows), :]
        return carry

    lax.fori_loop(0, chunk_count, give, 0, unroll=min(chunk_count, 16))


def local_terms(codes, blocks, halves, rows, out_tiles):
    far, chunk_rows, _ = blocks[0].shape
    virts = len(blocks) // NEAR
    total_rows = NEAR * far * rows
    in_local = chunk_rows // rows

    def kernel(*refs):
        ladder_kernel(virts, *refs)

    return pl.pallas_call(
        kernel,
        out_shape=jax.ShapeDtypeStruct((NEAR * far, out_tiles * rows, W), jnp.float32),
        in_specs=[VMEM, VMEM] + [VMEM] * len(blocks),
        out_specs=VMEM,
        scratch_shapes=[
            pltpu.VMEM((virts * in_local, 2 * total_rows, W), jnp.bfloat16),
            pltpu.VMEM((in_local, total_rows, W), jnp.float32),
            pltpu.VMEM((out_tiles + 1, total_rows, W), jnp.float32),
            pltpu.SMEM(codes.shape, jnp.int32),
            pltpu.SemaphoreType.DMA,
        ],
        compiler_params=pltpu.CompilerParams(vmem_limit_bytes=32 * 1024 * 1024),
    )(codes, halves, *blocks)


def near_mask(step, a, b):
    return SWITCHED[step] if (a ^ a // 2 ^ b) % 2 else step


def swap(value, pairs, virts, virt_mask, step=0, far=0):
    routes = [
        (a * virts + b, (a ^ far * NEAR ^ near_mask(step, a, b)) * virts + (b ^ virt_mask))
        for a in range(pairs)
        for b in range(virts)
    ]
    return lax.ppermute(value, ("pair", "virt"), routes)


def swap_sum(parts, pairs, virts, which):
    last = len(parts) - 1
    received = [swap(parts[i], pairs, virts, 1, **{which: i}) for i in (0, last, *range(1, last))]
    return sum(received[1:], received[0])


def shards(t2_amplitudes, integral_tiles, out_tiles, in_tiles, tile_counts):
    rows, columns = t2_amplitudes.shape
    local_tiles = columns // W
    slots = integral_tiles.shape[2]
    pairs, virts = lax.axis_size("pair"), lax.axis_size("virt")
    mine = t2_amplitudes.reshape(rows, local_tiles, W).transpose(1, 0, 2).reshape(local_tiles * rows, W)
    halves, codes, own = prepare(
        integral_tiles.reshape(slots, W, W),
        in_tiles.reshape(1, slots),
        out_tiles.reshape(1, slots),
        tile_counts,
        mine,
        local_tiles,
    )
    line = jnp.stack([own] + [swap(mine, pairs, virts, 1, far=mask) for mask in range(1, pairs // NEAR)])
    pieces = [line] + [swap(line, pairs, virts, 1, step=step) for step in range(1, NEAR)]
    blocks = pieces + [swap(piece, pairs, virts, mask) for mask in range(1, virts) for piece in pieces]
    partial_sums = local_terms(codes, blocks, halves, rows, local_tiles)
    line_sums = swap_sum(partial_sums.reshape((NEAR, pairs // NEAR) + mine.shape), pairs, virts, "step")
    summed = swap_sum(line_sums, pairs, virts, "far")
    return summed.reshape(local_tiles, rows, W).transpose(1, 0, 2).reshape(rows, columns)


def solution(mesh):
    return jax.shard_map(
        shards,
        mesh=mesh,
        in_specs=(
            P("pair", "virt"),
            P("pair", "virt", None, None, None),
            P("pair", "virt", None),
            P("pair", "virt", None),
            P("pair", "virt"),
        ),
        out_specs=P("pair", "virt"),
        check_vma=False,
    )
```

```python
import jax
import jax.numpy as jnp
from jax import lax
from jax.experimental import pallas as pl
from jax.experimental.pallas import tpu as pltpu
from jax.sharding import PartitionSpec as P

W = 128
COPY_GROUP = 8
GROUP = 16
NEAR = 4
SWITCHED = (0, 2, 1, 3)
SMEM = pl.BlockSpec(memory_space=pltpu.SMEM)
VMEM = pl.BlockSpec(memory_space=pltpu.VMEM)


def split(value):
    high = value.astype(jnp.bfloat16)
    low = (value - high.astype(jnp.float32)).astype(jnp.bfloat16)
    return high, low


def tile_kernel(out_tiles, live, ins, outs, tiles, mine, halves, codes, own, held, index_rows, arrived, singles):
    singles_of = ((ins, index_rows.at[0]), (outs, index_rows.at[1]), (mine, own))
    others = [pltpu.make_async_copy(here, there, singles.at[at]) for at, (here, there) in enumerate(singles_of)]
    for copy in others:
        copy.start()
    count = live[0, 0]
    groups = (count + COPY_GROUP - 1) // COPY_GROUP

    def tile_copy(index):
        part = pl.ds(index * COPY_GROUP, COPY_GROUP)
        return pltpu.make_async_copy(tiles.at[part], held.at[part], arrived.at[index])

    def begin(index, carry):
        tile_copy(index).start()
        return carry

    lax.fori_loop(0, groups, begin, 0)
    for copy in others:
        copy.wait()
    slots = lax.broadcasted_iota(jnp.int32, ins.shape, 1)
    tile_in = index_rows[0]
    owner = lax.bitwise_xor(lax.div(tile_in, out_tiles), lax.axis_index("virt"))
    codes[0:1, :] = owner * out_tiles + lax.rem(tile_in, out_tiles)
    codes[1:2, :] = jnp.where(slots < count, lax.rem(index_rows[1], out_tiles), out_tiles)
    codes[2:3, :] = jnp.full(ins.shape, count, jnp.int32)

    def one_group(index, carry):
        tile_copy(index).wait()
        for step in range(COPY_GROUP):
            slot = index * COPY_GROUP + step
            high, low = split(held[slot])
            halves[slot, :, :W] = high
            halves[slot, :, W:] = low
        return carry

    lax.fori_loop(0, groups, one_group, 0)


def prepare(tiles, ins, outs, live, mine, out_tiles):
    slots = tiles.shape[0]

    def kernel(*refs):
        tile_kernel(out_tiles, *refs)

    operands = [pltpu.with_memory_space_constraint(value, pltpu.HBM) for value in (ins, outs, tiles, mine)]
    return pl.pallas_call(
        kernel,
        out_shape=(
            jax.ShapeDtypeStruct((slots, W, 2 * W), jnp.bfloat16),
            jax.ShapeDtypeStruct((3, slots), jnp.int32),
            jax.ShapeDtypeStruct(mine.shape, mine.dtype),
        ),
        in_specs=[SMEM] + [pl.BlockSpec(memory_space=pltpu.HBM)] * 4,
        out_specs=(VMEM, VMEM, VMEM),
        scratch_shapes=[
            pltpu.VMEM((slots, W, W), jnp.float32),
            pltpu.VMEM((2, 1, slots), jnp.int32),
            pltpu.SemaphoreType.DMA((slots // COPY_GROUP,)),
            pltpu.SemaphoreType.DMA((3,)),
        ],
        compiler_params=pltpu.CompilerParams(vmem_limit_bytes=32 * 1024 * 1024),
        cost_estimate=pl.CostEstimate(flops=4 * slots * W * W, bytes_accessed=8 * slots * W * W, transcendentals=0),
    )(live, *operands)


def weave(first, second):
    half = first.shape[0] // 2
    upper = lax.broadcasted_iota(jnp.int32, first.shape, 0) < half
    return (
        jnp.where(upper, first, pltpu.roll(second, half, 0)),
        jnp.where(upper, pltpu.roll(first, half, 0), second),
    )


def ladder_kernel(virts, codes_here, halves, *refs):
    blocks, (result, columns, totals, codes, copied) = refs[: virts * NEAR], refs[virts * NEAR :]
    fetch = pltpu.make_async_copy(codes_here, codes, copied)
    fetch.start()
    far = blocks[0].shape[0]
    chunk_count = NEAR * far
    out_tiles = totals.shape[0] - 1
    rows = result.shape[1] // out_tiles
    total_rows = chunk_count * rows
    in_local = columns.shape[0] // virts
    totals[...] = jnp.zeros_like(totals)

    for owner in range(virts):
        for a in range(NEAR):
            sources = []
            for b in range(far):
                from_virt = owner ^ int((a > 0) != (b > 0))
                sources.append(blocks[from_virt * NEAR + (SWITCHED[a] if from_virt % 2 else a)])
            for b in range(0, far, 4):
                first_row = (a * far + b) * rows
                for tile in range(0, in_local, 2):
                    part = slice(tile * rows, (tile + 2) * rows)
                    four = [sources[b + at][b + at, part, :] for at in range(4)]
                    for at, pieces in enumerate(zip(weave(*four[:2]), weave(*four[2:]))):
                        high, low = split(jnp.concatenate(pieces, axis=0))
                        column = owner * in_local + tile + at
                        columns[column, first_row : first_row + 4 * rows, :] = high
                        columns[column, total_rows + first_row : total_rows + first_row + 4 * rows, :] = low

    fetch.wait()

    def one_group(index, carry):
        first = index * GROUP
        products = []
        for step in range(GROUP):
            got = jnp.dot(columns[codes[0, first + step]], halves[first + step], preferred_element_type=jnp.float32)
            upper, lower = got[:total_rows], got[total_rows:]
            products.append((upper[:, :W] + lower[:, :W]) + (upper[:, W:] + lower[:, W:]))
        for step in range(GROUP):
            place = codes[1, first + step]
            totals[place] = totals[place] + products[step]
        return carry

    lax.fori_loop(0, (codes[2, 0] + GROUP - 1) // GROUP, one_group, 0)
    for chunk in range(0, chunk_count, 2):
        part = slice(chunk * rows, (chunk + 2) * rows)
        for tile in range(0, out_tiles, 2):
            pieces = weave(totals[tile, part, :], totals[tile + 1, part, :])
            for at, piece in enumerate(pieces):
                result[chunk + at, tile * rows : (tile + 2) * rows, :] = piece


def local_terms(codes, blocks, halves, rows, out_tiles):
    far, chunk_rows, _ = blocks[0].shape
    virts = len(blocks) // NEAR
    total_rows = NEAR * far * rows
    in_local = chunk_rows // rows

    def kernel(*refs):
        ladder_kernel(virts, *refs)

    return pl.pallas_call(
        kernel,
        out_shape=jax.ShapeDtypeStruct((NEAR * far, out_tiles * rows, W), jnp.float32),
        in_specs=[VMEM, VMEM] + [VMEM] * len(blocks),
        out_specs=VMEM,
        scratch_shapes=[
            pltpu.VMEM((virts * in_local, 2 * total_rows, W), jnp.bfloat16),
            pltpu.VMEM((out_tiles + 1, total_rows, W), jnp.float32),
            pltpu.SMEM(codes.shape, jnp.int32),
            pltpu.SemaphoreType.DMA,
        ],
        compiler_params=pltpu.CompilerParams(vmem_limit_bytes=32 * 1024 * 1024),
    )(codes, halves, *blocks)


def near_mask(step, a, b):
    return SWITCHED[step] if (a ^ a // 2 ^ b) % 2 else step


def swap(value, pairs, virts, virt_mask, step=0, far=0):
    routes = [
        (a * virts + b, (a ^ far * NEAR ^ near_mask(step, a, b)) * virts + (b ^ virt_mask))
        for a in range(pairs)
        for b in range(virts)
    ]
    return lax.ppermute(value, ("pair", "virt"), routes)


def far_order(far):
    return [*range(far - 2), far - 1, far - 2]


def swap_sum(parts, pairs, virts, which, marks):
    last = len(marks) - 1
    order = (0, last, *range(1, last))
    received = [swap(parts[marks.index(mark)], pairs, virts, 1, **{which: mark}) for mark in order]
    return sum(received[1:], received[0])


def shards(t2_amplitudes, integral_tiles, out_tiles, in_tiles, tile_counts):
    rows, columns = t2_amplitudes.shape
    local_tiles = columns // W
    slots = integral_tiles.shape[2]
    pairs, virts = lax.axis_size("pair"), lax.axis_size("virt")
    mine = t2_amplitudes.reshape(rows, local_tiles, W).transpose(1, 0, 2).reshape(local_tiles * rows, W)
    halves, codes, own = prepare(
        integral_tiles.reshape(slots, W, W),
        in_tiles.reshape(1, slots),
        out_tiles.reshape(1, slots),
        tile_counts,
        mine,
        local_tiles,
    )
    order = far_order(pairs // NEAR)
    line = jnp.stack([own] + [swap(mine, pairs, virts, 1, far=mask) for mask in order[1:]])
    pieces = [line] + [swap(line, pairs, virts, 1, step=step) for step in range(1, NEAR)]
    blocks = pieces + [swap(piece, pairs, virts, mask) for mask in range(1, virts) for piece in pieces]
    partial_sums = local_terms(codes, blocks, halves, rows, local_tiles)
    line_sums = swap_sum(partial_sums.reshape((NEAR, pairs // NEAR) + mine.shape), pairs, virts, "step", list(range(NEAR)))
    summed = swap_sum(line_sums, pairs, virts, "far", order)
    return summed.reshape(local_tiles, rows, W).transpose(1, 0, 2).reshape(rows, columns)


def solution(mesh):
    return jax.shard_map(
        shards,
        mesh=mesh,
        in_specs=(
            P("pair", "virt"),
            P("pair", "virt", None, None, None),
            P("pair", "virt", None),
            P("pair", "virt", None),
            P("pair", "virt"),
        ),
        out_specs=P("pair", "virt"),
        check_vma=False,
    )
```

```python
import jax
import jax.numpy as jnp
from jax import lax
from jax.experimental import pallas as pl
from jax.experimental.pallas import tpu as pltpu
from jax.sharding import PartitionSpec as P

W = 128
COPY_GROUP = 8
GROUP = 8
NEAR = 4
SWITCHED = (0, 2, 1, 3)
SMEM = pl.BlockSpec(memory_space=pltpu.SMEM)
VMEM = pl.BlockSpec(memory_space=pltpu.VMEM)


def split(value):
    high = value.astype(jnp.bfloat16)
    low = (value - high.astype(jnp.float32)).astype(jnp.bfloat16)
    return high, low


def slot_list(chosen, rows):
    slots = chosen.shape[1]
    shape = (slots, slots)
    down, across = lax.broadcasted_iota(jnp.int32, shape, 0), lax.broadcasted_iota(jnp.int32, shape, 1)

    def turned(row):
        return jnp.sum(jnp.where(down == across, jnp.broadcast_to(row, shape), 0.0), axis=1, keepdims=True)

    ahead = jnp.sum(jnp.where(across < down, jnp.broadcast_to(chosen, shape), 0.0), axis=1, keepdims=True)
    here = (ahead.astype(jnp.int32) == across) & (turned(chosen) > 0.5)
    return [jnp.sum(jnp.where(here, turned(row), 0.0), axis=0, keepdims=True) for row in rows]


def tile_kernel(out_tiles, live, ins, outs, tiles, halves, codes, held, index_rows, arrived, singles):
    others = [pltpu.make_async_copy(rows, index_rows.at[at], singles.at[at]) for at, rows in enumerate((ins, outs))]
    for copy in others:
        copy.start()
    count = live[0, 0]
    groups = (count + COPY_GROUP - 1) // COPY_GROUP

    def tile_copy(index):
        part = pl.ds(index * COPY_GROUP, COPY_GROUP)
        return pltpu.make_async_copy(tiles.at[part], held.at[part], arrived.at[index])

    def begin(index, carry):
        tile_copy(index).start()
        return carry

    lax.fori_loop(0, groups, begin, 0)
    for copy in others:
        copy.wait()
    slots = lax.broadcasted_iota(jnp.int32, ins.shape, 1)
    tile_in = index_rows[0]
    owner = lax.bitwise_xor(lax.div(tile_in, out_tiles), lax.axis_index("virt"))
    local = lax.rem(tile_in, out_tiles)
    place = lax.rem(index_rows[1], out_tiles)
    for base, is_own in ((0, True), (4, False)):
        chosen = jnp.where((slots < count) & ((owner == 0) == is_own), 1.0, 0.0)
        column = local if is_own else local + (owner - 1) * out_tiles
        rows = [value.astype(jnp.float32) for value in (slots, column, place)]
        slot_row, column_row, place_row = [row.astype(jnp.int32) for row in slot_list(chosen, rows)]
        number = jnp.broadcast_to(jnp.sum(chosen, axis=1, keepdims=True), ins.shape).astype(jnp.int32)
        codes[base : base + 1, :] = slot_row
        codes[base + 1 : base + 2, :] = column_row
        codes[base + 2 : base + 3, :] = jnp.where(slots < number, place_row, out_tiles)
        codes[base + 3 : base + 4, :] = number

    def one_group(index, carry):
        tile_copy(index).wait()
        for step in range(COPY_GROUP):
            slot = index * COPY_GROUP + step
            high, low = split(held[slot])
            halves[slot, :, :W] = high
            halves[slot, :, W:] = low
        return carry

    lax.fori_loop(0, groups, one_group, 0)


def prepare(tiles, ins, outs, live, out_tiles):
    slots = tiles.shape[0]

    def kernel(*refs):
        tile_kernel(out_tiles, *refs)

    operands = [pltpu.with_memory_space_constraint(value, pltpu.HBM) for value in (ins, outs, tiles)]
    return pl.pallas_call(
        kernel,
        out_shape=(
            jax.ShapeDtypeStruct((slots, W, 2 * W), jnp.bfloat16),
            jax.ShapeDtypeStruct((8, slots), jnp.int32),
        ),
        in_specs=[SMEM] + [pl.BlockSpec(memory_space=pltpu.HBM)] * 3,
        out_specs=(VMEM, VMEM),
        scratch_shapes=[
            pltpu.VMEM((slots, W, W), jnp.float32),
            pltpu.VMEM((2, 1, slots), jnp.int32),
            pltpu.SemaphoreType.DMA((slots // COPY_GROUP,)),
            pltpu.SemaphoreType.DMA((2,)),
        ],
        compiler_params=pltpu.CompilerParams(vmem_limit_bytes=32 * 1024 * 1024),
        cost_estimate=pl.CostEstimate(flops=4 * slots * W * W, bytes_accessed=8 * slots * W * W, transcendentals=0),
    )(live, *operands)


def weave(first, second):
    half = first.shape[0] // 2
    upper = lax.broadcasted_iota(jnp.int32, first.shape, 0) < half
    return (
        jnp.where(upper, first, pltpu.roll(second, half, 0)),
        jnp.where(upper, pltpu.roll(first, half, 0), second),
    )


def fill_columns(columns, first_column, lines, rows):
    far, chunk_rows, _ = lines[0].shape
    total_rows = len(lines) * far * rows
    for a, line in enumerate(lines):
        for b in range(0, far, 4):
            first_row = (a * far + b) * rows
            for tile in range(0, chunk_rows // rows, 2):
                part = slice(tile * rows, (tile + 2) * rows)
                four = [line[b + at, part, :] for at in range(4)]
                for at, pieces in enumerate(zip(weave(*four[:2]), weave(*four[2:]))):
                    high, low = split(jnp.concatenate(pieces, axis=0))
                    column = first_column + tile + at
                    columns[column, first_row : first_row + 4 * rows, :] = high
                    columns[column, total_rows + first_row : total_rows + first_row + 4 * rows, :] = low


def add_products(base, codes, columns, halves, totals):
    total_rows = totals.shape[1]

    def one_group(index, carry):
        first = index * GROUP
        products = []
        for step in range(GROUP):
            slot, column = codes[base, first + step], codes[base + 1, first + step]
            got = jnp.dot(columns[column], halves[slot], preferred_element_type=jnp.float32)
            upper, lower = got[:total_rows], got[total_rows:]
            products.append((upper[:, :W] + lower[:, :W]) + (upper[:, W:] + lower[:, W:]))
        for step in range(GROUP):
            place = codes[base + 2, first + step]
            totals[place] = totals[place] + products[step]
        return carry

    lax.fori_loop(0, (codes[base + 3, 0] + GROUP - 1) // GROUP, one_group, 0)


def own_kernel(rows, codes_here, halves, *refs):
    lines, (totals, columns, codes, copied) = refs[:NEAR], refs[NEAR:]
    fetch = pltpu.make_async_copy(codes_here, codes, copied)
    fetch.start()
    totals[...] = jnp.zeros_like(totals)
    fill_columns(columns, 0, lines, rows)
    fetch.wait()
    add_products(0, codes, columns, halves, totals)


def rest_kernel(rows, codes_here, halves, own_totals, *refs):
    lines, (result, columns, totals, codes, copied) = refs[:-5], refs[-5:]
    fetch = pltpu.make_async_copy(codes_here, codes, copied)
    fetch.start()
    totals[...] = own_totals[...]
    in_local = lines[0].shape[1] // rows
    for owner in range(len(lines) // NEAR):
        fill_columns(columns, owner * in_local, lines[owner * NEAR : (owner + 1) * NEAR], rows)
    fetch.wait()
    add_products(4, codes, columns, halves, totals)
    for chunk in range(0, result.shape[0], 2):
        part = slice(chunk * rows, (chunk + 2) * rows)
        for tile in range(0, result.shape[1] // rows, 2):
            pieces = weave(totals[tile, part, :], totals[tile + 1, part, :])
            for at, piece in enumerate(pieces):
                result[chunk + at, tile * rows : (tile + 2) * rows, :] = piece


def local_terms(codes, owners, halves, rows, out_tiles):
    far, chunk_rows, _ = owners[0][0].shape
    total_rows = NEAR * far * rows
    in_local = chunk_rows // rows
    totals = jax.ShapeDtypeStruct((out_tiles + 1, total_rows, W), jnp.float32)

    def scratch(count):
        return [
            pltpu.VMEM((count * in_local, 2 * total_rows, W), jnp.bfloat16),
            pltpu.SMEM(codes.shape, jnp.int32),
            pltpu.SemaphoreType.DMA,
        ]

    def own(*refs):
        own_kernel(rows, *refs)

    def rest(*refs):
        rest_kernel(rows, *refs)

    settings = dict(
        compiler_params=pltpu.CompilerParams(vmem_limit_bytes=32 * 1024 * 1024),
        cost_estimate=pl.CostEstimate(flops=1 << 28, bytes_accessed=1 << 21, transcendentals=0),
    )
    own_totals = pl.pallas_call(
        own, out_shape=totals, in_specs=[VMEM] * (2 + NEAR), out_specs=VMEM, scratch_shapes=scratch(1), **settings
    )(codes, halves, *owners[0])
    others = [line for lines in owners[1:] for line in lines]
    columns, *others_scratch = scratch(len(owners) - 1)
    return pl.pallas_call(
        rest,
        out_shape=jax.ShapeDtypeStruct((NEAR * far, out_tiles * rows, W), jnp.float32),
        in_specs=[VMEM] * (3 + len(others)),
        out_specs=VMEM,
        scratch_shapes=[columns, pltpu.VMEM(totals.shape, totals.dtype)] + others_scratch,
        **settings,
    )(codes, halves, own_totals, *others)


def near_mask(step, a, b):
    return SWITCHED[step] if (a ^ a // 2 ^ b) % 2 else step


def swap(value, pairs, virts, virt_mask, step=0, far=0):
    routes = [
        (a * virts + b, (a ^ far * NEAR ^ near_mask(step, a, b)) * virts + (b ^ virt_mask))
        for a in range(pairs)
        for b in range(virts)
    ]
    return lax.ppermute(value, ("pair", "virt"), routes)


def far_order(far):
    return [*range(far - 2), far - 1, far - 2]


def swap_sum(parts, pairs, virts, which, marks):
    last = len(marks) - 1
    order = (0, last, *range(1, last))
    received = [swap(parts[marks.index(mark)], pairs, virts, 1, **{which: mark}) for mark in order]
    return sum(received[1:], received[0])


def shards(t2_amplitudes, integral_tiles, out_tiles, in_tiles, tile_counts):
    rows, columns = t2_amplitudes.shape
    local_tiles = columns // W
    slots = integral_tiles.shape[2]
    pairs, virts = lax.axis_size("pair"), lax.axis_size("virt")
    mine = t2_amplitudes.reshape(rows, local_tiles, W).transpose(1, 0, 2).reshape(local_tiles * rows, W)
    neighbour = swap(mine, pairs, virts, 1)
    halves, codes = prepare(
        integral_tiles.reshape(slots, W, W),
        in_tiles.reshape(1, slots),
        out_tiles.reshape(1, slots),
        tile_counts,
        local_tiles,
    )
    neighbour, codes = lax.optimization_barrier((neighbour, codes))
    order = far_order(pairs // NEAR)
    line = jnp.stack([neighbour] + [swap(mine, pairs, virts, 1, far=mask) for mask in order[1:]])
    pieces = [line] + [swap(line, pairs, virts, 1, step=step) for step in range(1, NEAR)]
    blocks = [pieces] + [[swap(piece, pairs, virts, mask) for piece in pieces] for mask in range(1, virts)]
    owners = [
        [blocks[mask ^ 1][0]] + [blocks[mask][SWITCHED[a] if mask % 2 else a] for a in range(1, NEAR)]
        for mask in range(virts)
    ]
    partial_sums = local_terms(codes, owners, halves, rows, local_tiles)
    line_sums = swap_sum(partial_sums.reshape((NEAR, pairs // NEAR) + mine.shape), pairs, virts, "step", list(range(NEAR)))
    summed = swap_sum(line_sums, pairs, virts, "far", order)
    return summed.reshape(local_tiles, rows, W).transpose(1, 0, 2).reshape(rows, columns)


def solution(mesh):
    return jax.shard_map(
        shards,
        mesh=mesh,
        in_specs=(
            P("pair", "virt"),
            P("pair", "virt", None, None, None),
            P("pair", "virt", None),
            P("pair", "virt", None),
            P("pair", "virt"),
        ),
        out_specs=P("pair", "virt"),
        check_vma=False,
    )
```

```python
import jax
import jax.numpy as jnp
from jax import lax
from jax.experimental import pallas as pl
from jax.experimental.pallas import tpu as pltpu
from jax.sharding import PartitionSpec as P

W = 128
COPY_GROUP = 8
GROUP = 16
NEAR = 4
SWITCHED = (0, 2, 1, 3)
SMEM = pl.BlockSpec(memory_space=pltpu.SMEM)
VMEM = pl.BlockSpec(memory_space=pltpu.VMEM)


def split(value):
    high = value.astype(jnp.bfloat16)
    low = (value - high.astype(jnp.float32)).astype(jnp.bfloat16)
    return high, low


def tile_kernel(out_tiles, live, ins, outs, tiles, mine, halves, codes, own, held, in_row, out_row, arrived, singles):
    singles_of = ((ins, in_row), (outs, out_row), (mine, own))
    others = [pltpu.make_async_copy(here, there, singles.at[at]) for at, (here, there) in enumerate(singles_of)]
    for copy in others:
        copy.start()
    count = live[0, 0]
    groups = (count + COPY_GROUP - 1) // COPY_GROUP

    def tile_copy(index):
        part = pl.ds(index * COPY_GROUP, COPY_GROUP)
        return pltpu.make_async_copy(tiles.at[part], held.at[part], arrived.at[index])

    def begin(index, carry):
        tile_copy(index).start()
        return carry

    lax.fori_loop(0, groups, begin, 0)
    for copy in others:
        copy.wait()
    me = lax.axis_index("virt")
    codes[2, 0] = count
    for slot in range(ins.shape[1]):
        tile_in = in_row[0, slot]
        owner = lax.bitwise_xor(lax.div(tile_in, out_tiles), me)
        codes[0, slot] = owner * out_tiles + lax.rem(tile_in, out_tiles)
        codes[1, slot] = jnp.where(slot < count, lax.rem(out_row[0, slot], out_tiles), out_tiles)

    def one_group(index, carry):
        tile_copy(index).wait()
        for step in range(COPY_GROUP):
            slot = index * COPY_GROUP + step
            high, low = split(held[slot])
            halves[slot, :, :W] = high
            halves[slot, :, W:] = low
        return carry

    lax.fori_loop(0, groups, one_group, 0)


def prepare(tiles, ins, outs, live, mine, out_tiles):
    slots = tiles.shape[0]

    def kernel(*refs):
        tile_kernel(out_tiles, *refs)

    operands = [pltpu.with_memory_space_constraint(value, pltpu.HBM) for value in (ins, outs, tiles, mine)]
    return pl.pallas_call(
        kernel,
        out_shape=(
            jax.ShapeDtypeStruct((slots, W, 2 * W), jnp.bfloat16),
            pltpu.SMEM((3, slots), jnp.int32),
            jax.ShapeDtypeStruct(mine.shape, mine.dtype),
        ),
        in_specs=[SMEM] + [pl.BlockSpec(memory_space=pltpu.HBM)] * 4,
        out_specs=(VMEM, SMEM, VMEM),
        scratch_shapes=[
            pltpu.VMEM((slots, W, W), jnp.float32),
            pltpu.SMEM((1, slots), jnp.int32),
            pltpu.SMEM((1, slots), jnp.int32),
            pltpu.SemaphoreType.DMA((slots // COPY_GROUP,)),
            pltpu.SemaphoreType.DMA((3,)),
        ],
        compiler_params=pltpu.CompilerParams(vmem_limit_bytes=32 * 1024 * 1024),
        cost_estimate=pl.CostEstimate(flops=4 * slots * W * W, bytes_accessed=8 * slots * W * W, transcendentals=0),
    )(live, *operands)


def weave(first, second):
    half = first.shape[0] // 2
    upper = lax.broadcasted_iota(jnp.int32, first.shape, 0) < half
    return (
        jnp.where(upper, first, pltpu.roll(second, half, 0)),
        jnp.where(upper, pltpu.roll(first, half, 0), second),
    )


def ladder_kernel(virts, codes, halves, *refs):
    blocks, (result, columns, totals) = refs[: virts * NEAR], refs[virts * NEAR :]
    far = blocks[0].shape[0]
    chunk_count = NEAR * far
    out_tiles = totals.shape[0] - 1
    rows = result.shape[1] // out_tiles
    total_rows = chunk_count * rows
    in_local = columns.shape[0] // virts
    totals[...] = jnp.zeros_like(totals)

    for owner in range(virts):
        for a in range(NEAR):
            sources = []
            for b in range(far):
                from_virt = owner ^ int((a > 0) != (b > 0))
                sources.append(blocks[from_virt * NEAR + (SWITCHED[a] if from_virt % 2 else a)])
            for b in range(0, far, 4):
                first_row = (a * far + b) * rows
                for tile in range(0, in_local, 2):
                    part = slice(tile * rows, (tile + 2) * rows)
                    four = [sources[b + at][b + at, part, :] for at in range(4)]
                    for at, pieces in enumerate(zip(weave(*four[:2]), weave(*four[2:]))):
                        high, low = split(jnp.concatenate(pieces, axis=0))
                        column = owner * in_local + tile + at
                        columns[column, first_row : first_row + 4 * rows, :] = high
                        columns[column, total_rows + first_row : total_rows + first_row + 4 * rows, :] = low

    def one_group(index, carry):
        first = index * GROUP
        products = []
        for step in range(GROUP):
            got = jnp.dot(columns[codes[0, first + step]], halves[first + step], preferred_element_type=jnp.float32)
            upper, lower = got[:total_rows], got[total_rows:]
            products.append((upper[:, :W] + lower[:, :W]) + (upper[:, W:] + lower[:, W:]))
        for step in range(GROUP):
            place = codes[1, first + step]
            totals[place] = totals[place] + products[step]
        return carry

    lax.fori_loop(0, (codes[2, 0] + GROUP - 1) // GROUP, one_group, 0)
    for chunk in range(0, chunk_count, 2):
        part = slice(chunk * rows, (chunk + 2) * rows)
        for tile in range(0, out_tiles, 2):
            pieces = weave(totals[tile, part, :], totals[tile + 1, part, :])
            for at, piece in enumerate(pieces):
                result[chunk + at, tile * rows : (tile + 2) * rows, :] = piece


def local_terms(codes, blocks, halves, rows, out_tiles):
    far, chunk_rows, _ = blocks[0].shape
    virts = len(blocks) // NEAR
    total_rows = NEAR * far * rows
    in_local = chunk_rows // rows

    def kernel(*refs):
        ladder_kernel(virts, *refs)

    return pl.pallas_call(
        kernel,
        out_shape=jax.ShapeDtypeStruct((NEAR * far, out_tiles * rows, W), jnp.float32),
        in_specs=[SMEM, VMEM] + [VMEM] * len(blocks),
        out_specs=VMEM,
        scratch_shapes=[
            pltpu.VMEM((virts * in_local, 2 * total_rows, W), jnp.bfloat16),
            pltpu.VMEM((out_tiles + 1, total_rows, W), jnp.float32),
        ],
        compiler_params=pltpu.CompilerParams(vmem_limit_bytes=32 * 1024 * 1024),
    )(pltpu.with_memory_space_constraint(codes, pltpu.SMEM), halves, *blocks)


def near_mask(step, a, b):
    return SWITCHED[step] if (a ^ a // 2 ^ b) % 2 else step


def swap(value, pairs, virts, virt_mask, step=0, far=0):
    routes = [
        (a * virts + b, (a ^ far * NEAR ^ near_mask(step, a, b)) * virts + (b ^ virt_mask))
        for a in range(pairs)
        for b in range(virts)
    ]
    return lax.ppermute(value, ("pair", "virt"), routes)


def far_order(far):
    return [*range(far - 2), far - 1, far - 2]


def swap_sum(parts, pairs, virts, which, marks):
    last = len(marks) - 1
    order = (0, last, *range(1, last))
    received = [swap(parts[marks.index(mark)], pairs, virts, 1, **{which: mark}) for mark in order]
    return sum(received[1:], received[0])


def shards(t2_amplitudes, integral_tiles, out_tiles, in_tiles, tile_counts):
    rows, columns = t2_amplitudes.shape
    local_tiles = columns // W
    slots = integral_tiles.shape[2]
    pairs, virts = lax.axis_size("pair"), lax.axis_size("virt")
    mine = t2_amplitudes.reshape(rows, local_tiles, W).transpose(1, 0, 2).reshape(local_tiles * rows, W)
    halves, codes, own = prepare(
        integral_tiles.reshape(slots, W, W),
        in_tiles.reshape(1, slots),
        out_tiles.reshape(1, slots),
        tile_counts,
        mine,
        local_tiles,
    )
    order = far_order(pairs // NEAR)
    line = jnp.stack([own] + [swap(mine, pairs, virts, 1, far=mask) for mask in order[1:]])
    pieces = [line] + [swap(line, pairs, virts, 1, step=step) for step in range(1, NEAR)]
    blocks = pieces + [swap(piece, pairs, virts, mask) for mask in range(1, virts) for piece in pieces]
    partial_sums = local_terms(codes, blocks, halves, rows, local_tiles)
    line_sums = swap_sum(partial_sums.reshape((NEAR, pairs // NEAR) + mine.shape), pairs, virts, "step", list(range(NEAR)))
    summed = swap_sum(line_sums, pairs, virts, "far", order)
    return summed.reshape(local_tiles, rows, W).transpose(1, 0, 2).reshape(rows, columns)


def solution(mesh):
    return jax.shard_map(
        shards,
        mesh=mesh,
        in_specs=(
            P("pair", "virt"),
            P("pair", "virt", None, None, None),
            P("pair", "virt", None),
            P("pair", "virt", None),
            P("pair", "virt"),
        ),
        out_specs=P("pair", "virt"),
        check_vma=False,
    )
```

```python
import jax
import jax.numpy as jnp
from jax import lax
from jax.experimental import pallas as pl
from jax.experimental.pallas import tpu as pltpu
from jax.sharding import PartitionSpec as P

W = 128
COPY_GROUP = 8
GROUP = 8
NEAR = 4
SWITCHED = (0, 2, 1, 3)
SMEM = pl.BlockSpec(memory_space=pltpu.SMEM)
VMEM = pl.BlockSpec(memory_space=pltpu.VMEM)


def split(value):
    high = value.astype(jnp.bfloat16)
    low = (value - high.astype(jnp.float32)).astype(jnp.bfloat16)
    return high, low


def tile_kernel(out_tiles, live, ins, outs, tiles, halves, codes, held, in_row, out_row, arrived, singles):
    indices = ((ins, in_row), (outs, out_row))
    others = [pltpu.make_async_copy(here, there, singles.at[at]) for at, (here, there) in enumerate(indices)]
    for copy in others:
        copy.start()
    count = live[0, 0]
    groups = (count + COPY_GROUP - 1) // COPY_GROUP

    def tile_copy(index):
        part = pl.ds(index * COPY_GROUP, COPY_GROUP)
        return pltpu.make_async_copy(tiles.at[part], held.at[part], arrived.at[index])

    def begin(index, carry):
        tile_copy(index).start()
        return carry

    lax.fori_loop(0, groups, begin, 0)
    for copy in others:
        copy.wait()
    for at in range(ins.shape[1]):
        for base in (0, 3):
            codes[base, at] = 0
            codes[base + 1, at] = 0
            codes[base + 2, at] = out_tiles
    me = lax.axis_index("virt")

    numbers = [jnp.int32(0), jnp.int32(0)]
    for slot in range(ins.shape[1]):
        tile_in, is_live = in_row[0, slot], slot < count
        owner = lax.bitwise_xor(lax.div(tile_in, out_tiles), me)
        is_own = owner == 0
        base = jnp.where(is_live, jnp.where(is_own, 0, 3), 6)
        at = jnp.where(is_own, numbers[0], numbers[1])
        codes[base, at] = slot
        codes[base + 1, at] = jnp.where(is_own, 0, owner - 1) * out_tiles + lax.rem(tile_in, out_tiles)
        codes[base + 2, at] = lax.rem(out_row[0, slot], out_tiles)
        numbers[0] += (is_live & is_own).astype(jnp.int32)
        numbers[1] += (is_live & (owner != 0)).astype(jnp.int32)
    codes[9, 0], codes[9, 1] = numbers

    def one_group(index, carry):
        tile_copy(index).wait()
        for step in range(COPY_GROUP):
            slot = index * COPY_GROUP + step
            high, low = split(held[slot])
            halves[slot, :, :W] = high
            halves[slot, :, W:] = low
        return carry

    lax.fori_loop(0, groups, one_group, 0)


def prepare(tiles, ins, outs, live, out_tiles):
    slots = tiles.shape[0]

    def kernel(*refs):
        tile_kernel(out_tiles, *refs)

    operands = [pltpu.with_memory_space_constraint(value, pltpu.HBM) for value in (ins, outs, tiles)]
    return pl.pallas_call(
        kernel,
        out_shape=(
            jax.ShapeDtypeStruct((slots, W, 2 * W), jnp.bfloat16),
            pltpu.SMEM((10, slots), jnp.int32),
        ),
        in_specs=[SMEM] + [pl.BlockSpec(memory_space=pltpu.HBM)] * 3,
        out_specs=(VMEM, SMEM),
        scratch_shapes=[
            pltpu.VMEM((slots, W, W), jnp.float32),
            pltpu.SMEM((1, slots), jnp.int32),
            pltpu.SMEM((1, slots), jnp.int32),
            pltpu.SemaphoreType.DMA((slots // COPY_GROUP,)),
            pltpu.SemaphoreType.DMA((2,)),
        ],
        compiler_params=pltpu.CompilerParams(vmem_limit_bytes=32 * 1024 * 1024),
        cost_estimate=pl.CostEstimate(flops=4 * slots * W * W, bytes_accessed=8 * slots * W * W, transcendentals=0),
    )(live, *operands)


def weave(first, second):
    half = first.shape[0] // 2
    upper = lax.broadcasted_iota(jnp.int32, first.shape, 0) < half
    return (
        jnp.where(upper, first, pltpu.roll(second, half, 0)),
        jnp.where(upper, pltpu.roll(first, half, 0), second),
    )


def fill_columns(columns, first_column, lines, rows):
    far, chunk_rows, _ = lines[0].shape
    total_rows = len(lines) * far * rows
    for a, line in enumerate(lines):
        for b in range(0, far, 4):
            first_row = (a * far + b) * rows
            for tile in range(0, chunk_rows // rows, 2):
                part = slice(tile * rows, (tile + 2) * rows)
                four = [line[b + at, part, :] for at in range(4)]
                for at, pieces in enumerate(zip(weave(*four[:2]), weave(*four[2:]))):
                    high, low = split(jnp.concatenate(pieces, axis=0))
                    column = first_column + tile + at
                    columns[column, first_row : first_row + 4 * rows, :] = high
                    columns[column, total_rows + first_row : total_rows + first_row + 4 * rows, :] = low


def add_products(which, codes, columns, halves, totals):
    total_rows = totals.shape[1]
    base = 3 * which

    def one_group(index, carry):
        first = index * GROUP
        products = []
        for step in range(GROUP):
            slot, column = codes[base, first + step], codes[base + 1, first + step]
            got = jnp.dot(columns[column], halves[slot], preferred_element_type=jnp.float32)
            upper, lower = got[:total_rows], got[total_rows:]
            products.append((upper[:, :W] + lower[:, :W]) + (upper[:, W:] + lower[:, W:]))
        for step in range(GROUP):
            place = codes[base + 2, first + step]
            totals[place] = totals[place] + products[step]
        return carry

    lax.fori_loop(0, (codes[9, which] + GROUP - 1) // GROUP, one_group, 0)


def own_kernel(rows, codes, halves, *refs):
    lines, (totals, columns) = refs[:NEAR], refs[NEAR:]
    totals[...] = jnp.zeros_like(totals)
    fill_columns(columns, 0, lines, rows)
    add_products(0, codes, columns, halves, totals)


def rest_kernel(rows, codes, halves, own_totals, *refs):
    lines, (result, columns, totals) = refs[:-3], refs[-3:]
    totals[...] = own_totals[...]
    in_local = lines[0].shape[1] // rows
    for owner in range(len(lines) // NEAR):
        fill_columns(columns, owner * in_local, lines[owner * NEAR : (owner + 1) * NEAR], rows)
    add_products(1, codes, columns, halves, totals)
    for chunk in range(0, result.shape[0], 2):
        part = slice(chunk * rows, (chunk + 2) * rows)
        for tile in range(0, result.shape[1] // rows, 2):
            pieces = weave(totals[tile, part, :], totals[tile + 1, part, :])
            for at, piece in enumerate(pieces):
                result[chunk + at, tile * rows : (tile + 2) * rows, :] = piece


def local_terms(codes, owners, halves, rows, out_tiles):
    far, chunk_rows, _ = owners[0][0].shape
    total_rows = NEAR * far * rows
    in_local = chunk_rows // rows
    totals = jax.ShapeDtypeStruct((out_tiles + 1, total_rows, W), jnp.float32)

    def columns(count):
        return pltpu.VMEM((count * in_local, 2 * total_rows, W), jnp.bfloat16)

    def own(*refs):
        own_kernel(rows, *refs)

    def rest(*refs):
        rest_kernel(rows, *refs)

    settings = dict(
        compiler_params=pltpu.CompilerParams(vmem_limit_bytes=32 * 1024 * 1024),
        cost_estimate=pl.CostEstimate(flops=1 << 28, bytes_accessed=1 << 21, transcendentals=0),
    )
    codes = pltpu.with_memory_space_constraint(codes, pltpu.SMEM)
    own_totals = pl.pallas_call(
        own,
        out_shape=totals,
        in_specs=[SMEM] + [VMEM] * (1 + NEAR),
        out_specs=VMEM,
        scratch_shapes=[columns(1)],
        **settings,
    )(codes, halves, *owners[0])
    others = [line for lines in owners[1:] for line in lines]
    return pl.pallas_call(
        rest,
        out_shape=jax.ShapeDtypeStruct((NEAR * far, out_tiles * rows, W), jnp.float32),
        in_specs=[SMEM] + [VMEM] * (2 + len(others)),
        out_specs=VMEM,
        scratch_shapes=[columns(len(owners) - 1), pltpu.VMEM(totals.shape, totals.dtype)],
        **settings,
    )(codes, halves, own_totals, *others)


def near_mask(step, a, b):
    return SWITCHED[step] if (a ^ a // 2 ^ b) % 2 else step


def swap(value, pairs, virts, virt_mask, step=0, far=0):
    routes = [
        (a * virts + b, (a ^ far * NEAR ^ near_mask(step, a, b)) * virts + (b ^ virt_mask))
        for a in range(pairs)
        for b in range(virts)
    ]
    return lax.ppermute(value, ("pair", "virt"), routes)


def far_order(far):
    return [*range(far - 2), far - 1, far - 2]


def swap_sum(parts, pairs, virts, which, marks):
    last = len(marks) - 1
    order = (0, last, *range(1, last))
    received = [swap(parts[marks.index(mark)], pairs, virts, 1, **{which: mark}) for mark in order]
    return sum(received[1:], received[0])


def shards(t2_amplitudes, integral_tiles, out_tiles, in_tiles, tile_counts):
    rows, columns = t2_amplitudes.shape
    local_tiles = columns // W
    slots = integral_tiles.shape[2]
    pairs, virts = lax.axis_size("pair"), lax.axis_size("virt")
    mine = t2_amplitudes.reshape(rows, local_tiles, W).transpose(1, 0, 2).reshape(local_tiles * rows, W)
    neighbour = swap(mine, pairs, virts, 1)
    halves, codes = prepare(
        integral_tiles.reshape(slots, W, W),
        in_tiles.reshape(1, slots),
        out_tiles.reshape(1, slots),
        tile_counts,
        local_tiles,
    )
    neighbour, halves = lax.optimization_barrier((neighbour, halves))
    order = far_order(pairs // NEAR)
    line = jnp.stack([neighbour] + [swap(mine, pairs, virts, 1, far=mask) for mask in order[1:]])
    pieces = [line] + [swap(line, pairs, virts, 1, step=step) for step in range(1, NEAR)]
    blocks = [pieces] + [[swap(piece, pairs, virts, mask) for piece in pieces] for mask in range(1, virts)]
    owners = [
        [blocks[mask ^ 1][0]] + [blocks[mask][SWITCHED[a] if mask % 2 else a] for a in range(1, NEAR)]
        for mask in range(virts)
    ]
    partial_sums = local_terms(codes, owners, halves, rows, local_tiles)
    line_sums = swap_sum(partial_sums.reshape((NEAR, pairs // NEAR) + mine.shape), pairs, virts, "step", list(range(NEAR)))
    summed = swap_sum(line_sums, pairs, virts, "far", order)
    return summed.reshape(local_tiles, rows, W).transpose(1, 0, 2).reshape(rows, columns)


def solution(mesh):
    return jax.shard_map(
        shards,
        mesh=mesh,
        in_specs=(
            P("pair", "virt"),
            P("pair", "virt", None, None, None),
            P("pair", "virt", None),
            P("pair", "virt", None),
            P("pair", "virt"),
        ),
        out_specs=P("pair", "virt"),
        check_vma=False,
    )
```

```python
import jax
import jax.numpy as jnp
from jax import lax
from jax.experimental import pallas as pl
from jax.experimental.pallas import tpu as pltpu
from jax.sharding import PartitionSpec as P

W = 128
COPY_GROUP = 8
GROUP = 8
NEAR = 4
SWITCHED = (0, 2, 1, 3)
SMEM = pl.BlockSpec(memory_space=pltpu.SMEM)
VMEM = pl.BlockSpec(memory_space=pltpu.VMEM)


def split(value):
    high = value.astype(jnp.bfloat16)
    low = (value - high.astype(jnp.float32)).astype(jnp.bfloat16)
    return high, low


def tile_kernel(out_tiles, live, ins, outs, tiles, halves, codes, held, in_row, out_row, arrived, singles):
    indices = ((ins, in_row), (outs, out_row))
    others = [pltpu.make_async_copy(here, there, singles.at[at]) for at, (here, there) in enumerate(indices)]
    for copy in others:
        copy.start()
    count = live[0, 0]
    groups = (count + COPY_GROUP - 1) // COPY_GROUP

    def tile_copy(index):
        part = pl.ds(index * COPY_GROUP, COPY_GROUP)
        return pltpu.make_async_copy(tiles.at[part], held.at[part], arrived.at[index])

    def begin(index, carry):
        tile_copy(index).start()
        return carry

    lax.fori_loop(0, groups, begin, 0)
    for copy in others:
        copy.wait()
    for at in range(ins.shape[1]):
        for base in (0, 3):
            codes[base, at] = 0
            codes[base + 1, at] = 0
            codes[base + 2, at] = out_tiles
    me = lax.axis_index("virt")

    numbers = [jnp.int32(0), jnp.int32(0)]
    for slot in range(ins.shape[1]):
        tile_in, is_live = in_row[0, slot], slot < count
        owner = lax.bitwise_xor(lax.div(tile_in, out_tiles), me)
        is_own = owner == 0
        base = jnp.where(is_live, jnp.where(is_own, 0, 3), 6)
        at = jnp.where(is_own, numbers[0], numbers[1])
        codes[base, at] = slot
        codes[base + 1, at] = jnp.where(is_own, 0, owner - 1) * out_tiles + lax.rem(tile_in, out_tiles)
        codes[base + 2, at] = lax.rem(out_row[0, slot], out_tiles)
        numbers[0] += (is_live & is_own).astype(jnp.int32)
        numbers[1] += (is_live & (owner != 0)).astype(jnp.int32)
    codes[9, 0], codes[9, 1] = numbers

    def one_group(index, carry):
        tile_copy(index).wait()
        for step in range(COPY_GROUP):
            slot = index * COPY_GROUP + step
            high, low = split(held[slot])
            halves[slot, :, :W] = high
            halves[slot, :, W:] = low
        return carry

    lax.fori_loop(0, groups, one_group, 0)


def prepare(tiles, ins, outs, live, out_tiles):
    slots = tiles.shape[0]

    def kernel(*refs):
        tile_kernel(out_tiles, *refs)

    operands = [pltpu.with_memory_space_constraint(value, pltpu.HBM) for value in (ins, outs, tiles)]
    return pl.pallas_call(
        kernel,
        out_shape=(
            jax.ShapeDtypeStruct((slots, W, 2 * W), jnp.bfloat16),
            pltpu.SMEM((10, slots), jnp.int32),
        ),
        in_specs=[SMEM] + [pl.BlockSpec(memory_space=pltpu.HBM)] * 3,
        out_specs=(VMEM, SMEM),
        scratch_shapes=[
            pltpu.VMEM((slots, W, W), jnp.float32),
            pltpu.SMEM((1, slots), jnp.int32),
            pltpu.SMEM((1, slots), jnp.int32),
            pltpu.SemaphoreType.DMA((slots // COPY_GROUP,)),
            pltpu.SemaphoreType.DMA((2,)),
        ],
        compiler_params=pltpu.CompilerParams(vmem_limit_bytes=32 * 1024 * 1024),
        cost_estimate=pl.CostEstimate(flops=4 * slots * W * W, bytes_accessed=8 * slots * W * W, transcendentals=0),
    )(live, *operands)


def weave(first, second):
    half = first.shape[0] // 2
    upper = lax.broadcasted_iota(jnp.int32, first.shape, 0) < half
    return (
        jnp.where(upper, first, pltpu.roll(second, half, 0)),
        jnp.where(upper, pltpu.roll(first, half, 0), second),
    )


def fill_columns(columns, first_column, lines, rows):
    far, chunk_rows, _ = lines[0].shape
    total_rows = len(lines) * far * rows
    for a, line in enumerate(lines):
        for b in range(0, far, 4):
            first_row = (a * far + b) * rows
            for tile in range(0, chunk_rows // rows, 2):
                part = slice(tile * rows, (tile + 2) * rows)
                four = [line[b + at, part, :] for at in range(4)]
                for at, pieces in enumerate(zip(weave(*four[:2]), weave(*four[2:]))):
                    high, low = split(jnp.concatenate(pieces, axis=0))
                    column = first_column + tile + at
                    columns[column, first_row : first_row + 4 * rows, :] = high
                    columns[column, total_rows + first_row : total_rows + first_row + 4 * rows, :] = low


def add_products(which, codes, columns, halves, totals):
    total_rows = totals.shape[1]
    base = 3 * which

    def one_group(index, carry):
        first = index * GROUP
        products = []
        for step in range(GROUP):
            slot, column = codes[base, first + step], codes[base + 1, first + step]
            got = jnp.dot(columns[column], halves[slot], preferred_element_type=jnp.float32)
            upper, lower = got[:total_rows], got[total_rows:]
            products.append((upper[:, :W] + lower[:, :W]) + (upper[:, W:] + lower[:, W:]))
        for step in range(GROUP):
            place = codes[base + 2, first + step]
            totals[place] = totals[place] + products[step]
        return carry

    lax.fori_loop(0, (codes[9, which] + GROUP - 1) // GROUP, one_group, 0)


def own_kernel(rows, codes, halves, *refs):
    lines, (totals, columns) = refs[:NEAR], refs[NEAR:]
    totals[...] = jnp.zeros_like(totals)
    fill_columns(columns, 0, lines, rows)
    add_products(0, codes, columns, halves, totals)


def rest_kernel(rows, codes, halves, own_totals, *refs):
    lines, (result, columns, totals) = refs[:-3], refs[-3:]
    totals[...] = own_totals[...]
    in_local = lines[0].shape[1] // rows
    for owner in range(len(lines) // NEAR):
        fill_columns(columns, owner * in_local, lines[owner * NEAR : (owner + 1) * NEAR], rows)
    add_products(1, codes, columns, halves, totals)
    for chunk in range(0, result.shape[0], 2):
        part = slice(chunk * rows, (chunk + 2) * rows)
        for tile in range(0, result.shape[1] // rows, 2):
            pieces = weave(totals[tile, part, :], totals[tile + 1, part, :])
            for at, piece in enumerate(pieces):
                result[chunk + at, tile * rows : (tile + 2) * rows, :] = piece


def local_terms(codes, owners, halves, rows, out_tiles):
    far, chunk_rows, _ = owners[0][0].shape
    total_rows = NEAR * far * rows
    in_local = chunk_rows // rows
    totals = jax.ShapeDtypeStruct((out_tiles + 1, total_rows, W), jnp.float32)

    def columns(count):
        return pltpu.VMEM((count * in_local, 2 * total_rows, W), jnp.bfloat16)

    def own(*refs):
        own_kernel(rows, *refs)

    def rest(*refs):
        rest_kernel(rows, *refs)

    settings = dict(
        compiler_params=pltpu.CompilerParams(vmem_limit_bytes=32 * 1024 * 1024),
        cost_estimate=pl.CostEstimate(flops=1 << 28, bytes_accessed=1 << 21, transcendentals=0),
    )
    codes = pltpu.with_memory_space_constraint(codes, pltpu.SMEM)
    own_totals = pl.pallas_call(
        own,
        out_shape=totals,
        in_specs=[SMEM] + [VMEM] * (1 + NEAR),
        out_specs=VMEM,
        scratch_shapes=[columns(1)],
        **settings,
    )(codes, halves, *owners[0])
    others = [line for lines in owners[1:] for line in lines]
    return pl.pallas_call(
        rest,
        out_shape=jax.ShapeDtypeStruct((NEAR * far, out_tiles * rows, W), jnp.float32),
        in_specs=[SMEM] + [VMEM] * (2 + len(others)),
        out_specs=VMEM,
        scratch_shapes=[columns(len(owners) - 1), pltpu.VMEM(totals.shape, totals.dtype)],
        **settings,
    )(codes, halves, own_totals, *others)


def near_mask(step, a, b):
    return SWITCHED[step] if (a ^ a // 2 ^ b) % 2 else step


def swap(value, pairs, virts, virt_mask, step=0, far=0):
    routes = [
        (a * virts + b, (a ^ far * NEAR ^ near_mask(step, a, b)) * virts + (b ^ virt_mask))
        for a in range(pairs)
        for b in range(virts)
    ]
    return lax.ppermute(value, ("pair", "virt"), routes)


def far_order(far):
    return [*range(far - 2), far - 1, far - 2]


def swap_parts(parts, pairs, virts, which, marks):
    last = len(marks) - 1
    order = (0, last, *range(1, last))
    return [swap(parts[marks.index(mark)], pairs, virts, 1, **{which: mark}) for mark in order]


def sum_kernel(*refs):
    parts, (result, total, copied) = refs[:-3], refs[-3:]
    total[...] = sum((part[...] for part in parts[1:]), parts[0][...])
    copy = pltpu.make_async_copy(total, result, copied)
    copy.start()
    copy.wait()


def last_sum(parts):
    shape, dtype = parts[0].shape, parts[0].dtype
    return pl.pallas_call(
        sum_kernel,
        out_shape=jax.ShapeDtypeStruct(shape, dtype),
        in_specs=[VMEM] * len(parts),
        out_specs=pl.BlockSpec(memory_space=pltpu.HBM),
        scratch_shapes=[pltpu.VMEM(shape, dtype), pltpu.SemaphoreType.DMA],
    )(*parts)


def shards(t2_amplitudes, integral_tiles, out_tiles, in_tiles, tile_counts):
    rows, columns = t2_amplitudes.shape
    local_tiles = columns // W
    slots = integral_tiles.shape[2]
    pairs, virts = lax.axis_size("pair"), lax.axis_size("virt")
    mine = t2_amplitudes.reshape(rows, local_tiles, W).transpose(1, 0, 2).reshape(local_tiles * rows, W)
    neighbour = swap(mine, pairs, virts, 1)
    halves, codes = prepare(
        integral_tiles.reshape(slots, W, W),
        in_tiles.reshape(1, slots),
        out_tiles.reshape(1, slots),
        tile_counts,
        local_tiles,
    )
    neighbour, halves = lax.optimization_barrier((neighbour, halves))
    order = far_order(pairs // NEAR)
    line = jnp.stack([neighbour] + [swap(mine, pairs, virts, 1, far=mask) for mask in order[1:]])
    pieces = [line] + [swap(line, pairs, virts, 1, step=step) for step in range(1, NEAR)]
    blocks = [pieces] + [[swap(piece, pairs, virts, mask) for piece in pieces] for mask in range(1, virts)]
    owners = [
        [blocks[mask ^ 1][0]] + [blocks[mask][SWITCHED[a] if mask % 2 else a] for a in range(1, NEAR)]
        for mask in range(virts)
    ]
    partial_sums = local_terms(codes, owners, halves, rows, local_tiles)
    parts = partial_sums.reshape((NEAR, pairs // NEAR) + mine.shape)
    line_parts = swap_parts(parts, pairs, virts, "step", list(range(NEAR)))
    line_sums = sum(line_parts[1:], line_parts[0])
    summed = last_sum(swap_parts(line_sums, pairs, virts, "far", order))
    return summed.reshape(local_tiles, rows, W).transpose(1, 0, 2).reshape(rows, columns)


def solution(mesh):
    return jax.shard_map(
        shards,
        mesh=mesh,
        in_specs=(
            P("pair", "virt"),
            P("pair", "virt", None, None, None),
            P("pair", "virt", None),
            P("pair", "virt", None),
            P("pair", "virt"),
        ),
        out_specs=P("pair", "virt"),
        check_vma=False,
    )
```

```python
import jax
import jax.numpy as jnp
from jax import lax
from jax.experimental import pallas as pl
from jax.experimental.pallas import tpu as pltpu
from jax.sharding import PartitionSpec as P

W = 128
COPY_GROUP = 8
GROUP = 8
NEAR = 4
SWITCHED = (0, 2, 1, 3)
SMEM = pl.BlockSpec(memory_space=pltpu.SMEM)
VMEM = pl.BlockSpec(memory_space=pltpu.VMEM)


def split(value):
    high = value.astype(jnp.bfloat16)
    low = (value - high.astype(jnp.float32)).astype(jnp.bfloat16)
    return high, low


def tile_kernel(out_tiles, live, ins, outs, tiles, halves, codes, held, in_row, out_row, arrived, singles):
    indices = ((ins, in_row), (outs, out_row))
    others = [pltpu.make_async_copy(here, there, singles.at[at]) for at, (here, there) in enumerate(indices)]
    for copy in others:
        copy.start()
    count = live[0, 0]
    groups = (count + COPY_GROUP - 1) // COPY_GROUP

    def tile_copy(index):
        part = pl.ds(index * COPY_GROUP, COPY_GROUP)
        return pltpu.make_async_copy(tiles.at[part], held.at[part], arrived.at[index])

    def begin(index, carry):
        tile_copy(index).start()
        return carry

    lax.fori_loop(0, groups, begin, 0)
    for copy in others:
        copy.wait()
    for at in range(ins.shape[1]):
        for base in (0, 3):
            codes[base, at] = 0
            codes[base + 1, at] = 0
            codes[base + 2, at] = out_tiles
    me = lax.axis_index("virt")

    numbers = [jnp.int32(0), jnp.int32(0)]
    for slot in range(ins.shape[1]):
        tile_in, is_live = in_row[0, slot], slot < count
        owner = lax.bitwise_xor(lax.div(tile_in, out_tiles), me)
        is_own = owner == 0
        base = jnp.where(is_live, jnp.where(is_own, 0, 3), 6)
        at = jnp.where(is_own, numbers[0], numbers[1])
        codes[base, at] = slot
        codes[base + 1, at] = jnp.where(is_own, 0, owner - 1) * out_tiles + lax.rem(tile_in, out_tiles)
        codes[base + 2, at] = lax.rem(out_row[0, slot], out_tiles)
        numbers[0] += (is_live & is_own).astype(jnp.int32)
        numbers[1] += (is_live & (owner != 0)).astype(jnp.int32)
    codes[9, 0], codes[9, 1] = numbers

    def one_group(index, carry):
        tile_copy(index).wait()
        for step in range(COPY_GROUP):
            slot = index * COPY_GROUP + step
            high, low = split(held[slot])
            halves[slot, :, :W] = high
            halves[slot, :, W:] = low
        return carry

    lax.fori_loop(0, groups, one_group, 0)


def prepare(tiles, ins, outs, live, out_tiles):
    slots = tiles.shape[0]

    def kernel(*refs):
        tile_kernel(out_tiles, *refs)

    operands = [pltpu.with_memory_space_constraint(value, pltpu.HBM) for value in (ins, outs, tiles)]
    return pl.pallas_call(
        kernel,
        out_shape=(
            jax.ShapeDtypeStruct((slots, W, 2 * W), jnp.bfloat16),
            pltpu.SMEM((10, slots), jnp.int32),
        ),
        in_specs=[SMEM] + [pl.BlockSpec(memory_space=pltpu.HBM)] * 3,
        out_specs=(VMEM, SMEM),
        scratch_shapes=[
            pltpu.VMEM((slots, W, W), jnp.float32),
            pltpu.SMEM((1, slots), jnp.int32),
            pltpu.SMEM((1, slots), jnp.int32),
            pltpu.SemaphoreType.DMA((slots // COPY_GROUP,)),
            pltpu.SemaphoreType.DMA((2,)),
        ],
        compiler_params=pltpu.CompilerParams(vmem_limit_bytes=32 * 1024 * 1024),
        cost_estimate=pl.CostEstimate(flops=4 * slots * W * W, bytes_accessed=8 * slots * W * W, transcendentals=0),
    )(live, *operands)


def weave(first, second):
    half = first.shape[0] // 2
    upper = lax.broadcasted_iota(jnp.int32, first.shape, 0) < half
    return (
        jnp.where(upper, first, pltpu.roll(second, half, 0)),
        jnp.where(upper, pltpu.roll(first, half, 0), second),
    )


def fill_columns(columns, first_column, lines, rows):
    far, chunk_rows, _ = lines[0].shape
    total_rows = len(lines) * far * rows
    for a, line in enumerate(lines):
        for b in range(0, far, 4):
            first_row = (a * far + b) * rows
            for tile in range(0, chunk_rows // rows, 2):
                part = slice(tile * rows, (tile + 2) * rows)
                four = [line[b + at, part, :] for at in range(4)]
                for at, pieces in enumerate(zip(weave(*four[:2]), weave(*four[2:]))):
                    high, low = split(jnp.concatenate(pieces, axis=0))
                    column = first_column + tile + at
                    columns[column, first_row : first_row + 4 * rows, :] = high
                    columns[column, total_rows + first_row : total_rows + first_row + 4 * rows, :] = low


def add_products(which, codes, columns, halves, totals):
    total_rows = totals.shape[1]
    base = 3 * which

    def one_group(index, carry):
        first = index * GROUP
        products = []
        for step in range(GROUP):
            slot, column = codes[base, first + step], codes[base + 1, first + step]
            got = jnp.dot(columns[column], halves[slot], preferred_element_type=jnp.float32)
            upper, lower = got[:total_rows], got[total_rows:]
            products.append((upper[:, :W] + lower[:, :W]) + (upper[:, W:] + lower[:, W:]))
        for step in range(GROUP):
            place = codes[base + 2, first + step]
            totals[place] = totals[place] + products[step]
        return carry

    lax.fori_loop(0, (codes[9, which] + GROUP - 1) // GROUP, one_group, 0)


def own_kernel(rows, codes, halves, *refs):
    lines, (totals, columns) = refs[:NEAR], refs[NEAR:]
    totals[...] = jnp.zeros_like(totals)
    fill_columns(columns, 0, lines, rows)
    add_products(0, codes, columns, halves, totals)


def rest_kernel(rows, codes, halves, own_totals, *refs):
    lines, (result, columns, totals) = refs[:-3], refs[-3:]
    totals[...] = own_totals[...]
    in_local = lines[0].shape[1] // rows
    for owner in range(len(lines) // NEAR):
        fill_columns(columns, owner * in_local, lines[owner * NEAR : (owner + 1) * NEAR], rows)
    add_products(1, codes, columns, halves, totals)
    for chunk in range(0, result.shape[0], 2):
        part = slice(chunk * rows, (chunk + 2) * rows)
        for tile in range(0, result.shape[1] // rows, 2):
            pieces = weave(totals[tile, part, :], totals[tile + 1, part, :])
            for at, piece in enumerate(pieces):
                result[chunk + at, tile * rows : (tile + 2) * rows, :] = piece


def local_terms(codes, owners, halves, rows, out_tiles):
    far, chunk_rows, _ = owners[0][0].shape
    total_rows = NEAR * far * rows
    in_local = chunk_rows // rows
    totals = jax.ShapeDtypeStruct((out_tiles + 1, total_rows, W), jnp.float32)

    def columns(count):
        return pltpu.VMEM((count * in_local, 2 * total_rows, W), jnp.bfloat16)

    def own(*refs):
        own_kernel(rows, *refs)

    def rest(*refs):
        rest_kernel(rows, *refs)

    settings = dict(
        compiler_params=pltpu.CompilerParams(vmem_limit_bytes=32 * 1024 * 1024),
        cost_estimate=pl.CostEstimate(flops=1 << 28, bytes_accessed=1 << 21, transcendentals=0),
    )
    codes = pltpu.with_memory_space_constraint(codes, pltpu.SMEM)
    own_totals = pl.pallas_call(
        own,
        out_shape=totals,
        in_specs=[SMEM] + [VMEM] * (1 + NEAR),
        out_specs=VMEM,
        scratch_shapes=[columns(1)],
        **settings,
    )(codes, halves, *owners[0])
    others = [line for lines in owners[1:] for line in lines]
    return pl.pallas_call(
        rest,
        out_shape=jax.ShapeDtypeStruct((NEAR * far, out_tiles * rows, W), jnp.float32),
        in_specs=[SMEM] + [VMEM] * (2 + len(others)),
        out_specs=VMEM,
        scratch_shapes=[columns(len(owners) - 1), pltpu.VMEM(totals.shape, totals.dtype)],
        **settings,
    )(codes, halves, own_totals, *others)


def near_mask(step, a, b):
    return SWITCHED[step] if (a ^ a // 2 ^ b) % 2 else step


def swap(value, pairs, virts, virt_mask, step=0, far=0):
    routes = [
        (a * virts + b, (a ^ far * NEAR ^ near_mask(step, a, b)) * virts + (b ^ virt_mask))
        for a in range(pairs)
        for b in range(virts)
    ]
    return lax.ppermute(value, ("pair", "virt"), routes)


def far_order(far):
    return [*range(far - 2), far - 1, far - 2]


def swap_parts(parts, pairs, virts, which, marks, order):
    return [swap(parts[marks.index(mark)], pairs, virts, 1, **{which: mark}) for mark in order]


def sum_kernel(*refs):
    parts, (result, total, copied) = refs[:-3], refs[-3:]
    total[...] = sum((part[...] for part in parts[1:]), parts[0][...])
    copy = pltpu.make_async_copy(total, result, copied)
    copy.start()
    copy.wait()


def last_sum(parts):
    shape, dtype = parts[0].shape, parts[0].dtype
    return pl.pallas_call(
        sum_kernel,
        out_shape=jax.ShapeDtypeStruct(shape, dtype),
        in_specs=[VMEM] * len(parts),
        out_specs=pl.BlockSpec(memory_space=pltpu.HBM),
        scratch_shapes=[pltpu.VMEM(shape, dtype), pltpu.SemaphoreType.DMA],
        compiler_params=pltpu.CompilerParams(vmem_limit_bytes=2 * 1024 * 1024),
    )(*parts)


def shards(t2_amplitudes, integral_tiles, out_tiles, in_tiles, tile_counts):
    rows, columns = t2_amplitudes.shape
    local_tiles = columns // W
    slots = integral_tiles.shape[2]
    pairs, virts = lax.axis_size("pair"), lax.axis_size("virt")
    mine = t2_amplitudes.reshape(rows, local_tiles, W).transpose(1, 0, 2).reshape(local_tiles * rows, W)
    neighbour = swap(mine, pairs, virts, 1)
    halves, codes = prepare(
        integral_tiles.reshape(slots, W, W),
        in_tiles.reshape(1, slots),
        out_tiles.reshape(1, slots),
        tile_counts,
        local_tiles,
    )
    neighbour, halves = lax.optimization_barrier((neighbour, halves))
    order = far_order(pairs // NEAR)
    line = jnp.stack([neighbour] + [swap(mine, pairs, virts, 1, far=mask) for mask in order[1:]])
    pieces = [line] + [swap(line, pairs, virts, 1, step=step) for step in range(1, NEAR)]
    blocks = [pieces] + [[swap(piece, pairs, virts, mask) for piece in pieces] for mask in range(1, virts)]
    owners = [
        [blocks[mask ^ 1][0]] + [blocks[mask][SWITCHED[a] if mask % 2 else a] for a in range(1, NEAR)]
        for mask in range(virts)
    ]
    partial_sums = local_terms(codes, owners, halves, rows, local_tiles)
    parts = partial_sums.reshape((NEAR, pairs // NEAR) + mine.shape)
    steps = list(range(NEAR))
    line_parts = swap_parts(parts, pairs, virts, "step", steps, (0, 3, 1, 2))
    line_sums = sum(line_parts[1:], line_parts[0])
    summed = last_sum(swap_parts(line_sums, pairs, virts, "far", order, range(len(order))))
    return summed.reshape(local_tiles, rows, W).transpose(1, 0, 2).reshape(rows, columns)


def solution(mesh):
    return jax.shard_map(
        shards,
        mesh=mesh,
        in_specs=(
            P("pair", "virt"),
            P("pair", "virt", None, None, None),
            P("pair", "virt", None),
            P("pair", "virt", None),
            P("pair", "virt"),
        ),
        out_specs=P("pair", "virt"),
        check_vma=False,
    )
```

```python
import jax
import jax.numpy as jnp
from jax import lax
from jax.experimental import pallas as pl
from jax.experimental.pallas import tpu as pltpu
from jax.sharding import PartitionSpec as P

W = 128
COPY_GROUP = 8
GROUP = 8
NEAR = 4
SWITCHED = (0, 2, 1, 3)
SMEM = pl.BlockSpec(memory_space=pltpu.SMEM)
VMEM = pl.BlockSpec(memory_space=pltpu.VMEM)


def split(value):
    high = value.astype(jnp.bfloat16)
    low = (value - high.astype(jnp.float32)).astype(jnp.bfloat16)
    return high, low


def tile_kernel(out_tiles, live, ins, outs, tiles, halves, codes, held, in_row, out_row, arrived, singles):
    indices = ((ins, in_row), (outs, out_row))
    others = [pltpu.make_async_copy(here, there, singles.at[at]) for at, (here, there) in enumerate(indices)]
    for copy in others:
        copy.start()
    count = live[0, 0]
    groups = (count + COPY_GROUP - 1) // COPY_GROUP

    def tile_copy(index):
        part = pl.ds(index * COPY_GROUP, COPY_GROUP)
        return pltpu.make_async_copy(tiles.at[part], held.at[part], arrived.at[index])

    def begin(index, carry):
        tile_copy(index).start()
        return carry

    lax.fori_loop(0, groups, begin, 0)
    for copy in others:
        copy.wait()
    for at in range(ins.shape[1]):
        for base in (0, 3):
            codes[base, at] = 0
            codes[base + 1, at] = 0
            codes[base + 2, at] = out_tiles
    me = lax.axis_index("virt")

    numbers = [jnp.int32(0), jnp.int32(0)]
    for slot in range(ins.shape[1]):
        tile_in, is_live = in_row[0, slot], slot < count
        owner = lax.bitwise_xor(lax.div(tile_in, out_tiles), me)
        is_own = owner == 0
        base = jnp.where(is_live, jnp.where(is_own, 0, 3), 6)
        at = jnp.where(is_own, numbers[0], numbers[1])
        codes[base, at] = slot
        codes[base + 1, at] = jnp.where(is_own, 0, owner - 1) * out_tiles + lax.rem(tile_in, out_tiles)
        codes[base + 2, at] = lax.rem(out_row[0, slot], out_tiles)
        numbers[0] += (is_live & is_own).astype(jnp.int32)
        numbers[1] += (is_live & (owner != 0)).astype(jnp.int32)
    codes[9, 0], codes[9, 1] = numbers

    def one_group(index, carry):
        tile_copy(index).wait()
        for step in range(COPY_GROUP):
            slot = index * COPY_GROUP + step
            high, low = split(held[slot])
            halves[slot, :, :W] = high
            halves[slot, :, W:] = low
        return carry

    lax.fori_loop(0, groups, one_group, 0)


def prepare(tiles, ins, outs, live, out_tiles):
    slots = tiles.shape[0]

    def kernel(*refs):
        tile_kernel(out_tiles, *refs)

    operands = [pltpu.with_memory_space_constraint(value, pltpu.HBM) for value in (ins, outs, tiles)]
    return pl.pallas_call(
        kernel,
        out_shape=(
            jax.ShapeDtypeStruct((slots, W, 2 * W), jnp.bfloat16),
            pltpu.SMEM((10, slots), jnp.int32),
        ),
        in_specs=[SMEM] + [pl.BlockSpec(memory_space=pltpu.HBM)] * 3,
        out_specs=(VMEM, SMEM),
        scratch_shapes=[
            pltpu.VMEM((slots, W, W), jnp.float32),
            pltpu.SMEM((1, slots), jnp.int32),
            pltpu.SMEM((1, slots), jnp.int32),
            pltpu.SemaphoreType.DMA((slots // COPY_GROUP,)),
            pltpu.SemaphoreType.DMA((2,)),
        ],
        compiler_params=pltpu.CompilerParams(vmem_limit_bytes=32 * 1024 * 1024),
        cost_estimate=pl.CostEstimate(flops=4 * slots * W * W, bytes_accessed=8 * slots * W * W, transcendentals=0),
    )(live, *operands)


def weave(first, second):
    half = first.shape[0] // 2
    upper = lax.broadcasted_iota(jnp.int32, first.shape, 0) < half
    return (
        jnp.where(upper, first, pltpu.roll(second, half, 0)),
        jnp.where(upper, pltpu.roll(first, half, 0), second),
    )


def fill_columns(columns, first_column, lines, rows):
    far, chunk_rows, _ = lines[0].shape
    total_rows = len(lines) * far * rows
    for a, line in enumerate(lines):
        for b in range(0, far, 4):
            first_row = (a * far + b) * rows
            for tile in range(0, chunk_rows // rows, 2):
                part = slice(tile * rows, (tile + 2) * rows)
                four = [line[b + at, part, :] for at in range(4)]
                for at, pieces in enumerate(zip(weave(*four[:2]), weave(*four[2:]))):
                    high, low = split(jnp.concatenate(pieces, axis=0))
                    column = first_column + tile + at
                    columns[column, first_row : first_row + 4 * rows, :] = high
                    columns[column, total_rows + first_row : total_rows + first_row + 4 * rows, :] = low


def add_products(which, codes, columns, halves, totals):
    total_rows = totals.shape[1]
    base = 3 * which

    def one_group(index, carry):
        first = index * GROUP
        products = []
        for step in range(GROUP):
            slot, column = codes[base, first + step], codes[base + 1, first + step]
            got = jnp.dot(columns[column], halves[slot], preferred_element_type=jnp.float32)
            upper, lower = got[:total_rows], got[total_rows:]
            products.append((upper[:, :W] + lower[:, :W]) + (upper[:, W:] + lower[:, W:]))
        for step in range(GROUP):
            place = codes[base + 2, first + step]
            totals[place] = totals[place] + products[step]
        return carry

    lax.fori_loop(0, (codes[9, which] + GROUP - 1) // GROUP, one_group, 0)


def own_kernel(rows, codes, halves, *refs):
    lines, (totals, columns) = refs[:NEAR], refs[NEAR:]
    totals[...] = jnp.zeros_like(totals)
    fill_columns(columns, 0, lines, rows)
    add_products(0, codes, columns, halves, totals)


def rest_kernel(rows, codes, halves, own_totals, *refs):
    lines, (result, columns, totals) = refs[:-3], refs[-3:]
    totals[...] = own_totals[...]
    in_local = lines[0].shape[1] // rows
    for owner in range(len(lines) // NEAR):
        fill_columns(columns, owner * in_local, lines[owner * NEAR : (owner + 1) * NEAR], rows)
    add_products(1, codes, columns, halves, totals)
    for chunk in range(0, result.shape[0], 2):
        part = slice(chunk * rows, (chunk + 2) * rows)
        for tile in range(0, result.shape[1] // rows, 2):
            pieces = weave(totals[tile, part, :], totals[tile + 1, part, :])
            for at, piece in enumerate(pieces):
                result[chunk + at, tile * rows : (tile + 2) * rows, :] = piece


def local_terms(codes, owners, halves, rows, out_tiles):
    far, chunk_rows, _ = owners[0][0].shape
    total_rows = NEAR * far * rows
    in_local = chunk_rows // rows
    totals = jax.ShapeDtypeStruct((out_tiles + 1, total_rows, W), jnp.float32)

    def columns(count):
        return pltpu.VMEM((count * in_local, 2 * total_rows, W), jnp.bfloat16)

    def own(*refs):
        own_kernel(rows, *refs)

    def rest(*refs):
        rest_kernel(rows, *refs)

    settings = dict(
        compiler_params=pltpu.CompilerParams(vmem_limit_bytes=32 * 1024 * 1024),
        cost_estimate=pl.CostEstimate(flops=1 << 28, bytes_accessed=1 << 21, transcendentals=0),
    )
    codes = pltpu.with_memory_space_constraint(codes, pltpu.SMEM)
    own_totals = pl.pallas_call(
        own,
        out_shape=totals,
        in_specs=[SMEM] + [VMEM] * (1 + NEAR),
        out_specs=VMEM,
        scratch_shapes=[columns(1)],
        **settings,
    )(codes, halves, *owners[0])
    others = [line for lines in owners[1:] for line in lines]
    return pl.pallas_call(
        rest,
        out_shape=jax.ShapeDtypeStruct((NEAR * far, out_tiles * rows, W), jnp.float32),
        in_specs=[SMEM] + [VMEM] * (2 + len(others)),
        out_specs=VMEM,
        scratch_shapes=[columns(len(owners) - 1), pltpu.VMEM(totals.shape, totals.dtype)],
        **settings,
    )(codes, halves, own_totals, *others)


def near_mask(step, a, b):
    return SWITCHED[step] if (a ^ a // 2 ^ b) % 2 else step


def swap(value, pairs, virts, virt_mask, step=0, far=0):
    routes = [
        (a * virts + b, (a ^ far * NEAR ^ near_mask(step, a, b)) * virts + (b ^ virt_mask))
        for a in range(pairs)
        for b in range(virts)
    ]
    return lax.ppermute(value, ("pair", "virt"), routes)


def far_order(far):
    return [*range(far - 2), far - 1, far - 2]


def swap_sum(parts, pairs, virts, which, marks):
    last = len(marks) - 1
    order = (0, last, *range(1, last))
    received = [swap(parts[marks.index(mark)], pairs, virts, 1, **{which: mark}) for mark in order]
    return sum(received[1:], received[0])


def shards(t2_amplitudes, integral_tiles, out_tiles, in_tiles, tile_counts):
    rows, columns = t2_amplitudes.shape
    local_tiles = columns // W
    slots = integral_tiles.shape[2]
    pairs, virts = lax.axis_size("pair"), lax.axis_size("virt")
    mine = t2_amplitudes.reshape(rows, local_tiles, W).transpose(1, 0, 2).reshape(local_tiles * rows, W)
    neighbour = swap(mine, pairs, virts, 1)
    halves, codes = prepare(
        integral_tiles.reshape(slots, W, W),
        in_tiles.reshape(1, slots),
        out_tiles.reshape(1, slots),
        tile_counts,
        local_tiles,
    )
    order = far_order(pairs // NEAR)
    chunks = [neighbour] + [swap(mine, pairs, virts, 1, far=mask) for mask in order[1:]]
    chunks[-1], halves = lax.optimization_barrier((chunks[-1], halves))
    line = jnp.stack(chunks)
    pieces = [line] + [swap(line, pairs, virts, 1, step=step) for step in range(1, NEAR)]
    blocks = [pieces] + [[swap(piece, pairs, virts, mask) for piece in pieces] for mask in range(1, virts)]
    owners = [
        [blocks[mask ^ 1][0]] + [blocks[mask][SWITCHED[a] if mask % 2 else a] for a in range(1, NEAR)]
        for mask in range(virts)
    ]
    partial_sums = local_terms(codes, owners, halves, rows, local_tiles)
    line_sums = swap_sum(partial_sums.reshape((NEAR, pairs // NEAR) + mine.shape), pairs, virts, "step", list(range(NEAR)))
    summed = swap_sum(line_sums, pairs, virts, "far", order)
    return summed.reshape(local_tiles, rows, W).transpose(1, 0, 2).reshape(rows, columns)


def solution(mesh):
    return jax.shard_map(
        shards,
        mesh=mesh,
        in_specs=(
            P("pair", "virt"),
            P("pair", "virt", None, None, None),
            P("pair", "virt", None),
            P("pair", "virt", None),
            P("pair", "virt"),
        ),
        out_specs=P("pair", "virt"),
        check_vma=False,
    )
```

```python
import jax
import jax.numpy as jnp
from jax import lax
from jax.experimental import pallas as pl
from jax.experimental.pallas import tpu as pltpu
from jax.sharding import PartitionSpec as P

W = 128
COPY_GROUP = 8
GROUP = 16
NEAR = 4
SWITCHED = (0, 2, 1, 3)
SMEM = pl.BlockSpec(memory_space=pltpu.SMEM)
VMEM = pl.BlockSpec(memory_space=pltpu.VMEM)


def split(value):
    high = value.astype(jnp.bfloat16)
    low = (value - high.astype(jnp.float32)).astype(jnp.bfloat16)
    return high, low


def tile_kernel(out_tiles, live, ins, outs, tiles, mine, halves, codes, own, held, in_row, out_row, arrived, singles):
    singles_of = ((ins, in_row), (outs, out_row), (mine, own))
    others = [pltpu.make_async_copy(here, there, singles.at[at]) for at, (here, there) in enumerate(singles_of)]
    for copy in others:
        copy.start()
    count = live[0, 0]
    groups = (count + COPY_GROUP - 1) // COPY_GROUP

    def tile_copy(index):
        part = pl.ds(index * COPY_GROUP, COPY_GROUP)
        return pltpu.make_async_copy(tiles.at[part], held.at[part], arrived.at[index])

    def begin(index, carry):
        tile_copy(index).start()
        return carry

    lax.fori_loop(0, groups, begin, 0)
    for copy in others:
        copy.wait()
    me = lax.axis_index("virt")
    codes[2, 0] = count
    for slot in range(ins.shape[1]):
        tile_in = in_row[0, slot]
        owner = lax.bitwise_xor(lax.div(tile_in, out_tiles), me)
        codes[0, slot] = owner * out_tiles + lax.rem(tile_in, out_tiles)
        codes[1, slot] = jnp.where(slot < count, lax.rem(out_row[0, slot], out_tiles), out_tiles)

    def one_group(index, carry):
        tile_copy(index).wait()
        for step in range(COPY_GROUP):
            slot = index * COPY_GROUP + step
            high, low = split(held[slot])
            halves[slot, :, :W] = high
            halves[slot, :, W:] = low
        return carry

    lax.fori_loop(0, groups, one_group, 0)


def prepare(tiles, ins, outs, live, mine, out_tiles):
    slots = tiles.shape[0]

    def kernel(*refs):
        tile_kernel(out_tiles, *refs)

    operands = [pltpu.with_memory_space_constraint(value, pltpu.HBM) for value in (ins, outs, tiles, mine)]
    return pl.pallas_call(
        kernel,
        out_shape=(
            jax.ShapeDtypeStruct((slots, W, 2 * W), jnp.bfloat16),
            pltpu.SMEM((3, slots), jnp.int32),
            jax.ShapeDtypeStruct(mine.shape, mine.dtype),
        ),
        in_specs=[SMEM] + [pl.BlockSpec(memory_space=pltpu.HBM)] * 4,
        out_specs=(VMEM, SMEM, VMEM),
        scratch_shapes=[
            pltpu.VMEM((slots, W, W), jnp.float32),
            pltpu.SMEM((1, slots), jnp.int32),
            pltpu.SMEM((1, slots), jnp.int32),
            pltpu.SemaphoreType.DMA((slots // COPY_GROUP,)),
            pltpu.SemaphoreType.DMA((3,)),
        ],
        compiler_params=pltpu.CompilerParams(vmem_limit_bytes=32 * 1024 * 1024),
        cost_estimate=pl.CostEstimate(flops=4 * slots * W * W, bytes_accessed=8 * slots * W * W, transcendentals=0),
    )(live, *operands)


def weave(first, second):
    half = first.shape[0] // 2
    upper = lax.broadcasted_iota(jnp.int32, first.shape, 0) < half
    return (
        jnp.where(upper, first, pltpu.roll(second, half, 0)),
        jnp.where(upper, pltpu.roll(first, half, 0), second),
    )


def ladder_kernel(quarters, virts, codes, halves, *refs):
    blocks, (result, columns, totals) = refs[:-3], refs[-3:]
    far, chunk_rows, _ = blocks[0].shape
    chunk_count = len(quarters) * far
    out_tiles = totals.shape[0] - 1
    rows = result.shape[1] // out_tiles
    total_rows = chunk_count * rows
    in_local = chunk_rows // rows
    totals[...] = jnp.zeros_like(totals)

    for owner in range(virts):
        for at_quarter, quarter in enumerate(quarters):
            crossed = [int((quarter > 0) != (b > 0)) for b in range(far)]
            sources = [blocks[at_quarter * virts + (owner ^ cross)] for cross in crossed]
            for b in range(0, far, 4):
                first_row = (at_quarter * far + b) * rows
                for tile in range(0, in_local, 2):
                    part = slice(tile * rows, (tile + 2) * rows)
                    four = [sources[b + at][b + at, part, :] for at in range(4)]
                    for at, pieces in enumerate(zip(weave(*four[:2]), weave(*four[2:]))):
                        high, low = split(jnp.concatenate(pieces, axis=0))
                        column = owner * in_local + tile + at
                        columns[column, first_row : first_row + 4 * rows, :] = high
                        columns[column, total_rows + first_row : total_rows + first_row + 4 * rows, :] = low

    def one_group(index, carry):
        first = index * GROUP
        products = []
        for step in range(GROUP):
            got = jnp.dot(columns[codes[0, first + step]], halves[first + step], preferred_element_type=jnp.float32)
            upper, lower = got[:total_rows], got[total_rows:]
            products.append((upper[:, :W] + lower[:, :W]) + (upper[:, W:] + lower[:, W:]))
        for step in range(GROUP):
            place = codes[1, first + step]
            totals[place] = totals[place] + products[step]
        return carry

    lax.fori_loop(0, (codes[2, 0] + GROUP - 1) // GROUP, one_group, 0)
    for chunk in range(0, chunk_count, 2):
        part = slice(chunk * rows, (chunk + 2) * rows)
        for tile in range(0, out_tiles, 2):
            pieces = weave(totals[tile, part, :], totals[tile + 1, part, :])
            for at, piece in enumerate(pieces):
                result[chunk + at, tile * rows : (tile + 2) * rows, :] = piece


def quarter_terms(codes, pieces, quarters, halves, rows, out_tiles):
    virts = len(pieces)
    blocks = [pieces[c][SWITCHED[a] if c % 2 else a] for a in quarters for c in range(virts)]
    far, chunk_rows, _ = blocks[0].shape
    total_rows = len(quarters) * far * rows
    in_local = chunk_rows // rows

    def kernel(*refs):
        ladder_kernel(quarters, virts, *refs)

    return pl.pallas_call(
        kernel,
        out_shape=jax.ShapeDtypeStruct((len(quarters) * far, out_tiles * rows, W), jnp.float32),
        in_specs=[SMEM, VMEM] + [VMEM] * len(blocks),
        out_specs=VMEM,
        scratch_shapes=[
            pltpu.VMEM((virts * in_local, 2 * total_rows, W), jnp.bfloat16),
            pltpu.VMEM((out_tiles + 1, total_rows, W), jnp.float32),
        ],
        compiler_params=pltpu.CompilerParams(vmem_limit_bytes=32 * 1024 * 1024),
        cost_estimate=pl.CostEstimate(flops=1 << 28, bytes_accessed=1 << 22, transcendentals=0),
    )(codes, halves, *blocks)


def near_mask(step, a, b):
    return SWITCHED[step] if (a ^ a // 2 ^ b) % 2 else step


def swap(value, pairs, virts, virt_mask, step=0, far=0):
    routes = [
        (a * virts + b, (a ^ far * NEAR ^ near_mask(step, a, b)) * virts + (b ^ virt_mask))
        for a in range(pairs)
        for b in range(virts)
    ]
    return lax.ppermute(value, ("pair", "virt"), routes)


def far_order(far):
    return [*range(far - 2), far - 1, far - 2]


def swap_sum(parts, pairs, virts, which, marks):
    order = (1, 2, 0, 3) if which == "step" else (1, 0, *range(2, len(marks)))
    received = [swap(parts[marks.index(mark)], pairs, virts, 1, **{which: mark}) for mark in order]
    return sum(received[1:], received[0])


def shards(t2_amplitudes, integral_tiles, out_tiles, in_tiles, tile_counts):
    rows, columns = t2_amplitudes.shape
    local_tiles = columns // W
    slots = integral_tiles.shape[2]
    pairs, virts = lax.axis_size("pair"), lax.axis_size("virt")
    mine = t2_amplitudes.reshape(rows, local_tiles, W).transpose(1, 0, 2).reshape(local_tiles * rows, W)
    halves, codes, own = prepare(
        integral_tiles.reshape(slots, W, W),
        in_tiles.reshape(1, slots),
        out_tiles.reshape(1, slots),
        tile_counts,
        mine,
        local_tiles,
    )
    order = far_order(pairs // NEAR)
    line = jnp.stack([own] + [swap(mine, pairs, virts, 1, far=mask) for mask in order[1:]])
    pieces = [line] + [swap(line, pairs, virts, 1, step=step) for step in range(1, NEAR)]
    pieces = [pieces] + [[swap(piece, pairs, virts, mask) for piece in pieces] for mask in range(1, virts)]
    codes = pltpu.with_memory_space_constraint(codes, pltpu.SMEM)
    parts, order_size = {}, len(order)
    for quarters in ((0, 3), (1, 2)):
        sums = quarter_terms(codes, pieces, quarters, halves, rows, local_tiles)
        halves, sums = lax.optimization_barrier((halves, sums))
        parts.update({a: sums[at * order_size : (at + 1) * order_size] for at, a in enumerate(quarters)})
    line_sums = swap_sum(parts, pairs, virts, "step", list(range(NEAR)))
    summed = swap_sum(line_sums, pairs, virts, "far", order)
    return summed.reshape(local_tiles, rows, W).transpose(1, 0, 2).reshape(rows, columns)


def solution(mesh):
    return jax.shard_map(
        shards,
        mesh=mesh,
        in_specs=(
            P("pair", "virt"),
            P("pair", "virt", None, None, None),
            P("pair", "virt", None),
            P("pair", "virt", None),
            P("pair", "virt"),
        ),
        out_specs=P("pair", "virt"),
        check_vma=False,
    )
```

```python
import jax
import jax.numpy as jnp
from jax import lax
from jax.experimental import pallas as pl
from jax.experimental.pallas import tpu as pltpu
from jax.sharding import PartitionSpec as P

W = 128
COPY_GROUP = 8
GROUP = 16
NEAR = 4
SWITCHED = (0, 2, 1, 3)
SMEM = pl.BlockSpec(memory_space=pltpu.SMEM)
VMEM = pl.BlockSpec(memory_space=pltpu.VMEM)


def split(value):
    high = value.astype(jnp.bfloat16)
    low = (value - high.astype(jnp.float32)).astype(jnp.bfloat16)
    return high, low


def tile_kernel(out_tiles, live, ins, outs, tiles, mine, halves, codes, own, held, in_row, out_row, arrived, singles):
    singles_of = ((ins, in_row), (outs, out_row), (mine, own))
    others = [pltpu.make_async_copy(here, there, singles.at[at]) for at, (here, there) in enumerate(singles_of)]
    for copy in others:
        copy.start()
    count = live[0, 0]
    groups = (count + COPY_GROUP - 1) // COPY_GROUP

    def tile_copy(index):
        part = pl.ds(index * COPY_GROUP, COPY_GROUP)
        return pltpu.make_async_copy(tiles.at[part], held.at[part], arrived.at[index])

    def begin(index, carry):
        tile_copy(index).start()
        return carry

    lax.fori_loop(0, groups, begin, 0)
    for copy in others:
        copy.wait()
    me = lax.axis_index("virt")
    codes[2, 0] = count
    for slot in range(ins.shape[1]):
        tile_in = in_row[0, slot]
        owner = lax.bitwise_xor(lax.div(tile_in, out_tiles), me)
        codes[0, slot] = owner * out_tiles + lax.rem(tile_in, out_tiles)
        codes[1, slot] = jnp.where(slot < count, lax.rem(out_row[0, slot], out_tiles), out_tiles)

    def one_group(index, carry):
        tile_copy(index).wait()
        for step in range(COPY_GROUP):
            slot = index * COPY_GROUP + step
            high, low = split(held[slot])
            halves[slot, :, :W] = high
            halves[slot, :, W:] = low
        return carry

    lax.fori_loop(0, groups, one_group, 0)


def prepare(tiles, ins, outs, live, mine, out_tiles):
    slots = tiles.shape[0]

    def kernel(*refs):
        tile_kernel(out_tiles, *refs)

    operands = [pltpu.with_memory_space_constraint(value, pltpu.HBM) for value in (ins, outs, tiles, mine)]
    return pl.pallas_call(
        kernel,
        out_shape=(
            jax.ShapeDtypeStruct((slots, W, 2 * W), jnp.bfloat16),
            pltpu.SMEM((3, slots), jnp.int32),
            jax.ShapeDtypeStruct(mine.shape, mine.dtype),
        ),
        in_specs=[SMEM] + [pl.BlockSpec(memory_space=pltpu.HBM)] * 4,
        out_specs=(VMEM, SMEM, VMEM),
        scratch_shapes=[
            pltpu.VMEM((slots, W, W), jnp.float32),
            pltpu.SMEM((1, slots), jnp.int32),
            pltpu.SMEM((1, slots), jnp.int32),
            pltpu.SemaphoreType.DMA((slots // COPY_GROUP,)),
            pltpu.SemaphoreType.DMA((3,)),
        ],
        compiler_params=pltpu.CompilerParams(vmem_limit_bytes=32 * 1024 * 1024),
        cost_estimate=pl.CostEstimate(flops=4 * slots * W * W, bytes_accessed=8 * slots * W * W, transcendentals=0),
    )(live, *operands)


def weave(first, second):
    half = first.shape[0] // 2
    upper = lax.broadcasted_iota(jnp.int32, first.shape, 0) < half
    return (
        jnp.where(upper, first, pltpu.roll(second, half, 0)),
        jnp.where(upper, pltpu.roll(first, half, 0), second),
    )


def ladder_kernel(quarters, virts, codes, halves, *refs):
    blocks, (result, columns, totals) = refs[:-3], refs[-3:]
    far, chunk_rows, _ = blocks[0].shape
    chunk_count = len(quarters) * far
    out_tiles = totals.shape[0] - 1
    rows = result.shape[1] // out_tiles
    total_rows = chunk_count * rows
    in_local = chunk_rows // rows
    totals[...] = jnp.zeros_like(totals)

    for owner in range(virts):
        for at_quarter, quarter in enumerate(quarters):
            crossed = [int((quarter > 0) != (b > 0)) for b in range(far)]
            sources = [blocks[at_quarter * virts + (owner ^ cross)] for cross in crossed]
            for b in range(0, far, 4):
                first_row = (at_quarter * far + b) * rows
                for tile in range(0, in_local, 2):
                    part = slice(tile * rows, (tile + 2) * rows)
                    four = [sources[b + at][b + at, part, :] for at in range(4)]
                    for at, pieces in enumerate(zip(weave(*four[:2]), weave(*four[2:]))):
                        high, low = split(jnp.concatenate(pieces, axis=0))
                        column = owner * in_local + tile + at
                        columns[column, first_row : first_row + 4 * rows, :] = high
                        columns[column, total_rows + first_row : total_rows + first_row + 4 * rows, :] = low

    def add_slots(number):
        products = []
        for slot in range(number):
            got = jnp.dot(columns[codes[0, slot]], halves[slot], preferred_element_type=jnp.float32)
            upper, lower = got[:total_rows], got[total_rows:]
            products.append((upper[:, :W] + lower[:, :W]) + (upper[:, W:] + lower[:, W:]))
        for slot, product in enumerate(products):
            place = codes[1, slot]
            totals[place] = totals[place] + product

    pl.when(codes[2, 0] <= GROUP)(lambda: add_slots(GROUP))
    pl.when(codes[2, 0] > GROUP)(lambda: add_slots(halves.shape[0]))
    for chunk in range(0, chunk_count, 2):
        part = slice(chunk * rows, (chunk + 2) * rows)
        for tile in range(0, out_tiles, 2):
            pieces = weave(totals[tile, part, :], totals[tile + 1, part, :])
            for at, piece in enumerate(pieces):
                result[chunk + at, tile * rows : (tile + 2) * rows, :] = piece


def quarter_terms(codes, pieces, quarters, halves, rows, out_tiles):
    virts = len(pieces)
    blocks = [pieces[c][SWITCHED[a] if c % 2 else a] for a in quarters for c in range(virts)]
    far, chunk_rows, _ = blocks[0].shape
    total_rows = len(quarters) * far * rows
    in_local = chunk_rows // rows

    def kernel(*refs):
        ladder_kernel(quarters, virts, *refs)

    return pl.pallas_call(
        kernel,
        out_shape=jax.ShapeDtypeStruct((len(quarters) * far, out_tiles * rows, W), jnp.float32),
        in_specs=[SMEM, VMEM] + [VMEM] * len(blocks),
        out_specs=VMEM,
        scratch_shapes=[
            pltpu.VMEM((virts * in_local, 2 * total_rows, W), jnp.bfloat16),
            pltpu.VMEM((out_tiles + 1, total_rows, W), jnp.float32),
        ],
        compiler_params=pltpu.CompilerParams(vmem_limit_bytes=32 * 1024 * 1024),
        cost_estimate=pl.CostEstimate(flops=1 << 28, bytes_accessed=1 << 22, transcendentals=0),
    )(codes, halves, *blocks)


def near_mask(step, a, b):
    return SWITCHED[step] if (a ^ a // 2 ^ b) % 2 else step


def swap(value, pairs, virts, virt_mask, step=0, far=0):
    routes = [
        (a * virts + b, (a ^ far * NEAR ^ near_mask(step, a, b)) * virts + (b ^ virt_mask))
        for a in range(pairs)
        for b in range(virts)
    ]
    return lax.ppermute(value, ("pair", "virt"), routes)


def far_order(far):
    return [*range(far - 2), far - 1, far - 2]


def swap_sum(parts, pairs, virts, which, marks):
    order = (1, 2, 0, 3) if which == "step" else (1, 0, *range(2, len(marks)))
    received = [swap(parts[marks.index(mark)], pairs, virts, 1, **{which: mark}) for mark in order]
    return sum(received[1:], received[0])


def shards(t2_amplitudes, integral_tiles, out_tiles, in_tiles, tile_counts):
    rows, columns = t2_amplitudes.shape
    local_tiles = columns // W
    slots = integral_tiles.shape[2]
    pairs, virts = lax.axis_size("pair"), lax.axis_size("virt")
    mine = t2_amplitudes.reshape(rows, local_tiles, W).transpose(1, 0, 2).reshape(local_tiles * rows, W)
    halves, codes, own = prepare(
        integral_tiles.reshape(slots, W, W),
        in_tiles.reshape(1, slots),
        out_tiles.reshape(1, slots),
        tile_counts,
        mine,
        local_tiles,
    )
    order = far_order(pairs // NEAR)
    line = jnp.stack([own] + [swap(mine, pairs, virts, 1, far=mask) for mask in order[1:]])
    pieces = [line] + [swap(line, pairs, virts, 1, step=step) for step in range(1, NEAR)]
    pieces = [pieces] + [[swap(piece, pairs, virts, mask) for piece in pieces] for mask in range(1, virts)]
    codes = pltpu.with_memory_space_constraint(codes, pltpu.SMEM)
    parts, order_size = {}, len(order)
    for quarters in ((0, 3), (1, 2)):
        sums = quarter_terms(codes, pieces, quarters, halves, rows, local_tiles)
        halves, sums = lax.optimization_barrier((halves, sums))
        parts.update({a: sums[at * order_size : (at + 1) * order_size] for at, a in enumerate(quarters)})
    line_sums = swap_sum(parts, pairs, virts, "step", list(range(NEAR)))
    summed = swap_sum(line_sums, pairs, virts, "far", order)
    return summed.reshape(local_tiles, rows, W).transpose(1, 0, 2).reshape(rows, columns)


def solution(mesh):
    return jax.shard_map(
        shards,
        mesh=mesh,
        in_specs=(
            P("pair", "virt"),
            P("pair", "virt", None, None, None),
            P("pair", "virt", None),
            P("pair", "virt", None),
            P("pair", "virt"),
        ),
        out_specs=P("pair", "virt"),
        check_vma=False,
    )
```

```python
import jax
import jax.numpy as jnp
from jax import lax
from jax.experimental import pallas as pl
from jax.experimental.pallas import tpu as pltpu
from jax.sharding import PartitionSpec as P

W = 128
COPY_GROUP = 8
GROUP = 16
NEAR = 4
SWITCHED = (0, 2, 1, 3)
SMEM = pl.BlockSpec(memory_space=pltpu.SMEM)
VMEM = pl.BlockSpec(memory_space=pltpu.VMEM)


def split(value):
    high = value.astype(jnp.bfloat16)
    low = (value - high.astype(jnp.float32)).astype(jnp.bfloat16)
    return high, low


def tile_kernel(out_tiles, live, ins, outs, tiles, mine, halves, codes, own, held, in_row, out_row, arrived, singles):
    singles_of = ((ins, in_row), (outs, out_row), (mine, own))
    others = [pltpu.make_async_copy(here, there, singles.at[at]) for at, (here, there) in enumerate(singles_of)]
    for copy in others:
        copy.start()
    count = live[0, 0]
    groups = (count + COPY_GROUP - 1) // COPY_GROUP

    def tile_copy(index):
        part = pl.ds(index * COPY_GROUP, COPY_GROUP)
        return pltpu.make_async_copy(tiles.at[part], held.at[part], arrived.at[index])

    def begin(index, carry):
        tile_copy(index).start()
        return carry

    lax.fori_loop(0, groups, begin, 0)
    for copy in others:
        copy.wait()
    me = lax.axis_index("virt")
    codes[2, 0] = count
    for slot in range(ins.shape[1]):
        tile_in = in_row[0, slot]
        owner = lax.bitwise_xor(lax.div(tile_in, out_tiles), me)
        codes[0, slot] = owner * out_tiles + lax.rem(tile_in, out_tiles)
        codes[1, slot] = jnp.where(slot < count, lax.rem(out_row[0, slot], out_tiles), out_tiles)

    def one_group(index, carry):
        tile_copy(index).wait()
        for step in range(COPY_GROUP):
            slot = index * COPY_GROUP + step
            high, low = split(held[slot])
            halves[slot, :, :W] = high
            halves[slot, :, W:] = low
        return carry

    lax.fori_loop(0, groups, one_group, 0)


def prepare(tiles, ins, outs, live, mine, out_tiles):
    slots = tiles.shape[0]

    def kernel(*refs):
        tile_kernel(out_tiles, *refs)

    operands = [pltpu.with_memory_space_constraint(value, pltpu.HBM) for value in (ins, outs, tiles, mine)]
    return pl.pallas_call(
        kernel,
        out_shape=(
            jax.ShapeDtypeStruct((slots, W, 2 * W), jnp.bfloat16),
            pltpu.SMEM((3, slots), jnp.int32),
            jax.ShapeDtypeStruct(mine.shape, mine.dtype),
        ),
        in_specs=[SMEM] + [pl.BlockSpec(memory_space=pltpu.HBM)] * 4,
        out_specs=(VMEM, SMEM, VMEM),
        scratch_shapes=[
            pltpu.VMEM((slots, W, W), jnp.float32),
            pltpu.SMEM((1, slots), jnp.int32),
            pltpu.SMEM((1, slots), jnp.int32),
            pltpu.SemaphoreType.DMA((slots // COPY_GROUP,)),
            pltpu.SemaphoreType.DMA((3,)),
        ],
        compiler_params=pltpu.CompilerParams(vmem_limit_bytes=32 * 1024 * 1024),
        cost_estimate=pl.CostEstimate(flops=4 * slots * W * W, bytes_accessed=8 * slots * W * W, transcendentals=0),
    )(live, *operands)


def weave(first, second):
    half = first.shape[0] // 2
    upper = lax.broadcasted_iota(jnp.int32, first.shape, 0) < half
    return (
        jnp.where(upper, first, pltpu.roll(second, half, 0)),
        jnp.where(upper, pltpu.roll(first, half, 0), second),
    )


def ladder_kernel(quarters, virts, codes, halves, *refs):
    blocks, (result, columns, totals) = refs[:-3], refs[-3:]
    far, chunk_rows, _ = blocks[0].shape
    chunk_count = len(quarters) * far
    out_tiles = totals.shape[0] - 1
    rows = result.shape[1] // out_tiles
    total_rows = chunk_count * rows
    in_local = chunk_rows // rows
    totals[...] = jnp.zeros_like(totals)

    for owner in range(virts):
        for at_quarter, quarter in enumerate(quarters):
            crossed = [int((quarter > 0) != (b > 0)) for b in range(far)]
            sources = [blocks[at_quarter * virts + (owner ^ cross)] for cross in crossed]
            for b in range(0, far, 4):
                first_row = (at_quarter * far + b) * rows
                for tile in range(0, in_local, 2):
                    part = slice(tile * rows, (tile + 2) * rows)
                    four = [sources[b + at][b + at, part, :] for at in range(4)]
                    for at, pieces in enumerate(zip(weave(*four[:2]), weave(*four[2:]))):
                        high, low = split(jnp.concatenate(pieces, axis=0))
                        column = owner * in_local + tile + at
                        columns[column, first_row : first_row + 4 * rows, :] = high
                        columns[column, total_rows + first_row : total_rows + first_row + 4 * rows, :] = low

    def add_slots(number):
        products = []
        for slot in range(number):
            got = jnp.dot(columns[codes[0, slot]], halves[slot], preferred_element_type=jnp.float32)
            upper, lower = got[:total_rows], got[total_rows:]
            products.append((upper[:, :W] + lower[:, :W]) + (upper[:, W:] + lower[:, W:]))
        for slot, product in enumerate(products):
            place = codes[1, slot]
            totals[place] = totals[place] + product

    pl.when(codes[2, 0] <= GROUP)(lambda: add_slots(GROUP))
    pl.when(codes[2, 0] > GROUP)(lambda: add_slots(halves.shape[0]))
    for chunk in range(0, chunk_count, 2):
        part = slice(chunk * rows, (chunk + 2) * rows)
        for tile in range(0, out_tiles, 2):
            pieces = weave(totals[tile, part, :], totals[tile + 1, part, :])
            for at, piece in enumerate(pieces):
                result[chunk + at, tile * rows : (tile + 2) * rows, :] = piece


def quarter_terms(codes, pieces, quarters, halves, rows, out_tiles):
    virts = len(pieces)
    blocks = [pieces[c][SWITCHED[a] if c % 2 else a] for a in quarters for c in range(virts)]
    far, chunk_rows, _ = blocks[0].shape
    total_rows = len(quarters) * far * rows
    in_local = chunk_rows // rows

    def kernel(*refs):
        ladder_kernel(quarters, virts, *refs)

    return pl.pallas_call(
        kernel,
        out_shape=jax.ShapeDtypeStruct((len(quarters) * far, out_tiles * rows, W), jnp.float32),
        in_specs=[SMEM, VMEM] + [VMEM] * len(blocks),
        out_specs=VMEM,
        scratch_shapes=[
            pltpu.VMEM((virts * in_local, 2 * total_rows, W), jnp.bfloat16),
            pltpu.VMEM((out_tiles + 1, total_rows, W), jnp.float32),
        ],
        compiler_params=pltpu.CompilerParams(vmem_limit_bytes=32 * 1024 * 1024),
        cost_estimate=pl.CostEstimate(flops=1 << 28, bytes_accessed=1 << 22, transcendentals=0),
    )(codes, halves, *blocks)


def near_mask(step, a, b):
    return SWITCHED[step] if (a ^ a // 2 ^ b) % 2 else step


def swap(value, pairs, virts, virt_mask, step=0, far=0):
    routes = [
        (a * virts + b, (a ^ far * NEAR ^ near_mask(step, a, b)) * virts + (b ^ virt_mask))
        for a in range(pairs)
        for b in range(virts)
    ]
    return lax.ppermute(value, ("pair", "virt"), routes)


def far_order(far):
    return [*range(far - 2), far - 1, far - 2]


def swap_sum(parts, pairs, virts, which, marks):
    order = (1, 0, 2, 3) if which == "step" else (1, 0, *range(2, len(marks)))
    received = [swap(parts[marks.index(mark)], pairs, virts, 1, **{which: mark}) for mark in order]
    return sum(received[1:], received[0])


def shards(t2_amplitudes, integral_tiles, out_tiles, in_tiles, tile_counts):
    rows, columns = t2_amplitudes.shape
    local_tiles = columns // W
    slots = integral_tiles.shape[2]
    pairs, virts = lax.axis_size("pair"), lax.axis_size("virt")
    mine = t2_amplitudes.reshape(rows, local_tiles, W).transpose(1, 0, 2).reshape(local_tiles * rows, W)
    halves, codes, own = prepare(
        integral_tiles.reshape(slots, W, W),
        in_tiles.reshape(1, slots),
        out_tiles.reshape(1, slots),
        tile_counts,
        mine,
        local_tiles,
    )
    order = far_order(pairs // NEAR)
    line = jnp.stack([own] + [swap(mine, pairs, virts, 1, far=mask) for mask in order[1:]])
    pieces = [line] + [swap(line, pairs, virts, 1, step=step) for step in range(1, NEAR)]
    pieces = [pieces] + [[swap(piece, pairs, virts, mask) for piece in pieces] for mask in range(1, virts)]
    codes = pltpu.with_memory_space_constraint(codes, pltpu.SMEM)
    parts, order_size = {}, len(order)
    for quarters in ((3,), (0, 1, 2)):
        sums = quarter_terms(codes, pieces, quarters, halves, rows, local_tiles)
        halves, sums = lax.optimization_barrier((halves, sums))
        parts.update({a: sums[at * order_size : (at + 1) * order_size] for at, a in enumerate(quarters)})
    line_sums = swap_sum(parts, pairs, virts, "step", list(range(NEAR)))
    summed = swap_sum(line_sums, pairs, virts, "far", order)
    return summed.reshape(local_tiles, rows, W).transpose(1, 0, 2).reshape(rows, columns)


def solution(mesh):
    return jax.shard_map(
        shards,
        mesh=mesh,
        in_specs=(
            P("pair", "virt"),
            P("pair", "virt", None, None, None),
            P("pair", "virt", None),
            P("pair", "virt", None),
            P("pair", "virt"),
        ),
        out_specs=P("pair", "virt"),
        check_vma=False,
    )
```

```python
import jax
import jax.numpy as jnp
from jax import lax
from jax.experimental import pallas as pl
from jax.experimental.pallas import tpu as pltpu
from jax.sharding import PartitionSpec as P

W = 128
COPY_GROUP = 8
GROUP = 16
NEAR = 4
SWITCHED = (0, 1, 2, 3)
SMEM = pl.BlockSpec(memory_space=pltpu.SMEM)
VMEM = pl.BlockSpec(memory_space=pltpu.VMEM)


def split(value):
    high = value.astype(jnp.bfloat16)
    low = (value - high.astype(jnp.float32)).astype(jnp.bfloat16)
    return high, low


def tile_kernel(out_tiles, live, ins, outs, tiles, mine, halves, codes, own, held, in_row, out_row, arrived, singles):
    singles_of = ((ins, in_row), (outs, out_row), (mine, own))
    others = [pltpu.make_async_copy(here, there, singles.at[at]) for at, (here, there) in enumerate(singles_of)]
    for copy in others:
        copy.start()
    count = live[0, 0]
    groups = (count + COPY_GROUP - 1) // COPY_GROUP

    def tile_copy(index):
        part = pl.ds(index * COPY_GROUP, COPY_GROUP)
        return pltpu.make_async_copy(tiles.at[part], held.at[part], arrived.at[index])

    def begin(index, carry):
        tile_copy(index).start()
        return carry

    lax.fori_loop(0, groups, begin, 0)
    for copy in others:
        copy.wait()
    me = lax.axis_index("virt")
    codes[2, 0] = count
    for slot in range(ins.shape[1]):
        tile_in = in_row[0, slot]
        owner = lax.bitwise_xor(lax.div(tile_in, out_tiles), me)
        codes[0, slot] = owner * out_tiles + lax.rem(tile_in, out_tiles)
        codes[1, slot] = jnp.where(slot < count, lax.rem(out_row[0, slot], out_tiles), out_tiles)

    def one_group(index, carry):
        tile_copy(index).wait()
        for step in range(COPY_GROUP):
            slot = index * COPY_GROUP + step
            high, low = split(held[slot])
            halves[slot, :, :W] = high
            halves[slot, :, W:] = low
        return carry

    lax.fori_loop(0, groups, one_group, 0)


def prepare(tiles, ins, outs, live, mine, out_tiles):
    slots = tiles.shape[0]

    def kernel(*refs):
        tile_kernel(out_tiles, *refs)

    operands = [pltpu.with_memory_space_constraint(value, pltpu.HBM) for value in (ins, outs, tiles, mine)]
    return pl.pallas_call(
        kernel,
        out_shape=(
            jax.ShapeDtypeStruct((slots, W, 2 * W), jnp.bfloat16),
            pltpu.SMEM((3, slots), jnp.int32),
            jax.ShapeDtypeStruct(mine.shape, mine.dtype),
        ),
        in_specs=[SMEM] + [pl.BlockSpec(memory_space=pltpu.HBM)] * 4,
        out_specs=(VMEM, SMEM, VMEM),
        scratch_shapes=[
            pltpu.VMEM((slots, W, W), jnp.float32),
            pltpu.SMEM((1, slots), jnp.int32),
            pltpu.SMEM((1, slots), jnp.int32),
            pltpu.SemaphoreType.DMA((slots // COPY_GROUP,)),
            pltpu.SemaphoreType.DMA((3,)),
        ],
        compiler_params=pltpu.CompilerParams(vmem_limit_bytes=32 * 1024 * 1024),
        cost_estimate=pl.CostEstimate(flops=4 * slots * W * W, bytes_accessed=8 * slots * W * W, transcendentals=0),
    )(live, *operands)


def weave(first, second):
    half = first.shape[0] // 2
    upper = lax.broadcasted_iota(jnp.int32, first.shape, 0) < half
    return (
        jnp.where(upper, first, pltpu.roll(second, half, 0)),
        jnp.where(upper, pltpu.roll(first, half, 0), second),
    )


def ladder_kernel(quarters, virts, codes, halves, *refs):
    blocks, (result, columns, totals) = refs[:-3], refs[-3:]
    far, chunk_rows, _ = blocks[0].shape
    chunk_count = len(quarters) * far
    out_tiles = totals.shape[0] - 1
    rows = result.shape[1] // out_tiles
    total_rows = chunk_count * rows
    in_local = chunk_rows // rows
    totals[...] = jnp.zeros_like(totals)

    for owner in range(virts):
        for at_quarter, quarter in enumerate(quarters):
            crossed = [int((quarter > 0) != (b > 0)) for b in range(far)]
            sources = [blocks[at_quarter * virts + (owner ^ cross)] for cross in crossed]
            for b in range(0, far, 4):
                first_row = (at_quarter * far + b) * rows
                for tile in range(0, in_local, 2):
                    part = slice(tile * rows, (tile + 2) * rows)
                    four = [sources[b + at][b + at, part, :] for at in range(4)]
                    for at, pieces in enumerate(zip(weave(*four[:2]), weave(*four[2:]))):
                        high, low = split(jnp.concatenate(pieces, axis=0))
                        column = owner * in_local + tile + at
                        columns[column, first_row : first_row + 4 * rows, :] = high
                        columns[column, total_rows + first_row : total_rows + first_row + 4 * rows, :] = low

    def add_slots(number):
        products = []
        for slot in range(number):
            got = jnp.dot(columns[codes[0, slot]], halves[slot], preferred_element_type=jnp.float32)
            upper, lower = got[:total_rows], got[total_rows:]
            products.append((upper[:, :W] + lower[:, :W]) + (upper[:, W:] + lower[:, W:]))
        for slot, product in enumerate(products):
            place = codes[1, slot]
            totals[place] = totals[place] + product

    pl.when(codes[2, 0] <= GROUP)(lambda: add_slots(GROUP))
    pl.when(codes[2, 0] > GROUP)(lambda: add_slots(halves.shape[0]))
    for chunk in range(0, chunk_count, 2):
        part = slice(chunk * rows, (chunk + 2) * rows)
        for tile in range(0, out_tiles, 2):
            pieces = weave(totals[tile, part, :], totals[tile + 1, part, :])
            for at, piece in enumerate(pieces):
                result[chunk + at, tile * rows : (tile + 2) * rows, :] = piece


def quarter_terms(codes, pieces, quarters, halves, rows, out_tiles):
    virts = len(pieces)
    blocks = [pieces[c][SWITCHED[a] if c % 2 else a] for a in quarters for c in range(virts)]
    far, chunk_rows, _ = blocks[0].shape
    total_rows = len(quarters) * far * rows
    in_local = chunk_rows // rows

    def kernel(*refs):
        ladder_kernel(quarters, virts, *refs)

    return pl.pallas_call(
        kernel,
        out_shape=jax.ShapeDtypeStruct((len(quarters) * far, out_tiles * rows, W), jnp.float32),
        in_specs=[SMEM, VMEM] + [VMEM] * len(blocks),
        out_specs=VMEM,
        scratch_shapes=[
            pltpu.VMEM((virts * in_local, 2 * total_rows, W), jnp.bfloat16),
            pltpu.VMEM((out_tiles + 1, total_rows, W), jnp.float32),
        ],
        compiler_params=pltpu.CompilerParams(vmem_limit_bytes=32 * 1024 * 1024),
        cost_estimate=pl.CostEstimate(flops=1 << 28, bytes_accessed=1 << 22, transcendentals=0),
    )(codes, halves, *blocks)


def near_mask(step, a, b):
    return SWITCHED[step] if (a ^ a // 2 ^ b) % 2 else step


def swap(value, pairs, virts, virt_mask, step=0, far=0):
    routes = [
        (a * virts + b, (a ^ far * NEAR ^ near_mask(step, a, b)) * virts + (b ^ virt_mask))
        for a in range(pairs)
        for b in range(virts)
    ]
    return lax.ppermute(value, ("pair", "virt"), routes)


def far_order(far):
    return [*range(far - 2), far - 1, far - 2]


def swap_sum(parts, pairs, virts, which, marks):
    order = (1, 0, 2, 3) if which == "step" else (1, 0, *range(2, len(marks)))
    received = [swap(parts[marks.index(mark)], pairs, virts, 1, **{which: mark}) for mark in order]
    return sum(received[1:], received[0])


def shards(t2_amplitudes, integral_tiles, out_tiles, in_tiles, tile_counts):
    rows, columns = t2_amplitudes.shape
    local_tiles = columns // W
    slots = integral_tiles.shape[2]
    pairs, virts = lax.axis_size("pair"), lax.axis_size("virt")
    mine = t2_amplitudes.reshape(rows, local_tiles, W).transpose(1, 0, 2).reshape(local_tiles * rows, W)
    halves, codes, own = prepare(
        integral_tiles.reshape(slots, W, W),
        in_tiles.reshape(1, slots),
        out_tiles.reshape(1, slots),
        tile_counts,
        mine,
        local_tiles,
    )
    order = far_order(pairs // NEAR)
    line = jnp.stack([own] + [swap(mine, pairs, virts, 1, far=mask) for mask in order[1:]])
    pieces = [line] + [swap(line, pairs, virts, 1, step=step) for step in range(1, NEAR)]
    pieces = [pieces] + [[swap(piece, pairs, virts, mask) for piece in pieces] for mask in range(1, virts)]
    codes = pltpu.with_memory_space_constraint(codes, pltpu.SMEM)
    parts, order_size = {}, len(order)
    for quarters in ((3,), (0, 1, 2)):
        sums = quarter_terms(codes, pieces, quarters, halves, rows, local_tiles)
        halves, sums = lax.optimization_barrier((halves, sums))
        parts.update({a: sums[at * order_size : (at + 1) * order_size] for at, a in enumerate(quarters)})
    line_sums = swap_sum(parts, pairs, virts, "step", list(range(NEAR)))
    summed = swap_sum(line_sums, pairs, virts, "far", order)
    return summed.reshape(local_tiles, rows, W).transpose(1, 0, 2).reshape(rows, columns)


def solution(mesh):
    return jax.shard_map(
        shards,
        mesh=mesh,
        in_specs=(
            P("pair", "virt"),
            P("pair", "virt", None, None, None),
            P("pair", "virt", None),
            P("pair", "virt", None),
            P("pair", "virt"),
        ),
        out_specs=P("pair", "virt"),
        check_vma=False,
    )
```

```python
import jax
import jax.numpy as jnp
from jax import lax
from jax.experimental import pallas as pl
from jax.experimental.pallas import tpu as pltpu
from jax.sharding import PartitionSpec as P

W = 128
COPY_GROUP = 8
GROUP = 16
NEAR = 4
SWITCHED = (0, 2, 1, 3)
SMEM = pl.BlockSpec(memory_space=pltpu.SMEM)
VMEM = pl.BlockSpec(memory_space=pltpu.VMEM)


def split(value):
    high = value.astype(jnp.bfloat16)
    low = (value - high.astype(jnp.float32)).astype(jnp.bfloat16)
    return high, low


def tile_kernel(out_tiles, live, ins, outs, tiles, mine, halves, codes, own, held, in_row, out_row, arrived, singles):
    singles_of = ((ins, in_row), (outs, out_row), (mine, own))
    others = [pltpu.make_async_copy(here, there, singles.at[at]) for at, (here, there) in enumerate(singles_of)]
    for copy in others:
        copy.start()
    count = live[0, 0]
    groups = (count + COPY_GROUP - 1) // COPY_GROUP

    def tile_copy(index):
        part = pl.ds(index * COPY_GROUP, COPY_GROUP)
        return pltpu.make_async_copy(tiles.at[part], held.at[part], arrived.at[index])

    def begin(index, carry):
        tile_copy(index).start()
        return carry

    lax.fori_loop(0, groups, begin, 0)
    for copy in others:
        copy.wait()
    me = lax.axis_index("virt")
    codes[2, 0] = count
    for slot in range(ins.shape[1]):
        tile_in = in_row[0, slot]
        owner = lax.bitwise_xor(lax.div(tile_in, out_tiles), me)
        codes[0, slot] = owner * out_tiles + lax.rem(tile_in, out_tiles)
        codes[1, slot] = jnp.where(slot < count, lax.rem(out_row[0, slot], out_tiles), out_tiles)

    def one_group(index, carry):
        tile_copy(index).wait()
        for step in range(COPY_GROUP):
            slot = index * COPY_GROUP + step
            high, low = split(held[slot])
            halves[slot, :, :W] = high
            halves[slot, :, W:] = low
        return carry

    lax.fori_loop(0, groups, one_group, 0)


def prepare(tiles, ins, outs, live, mine, out_tiles):
    slots = tiles.shape[0]

    def kernel(*refs):
        tile_kernel(out_tiles, *refs)

    operands = [pltpu.with_memory_space_constraint(value, pltpu.HBM) for value in (ins, outs, tiles, mine)]
    return pl.pallas_call(
        kernel,
        out_shape=(
            jax.ShapeDtypeStruct((slots, W, 2 * W), jnp.bfloat16),
            pltpu.SMEM((3, slots), jnp.int32),
            jax.ShapeDtypeStruct(mine.shape, mine.dtype),
        ),
        in_specs=[SMEM] + [pl.BlockSpec(memory_space=pltpu.HBM)] * 4,
        out_specs=(VMEM, SMEM, VMEM),
        scratch_shapes=[
            pltpu.VMEM((slots, W, W), jnp.float32),
            pltpu.SMEM((1, slots), jnp.int32),
            pltpu.SMEM((1, slots), jnp.int32),
            pltpu.SemaphoreType.DMA((slots // COPY_GROUP,)),
            pltpu.SemaphoreType.DMA((3,)),
        ],
        compiler_params=pltpu.CompilerParams(vmem_limit_bytes=32 * 1024 * 1024),
        cost_estimate=pl.CostEstimate(flops=4 * slots * W * W, bytes_accessed=8 * slots * W * W, transcendentals=0),
    )(live, *operands)


def weave(first, second):
    half = first.shape[0] // 2
    upper = lax.broadcasted_iota(jnp.int32, first.shape, 0) < half
    return (
        jnp.where(upper, first, pltpu.roll(second, half, 0)),
        jnp.where(upper, pltpu.roll(first, half, 0), second),
    )


def ladder_kernel(quarters, virts, codes, halves, *refs):
    blocks, (result, columns, totals) = refs[:-3], refs[-3:]
    far, chunk_rows, _ = blocks[0].shape
    chunk_count = len(quarters) * far
    out_tiles = totals.shape[0] - 1
    rows = result.shape[1] // out_tiles
    total_rows = chunk_count * rows
    in_local = chunk_rows // rows
    totals[...] = jnp.zeros_like(totals)

    for owner in range(virts):
        for at_quarter, quarter in enumerate(quarters):
            crossed = [int((quarter > 0) != (b > 0)) for b in range(far)]
            sources = [blocks[at_quarter * virts + (owner ^ cross)] for cross in crossed]
            for b in range(0, far, 4):
                first_row = (at_quarter * far + b) * rows
                for tile in range(0, in_local, 2):
                    part = slice(tile * rows, (tile + 2) * rows)
                    four = [sources[b + at][b + at, part, :] for at in range(4)]
                    for at, pieces in enumerate(zip(weave(*four[:2]), weave(*four[2:]))):
                        high, low = split(jnp.concatenate(pieces, axis=0))
                        column = owner * in_local + tile + at
                        columns[column, first_row : first_row + 4 * rows, :] = high
                        columns[column, total_rows + first_row : total_rows + first_row + 4 * rows, :] = low

    def add_slots(number):
        products = []
        for slot in range(number):
            got = jnp.dot(columns[codes[0, slot]], halves[slot], preferred_element_type=jnp.float32)
            upper, lower = got[:total_rows], got[total_rows:]
            products.append((upper[:, :W] + lower[:, :W]) + (upper[:, W:] + lower[:, W:]))
        for slot, product in enumerate(products):
            place = codes[1, slot]
            totals[place] = totals[place] + product

    count = codes[2, 0]
    pl.when(count <= GROUP // 2)(lambda: add_slots(GROUP // 2))
    pl.when((count > GROUP // 2) & (count <= GROUP))(lambda: add_slots(GROUP))
    pl.when(count > GROUP)(lambda: add_slots(halves.shape[0]))
    for chunk in range(0, chunk_count, 2):
        part = slice(chunk * rows, (chunk + 2) * rows)
        for tile in range(0, out_tiles, 2):
            pieces = weave(totals[tile, part, :], totals[tile + 1, part, :])
            for at, piece in enumerate(pieces):
                result[chunk + at, tile * rows : (tile + 2) * rows, :] = piece


def quarter_terms(codes, pieces, quarters, halves, rows, out_tiles):
    virts = len(pieces)
    blocks = [pieces[c][SWITCHED[a] if c % 2 else a] for a in quarters for c in range(virts)]
    far, chunk_rows, _ = blocks[0].shape
    total_rows = len(quarters) * far * rows
    in_local = chunk_rows // rows

    def kernel(*refs):
        ladder_kernel(quarters, virts, *refs)

    return pl.pallas_call(
        kernel,
        out_shape=jax.ShapeDtypeStruct((len(quarters) * far, out_tiles * rows, W), jnp.float32),
        in_specs=[SMEM, VMEM] + [VMEM] * len(blocks),
        out_specs=VMEM,
        scratch_shapes=[
            pltpu.VMEM((virts * in_local, 2 * total_rows, W), jnp.bfloat16),
            pltpu.VMEM((out_tiles + 1, total_rows, W), jnp.float32),
        ],
        compiler_params=pltpu.CompilerParams(vmem_limit_bytes=32 * 1024 * 1024),
        cost_estimate=pl.CostEstimate(flops=1 << 28, bytes_accessed=1 << 22, transcendentals=0),
    )(codes, halves, *blocks)


def near_mask(step, a, b):
    return SWITCHED[step] if (a ^ a // 2 ^ b) % 2 else step


def swap(value, pairs, virts, virt_mask, step=0, far=0):
    routes = [
        (a * virts + b, (a ^ far * NEAR ^ near_mask(step, a, b)) * virts + (b ^ virt_mask))
        for a in range(pairs)
        for b in range(virts)
    ]
    return lax.ppermute(value, ("pair", "virt"), routes)


def far_order(far):
    return [*range(far - 2), far - 1, far - 2]


def swap_sum(parts, pairs, virts, which, marks):
    order = (1, 0, 2, 3) if which == "step" else (1, 0, *range(2, len(marks)))
    received = [swap(parts[marks.index(mark)], pairs, virts, 1, **{which: mark}) for mark in order]
    return sum(received[1:], received[0])


def shards(t2_amplitudes, integral_tiles, out_tiles, in_tiles, tile_counts):
    rows, columns = t2_amplitudes.shape
    local_tiles = columns // W
    slots = integral_tiles.shape[2]
    pairs, virts = lax.axis_size("pair"), lax.axis_size("virt")
    mine = t2_amplitudes.reshape(rows, local_tiles, W).transpose(1, 0, 2).reshape(local_tiles * rows, W)
    halves, codes, own = prepare(
        integral_tiles.reshape(slots, W, W),
        in_tiles.reshape(1, slots),
        out_tiles.reshape(1, slots),
        tile_counts,
        mine,
        local_tiles,
    )
    order = far_order(pairs // NEAR)
    line = jnp.stack([own] + [swap(mine, pairs, virts, 1, far=mask) for mask in order[1:]])
    pieces = [line] + [swap(line, pairs, virts, 1, step=step) for step in range(1, NEAR)]
    pieces = [pieces] + [[swap(piece, pairs, virts, mask) for piece in pieces] for mask in range(1, virts)]
    codes = pltpu.with_memory_space_constraint(codes, pltpu.SMEM)
    parts, order_size = {}, len(order)
    for quarters in ((3,), (0, 1, 2)):
        sums = quarter_terms(codes, pieces, quarters, halves, rows, local_tiles)
        halves, sums = lax.optimization_barrier((halves, sums))
        parts.update({a: sums[at * order_size : (at + 1) * order_size] for at, a in enumerate(quarters)})
    line_sums = swap_sum(parts, pairs, virts, "step", list(range(NEAR)))
    summed = swap_sum(line_sums, pairs, virts, "far", order)
    return summed.reshape(local_tiles, rows, W).transpose(1, 0, 2).reshape(rows, columns)


def solution(mesh):
    return jax.shard_map(
        shards,
        mesh=mesh,
        in_specs=(
            P("pair", "virt"),
            P("pair", "virt", None, None, None),
            P("pair", "virt", None),
            P("pair", "virt", None),
            P("pair", "virt"),
        ),
        out_specs=P("pair", "virt"),
        check_vma=False,
    )
```

```python
import jax
import jax.numpy as jnp
from jax import lax
from jax.experimental import pallas as pl
from jax.experimental.pallas import tpu as pltpu
from jax.sharding import PartitionSpec as P

W = 128
COPY_GROUP = 8
GROUP = 16
NEAR = 4
SWITCHED = (0, 2, 1, 3)
SMEM = pl.BlockSpec(memory_space=pltpu.SMEM)
VMEM = pl.BlockSpec(memory_space=pltpu.VMEM)


def split(value):
    high = value.astype(jnp.bfloat16)
    low = (value - high.astype(jnp.float32)).astype(jnp.bfloat16)
    return high, low


def tile_kernel(out_tiles, live, ins, outs, tiles, mine, halves, codes, own, held, in_row, out_row, arrived, singles):
    singles_of = ((ins, in_row), (outs, out_row), (mine, own))
    others = [pltpu.make_async_copy(here, there, singles.at[at]) for at, (here, there) in enumerate(singles_of)]
    for copy in others:
        copy.start()
    count = live[0, 0]
    groups = (count + COPY_GROUP - 1) // COPY_GROUP

    def tile_copy(index):
        part = pl.ds(index * COPY_GROUP, COPY_GROUP)
        return pltpu.make_async_copy(tiles.at[part], held.at[part], arrived.at[index])

    def begin(index, carry):
        tile_copy(index).start()
        return carry

    lax.fori_loop(0, groups, begin, 0)
    for copy in others:
        copy.wait()
    me = lax.axis_index("virt")
    codes[2, 0] = count
    for slot in range(ins.shape[1]):
        tile_in = in_row[0, slot]
        owner = lax.bitwise_xor(lax.div(tile_in, out_tiles), me)
        codes[0, slot] = owner * out_tiles + lax.rem(tile_in, out_tiles)
        codes[1, slot] = jnp.where(slot < count, lax.rem(out_row[0, slot], out_tiles), out_tiles)

    def one_group(index, carry):
        tile_copy(index).wait()
        for step in range(COPY_GROUP):
            slot = index * COPY_GROUP + step
            high, low = split(held[slot])
            halves[slot, :, :W] = high
            halves[slot, :, W:] = low
        return carry

    lax.fori_loop(0, groups, one_group, 0)


def prepare(tiles, ins, outs, live, mine, out_tiles):
    slots = tiles.shape[0]

    def kernel(*refs):
        tile_kernel(out_tiles, *refs)

    operands = [pltpu.with_memory_space_constraint(value, pltpu.HBM) for value in (ins, outs, tiles, mine)]
    return pl.pallas_call(
        kernel,
        out_shape=(
            jax.ShapeDtypeStruct((slots, W, 2 * W), jnp.bfloat16),
            pltpu.SMEM((3, slots), jnp.int32),
            jax.ShapeDtypeStruct(mine.shape, mine.dtype),
        ),
        in_specs=[SMEM] + [pl.BlockSpec(memory_space=pltpu.HBM)] * 4,
        out_specs=(VMEM, SMEM, VMEM),
        scratch_shapes=[
            pltpu.VMEM((slots, W, W), jnp.float32),
            pltpu.SMEM((1, slots), jnp.int32),
            pltpu.SMEM((1, slots), jnp.int32),
            pltpu.SemaphoreType.DMA((slots // COPY_GROUP,)),
            pltpu.SemaphoreType.DMA((3,)),
        ],
        compiler_params=pltpu.CompilerParams(vmem_limit_bytes=32 * 1024 * 1024),
        cost_estimate=pl.CostEstimate(flops=4 * slots * W * W, bytes_accessed=8 * slots * W * W, transcendentals=0),
    )(live, *operands)


def weave(first, second):
    half = first.shape[0] // 2
    upper = lax.broadcasted_iota(jnp.int32, first.shape, 0) < half
    return (
        jnp.where(upper, first, pltpu.roll(second, half, 0)),
        jnp.where(upper, pltpu.roll(first, half, 0), second),
    )


def ladder_kernel(quarters, virts, codes, halves, *refs):
    blocks, (result, columns, totals) = refs[:-3], refs[-3:]
    far, chunk_rows, _ = blocks[0].shape
    chunk_count = len(quarters) * far
    out_tiles = totals.shape[0] - 1
    rows = result.shape[1] // out_tiles
    total_rows = chunk_count * rows
    in_local = chunk_rows // rows
    totals[...] = jnp.zeros_like(totals)

    for owner in range(virts):
        for at_quarter, quarter in enumerate(quarters):
            crossed = [int((quarter > 0) != (b > 0)) for b in range(far)]
            sources = [blocks[at_quarter * virts + (owner ^ cross)] for cross in crossed]
            for b in range(0, far, 4):
                first_row = (at_quarter * far + b) * rows
                for tile in range(0, in_local, 2):
                    part = slice(tile * rows, (tile + 2) * rows)
                    four = [sources[b + at][b + at, part, :] for at in range(4)]
                    for at, pieces in enumerate(zip(weave(*four[:2]), weave(*four[2:]))):
                        high, low = split(jnp.concatenate(pieces, axis=0))
                        column = owner * in_local + tile + at
                        columns[column, first_row : first_row + 4 * rows, :] = high
                        columns[column, total_rows + first_row : total_rows + first_row + 4 * rows, :] = low

    def add_slots(number):
        products = []
        for slot in range(number):
            got = jnp.dot(columns[codes[0, slot]], halves[slot], preferred_element_type=jnp.float32)
            upper, lower = got[:total_rows], got[total_rows:]
            products.append((upper[:, :W] + lower[:, :W]) + (upper[:, W:] + lower[:, W:]))
        for slot, product in enumerate(products):
            place = codes[1, slot]
            totals[place] = totals[place] + product

    pl.when(codes[2, 0] <= GROUP)(lambda: add_slots(GROUP))
    pl.when(codes[2, 0] > GROUP)(lambda: add_slots(halves.shape[0]))
    for chunk in range(0, chunk_count, 2):
        part = slice(chunk * rows, (chunk + 2) * rows)
        for tile in range(0, out_tiles, 2):
            pieces = weave(totals[tile, part, :], totals[tile + 1, part, :])
            for at, piece in enumerate(pieces):
                result[chunk + at, tile * rows : (tile + 2) * rows, :] = piece


def quarter_terms(codes, pieces, quarters, halves, rows, out_tiles):
    virts = len(pieces)
    blocks = [pieces[c][SWITCHED[a] if c % 2 else a] for a in quarters for c in range(virts)]
    far, chunk_rows, _ = blocks[0].shape
    total_rows = len(quarters) * far * rows
    in_local = chunk_rows // rows

    def kernel(*refs):
        ladder_kernel(quarters, virts, *refs)

    return pl.pallas_call(
        kernel,
        out_shape=jax.ShapeDtypeStruct((len(quarters) * far, out_tiles * rows, W), jnp.float32),
        in_specs=[SMEM, VMEM] + [VMEM] * len(blocks),
        out_specs=VMEM,
        scratch_shapes=[
            pltpu.VMEM((virts * in_local, 2 * total_rows, W), jnp.bfloat16),
            pltpu.VMEM((out_tiles + 1, total_rows, W), jnp.float32),
        ],
        compiler_params=pltpu.CompilerParams(vmem_limit_bytes=32 * 1024 * 1024),
        cost_estimate=pl.CostEstimate(flops=1 << 28, bytes_accessed=1 << 22, transcendentals=0),
    )(codes, halves, *blocks)


def near_mask(step, a, b):
    return SWITCHED[step] if (a ^ a // 2 ^ b) % 2 else step


def swap(value, pairs, virts, virt_mask, step=0, far=0):
    routes = [
        (a * virts + b, (a ^ far * NEAR ^ near_mask(step, a, b)) * virts + (b ^ virt_mask))
        for a in range(pairs)
        for b in range(virts)
    ]
    return lax.ppermute(value, ("pair", "virt"), routes)


def far_order(far):
    return [*range(far - 2), far - 1, far - 2]


def swap_sum(parts, pairs, virts, which, marks):
    order = (2, 0, 1, 3) if which == "step" else (1, 0, *range(2, len(marks)))
    received = [swap(parts[marks.index(mark)], pairs, virts, 1, **{which: mark}) for mark in order]
    return sum(received[1:], received[0])


def shards(t2_amplitudes, integral_tiles, out_tiles, in_tiles, tile_counts):
    rows, columns = t2_amplitudes.shape
    local_tiles = columns // W
    slots = integral_tiles.shape[2]
    pairs, virts = lax.axis_size("pair"), lax.axis_size("virt")
    mine = t2_amplitudes.reshape(rows, local_tiles, W).transpose(1, 0, 2).reshape(local_tiles * rows, W)
    halves, codes, own = prepare(
        integral_tiles.reshape(slots, W, W),
        in_tiles.reshape(1, slots),
        out_tiles.reshape(1, slots),
        tile_counts,
        mine,
        local_tiles,
    )
    order = far_order(pairs // NEAR)
    line = jnp.stack([own] + [swap(mine, pairs, virts, 1, far=mask) for mask in order[1:]])
    pieces = [line] + [swap(line, pairs, virts, 1, step=step) for step in range(1, NEAR)]
    pieces = [pieces] + [[swap(piece, pairs, virts, mask) for piece in pieces] for mask in range(1, virts)]
    codes = pltpu.with_memory_space_constraint(codes, pltpu.SMEM)
    parts, order_size = {}, len(order)
    for quarters in ((3,), (0, 1, 2)):
        sums = quarter_terms(codes, pieces, quarters, halves, rows, local_tiles)
        halves, sums = lax.optimization_barrier((halves, sums))
        parts.update({a: sums[at * order_size : (at + 1) * order_size] for at, a in enumerate(quarters)})
    line_sums = swap_sum(parts, pairs, virts, "step", list(range(NEAR)))
    summed = swap_sum(line_sums, pairs, virts, "far", order)
    return summed.reshape(local_tiles, rows, W).transpose(1, 0, 2).reshape(rows, columns)


def solution(mesh):
    return jax.shard_map(
        shards,
        mesh=mesh,
        in_specs=(
            P("pair", "virt"),
            P("pair", "virt", None, None, None),
            P("pair", "virt", None),
            P("pair", "virt", None),
            P("pair", "virt"),
        ),
        out_specs=P("pair", "virt"),
        check_vma=False,
    )
```
